32 devices in a mesh: shard: 8 (over z, y), rep: 4 (over x, core).
Axes of the slice: x: 2, y: 2, z: 4, core: 2. Of those that a mesh axis runs over, the one named last changes fastest.
Arguments:
- embeddings: bfloat16 [16384, 1024], P('shard'), may hold values from -200 to 200
- labels: int32 [16384], P('shard'), may hold values from 0 to 15, never falling along the last dimension, each value on 1 to 8193 neighbouring positions
Outputs:
- best_similarity: float32 [16384], P('shard')
The draws below stay inside these ranges and needn't reach their ends.
Inputs may be any that keep to these rules, and one draw needn't show every extreme that they name: labels never fall along the rows; each cluster holds at most 8193 consecutive rows, and one cluster holds exactly that many.
All inputs are finite; a program needn't handle non-finite values.
Results may differ from the reference program's by a relative error of at most 0.00063.
Values may be sent and summed in bfloat16 or wider, within the bound.
No kernel may reach another device: no remote copies, remote signals or barrier semaphores. Data moves between devices by JAX's collectives and lax.ppermute only.
A program may use at most 64 MiB of HBM per device.

```python
import math
import jax
import jax.numpy as jnp
import numpy as np
from jax import lax

D = 1024
TOK_DEV = 2048
LOOK = 4
ROWS = 16384
CLUSTERS = 16


def draw_embeddings(key, part):
    key_noise = jax.random.fold_in(key, 11)
    key_offset = jax.random.fold_in(key, 12)
    key_weight = jax.random.fold_in(key, 13)
    noise = jax.random.normal(key_noise, (ROWS, D), jnp.float32)
    offset = jax.random.randint(key_offset, (ROWS,), 1, LOOK * TOK_DEV + 1)
    source = (jnp.arange(ROWS, dtype=jnp.int32) - offset) % ROWS
    weight = jax.random.uniform(key_weight, (ROWS, 1), jnp.float32, 0.2, 1.5)
    mixed = noise + weight * noise[source]
    return mixed.astype(jnp.bfloat16)


def split_up(count, total, most, skew):
    weights = [(1 << 20) // math.isqrt(grade ** skew) + 1 for grade in range(2, count + 1)]
    spare, given = total - most - (count - 1), [1] * (count - 1)
    while spare > 0:
        free = [i for i in range(count - 1) if given[i] < most]
        mass, left = sum([weights[i] for i in free]), spare
        for i in free:
            more = min(most - given[i], max(1, left * weights[i] // mass), spare)
            given[i] = given[i] + more
            spare = spare - more
    return np.array([most] + given)


def ragged_sizes(key, number_of, total, bound, skew):
    if number_of == 2:
        one = jax.random.randint(key, (), max(1, total - bound), min(bound, total - 1) + 1)
        return jnp.stack([one, total - one])
    sizes = jnp.asarray(split_up(number_of, total, bound, skew), jnp.int32)
    couples = (number_of - 1) // 2
    source_of, receiver = sizes[1:1 + 2 * couples:2], sizes[2:2 + 2 * couples:2]
    slack = jnp.minimum(source_of - 1, bound - receiver)
    shifted = jax.random.randint(jax.random.fold_in(key, 1), (couples,), 0, 1 << 20) % (slack + 1)
    sizes = sizes.at[1:1 + 2 * couples:2].set(source_of - shifted).at[2:2 + 2 * couples:2].set(receiver + shifted)
    return sizes[jax.random.permutation(jax.random.fold_in(key, 2), number_of)]


def setup_inputs(seed: int = 0) -> dict:
    seeds = jax.random.split(jax.random.key(seed), 3)
    return {
        "embeddings": draw_embeddings(jax.random.fold_in(seeds[2], 71), 0),
        "labels": jnp.searchsorted(jnp.cumsum(ragged_sizes(seeds[1], CLUSTERS, ROWS, LOOK * TOK_DEV + 1, 2)), jnp.arange(ROWS), side="right").astype(jnp.int32),
    }


def normalize(values):
    as_float = values.astype(jnp.float32)
    inverse = lax.rsqrt(lax.optimization_barrier(jnp.mean(as_float * as_float, axis=1, keepdims=True)) + 1e-06)
    return (as_float * inverse / math.sqrt(values.shape[1])).astype(jnp.bfloat16)

def reference(embeddings, labels):
    unit_rows = normalize(embeddings)
    reach = LOOK * TOK_DEV
    padded_rows = jnp.concatenate([jnp.zeros((reach, D), jnp.bfloat16), unit_rows], axis=0)
    padded_labels = jnp.concatenate([jnp.full((reach,), -1, jnp.int32), labels.astype(jnp.int32)], axis=0)

    def one_block(block):
        start_row = (block * TOK_DEV).astype(jnp.int32)
        queries = lax.dynamic_slice_in_dim(unit_rows, start_row, TOK_DEV, 0)
        query_labels = lax.dynamic_slice_in_dim(labels.astype(jnp.int32), start_row, TOK_DEV, 0)
        query_pos = start_row + jnp.arange(TOK_DEV, dtype=jnp.int32)
        keys = lax.dynamic_slice_in_dim(padded_rows, start_row, reach + TOK_DEV, 0)
        key_labels = lax.dynamic_slice_in_dim(padded_labels, start_row, reach + TOK_DEV, 0)
        key_pos = start_row - reach + jnp.arange(reach + TOK_DEV, dtype=jnp.int32)
        scores = lax.dot_general(queries, keys, (((1,), (1,)), ((), ())), preferred_element_type=jnp.float32)
        keep = (key_labels[None, :] == query_labels[:, None]) & (key_pos[None, :] < query_pos[:, None])
        return lax.optimization_barrier(jnp.max(jnp.where(keep, scores, jnp.float32(-1.0)), axis=1))
    blocks = lax.map(one_block, jnp.arange(ROWS // TOK_DEV, dtype=jnp.int32))
    return blocks.reshape(ROWS)
```

```python
import functools
import math

import jax
import jax.numpy as jnp
from jax import lax
from jax.experimental import pallas as pl
from jax.experimental.pallas import tpu as pltpu
from jax.sharding import PartitionSpec as P

F32 = jnp.float32
TILE_Q = 512
TILE_K = 256
VMEM_LIMIT = 48 * 1024 * 1024


def normalize(values):
    as_float = values.astype(F32)
    inverse = lax.rsqrt(jnp.mean(as_float * as_float, axis=1, keepdims=True) + 1e-06)
    return (as_float * inverse / math.sqrt(values.shape[1])).astype(jnp.bfloat16)


def score(keys, queries):
    return lax.dot_general(keys, queries, (((1,), (1,)), ((), ())), preferred_element_type=F32)


def fold(values):
    rows, cols = values.shape
    return jnp.max(values.reshape(rows // 8, 8, cols), axis=0)


def rectangle(keys_ref, queries_ref, out_ref, first_key, query_count):
    tiles = keys_ref.shape[0] // TILE_K

    def over_queries(j, _):
        cols = pl.ds(pl.multiple_of(j * TILE_Q, TILE_Q), TILE_Q)
        queries = queries_ref[cols, :]

        def over_keys(i, best):
            keys = keys_ref[pl.ds(pl.multiple_of(i * TILE_K, TILE_K), TILE_K), :]
            scores = score(keys, queries)
            row = lax.broadcasted_iota(jnp.int32, scores.shape, 0) + i * TILE_K
            return jnp.maximum(best, fold(jnp.where(row >= first_key, scores, -1.0)))

        best = lax.fori_loop(
            first_key // TILE_K, tiles, over_keys, jnp.full((8, TILE_Q), -1.0, F32)
        )
        best = jnp.max(best, axis=0, keepdims=True)
        col = lax.broadcasted_iota(jnp.int32, best.shape, 1) + j * TILE_Q
        out_ref[:, cols] = jnp.maximum(
            out_ref[:, cols], jnp.where(col < query_count, best, -1.0)
        )
        return 0

    lax.fori_loop(0, pl.cdiv(query_count, TILE_Q), over_queries, 0)


def diagonal_kernel(tiles_ref, start_ref, own_ref, out_ref):
    rows = own_ref.shape[0]
    out_ref[...] = jnp.full(out_ref.shape, -1.0, F32)
    for n in range(tiles_ref.shape[0]):
        tile = tiles_ref[n]
        keys = own_ref[pl.ds(pl.multiple_of(tile * TILE_K, TILE_K), TILE_K), :]

        def over_queries(j, _):
            cols = pl.ds(pl.multiple_of(j * TILE_Q, TILE_Q), TILE_Q)
            scores = score(keys, own_ref[cols, :])
            row = lax.broadcasted_iota(jnp.int32, scores.shape, 0) + tile * TILE_K
            col = lax.broadcasted_iota(jnp.int32, scores.shape, 1) + j * TILE_Q
            keep = (row >= start_ref[:, cols]) & (row < col)
            best = jnp.max(fold(jnp.where(keep, scores, -1.0)), axis=0, keepdims=True)
            out_ref[:, cols] = jnp.maximum(out_ref[:, cols], best)
            return 0

        lax.fori_loop(tile * TILE_K // TILE_Q, rows // TILE_Q, over_queries, 0)


def tasks_kernel(tasks, outs, bounds_ref, *refs):
    ins, results = refs[: len(refs) - outs], refs[len(refs) - outs :]
    for result in results:
        result[...] = jnp.full(result.shape, -1.0, F32)
    for n, (keys, queries, result) in enumerate(tasks):
        rectangle(ins[keys], ins[queries], results[result], bounds_ref[2 * n], bounds_ref[2 * n + 1])


def run_tasks(name, tasks, bounds, arrays, widths):
    vmem, smem = pl.BlockSpec(memory_space=pltpu.VMEM), pl.BlockSpec(memory_space=pltpu.SMEM)
    work = sum(arrays[k].shape[0] * arrays[q].shape[0] for k, q, _ in tasks)
    return pl.pallas_call(
        functools.partial(tasks_kernel, tasks, len(widths)),
        out_shape=[jax.ShapeDtypeStruct((1, width), F32) for width in widths],
        in_specs=[smem] + [vmem] * len(arrays),
        out_specs=[vmem] * len(widths),
        compiler_params=pltpu.CompilerParams(vmem_limit_bytes=VMEM_LIMIT),
        cost_estimate=pl.CostEstimate(
            flops=2 * work * arrays[0].shape[1],
            bytes_accessed=sum(a.size * 2 for a in arrays),
            transcendentals=0,
        ),
        name=name,
    )(bounds, *arrays)


def local(embeddings, labels):
    rows = embeddings.shape[0]
    shards, reps = lax.axis_size("shard"), lax.axis_size("rep")
    s, r = lax.axis_index("shard"), lax.axis_index("rep")
    odd = s % 2
    quarter = rows // reps

    def along_shard(block, distance, keep=lambda i: True):
        route = [
            (i, i + distance) for i in range(shards) if i + distance in range(shards) and keep(i)
        ]
        return lax.ppermute(block, "shard", route)

    def partner(block):
        return lax.ppermute(block, "shard", [(i, i ^ 1) for i in range(shards)])

    def other_rep(block, flip):
        return lax.ppermute(block, "rep", [(i, i ^ flip) for i in range(reps)])

    def piece(index):
        return normalize(lax.dynamic_slice_in_dim(embeddings, index * quarter, quarter, 0))

    mine = piece(r)
    half = quarter // 2
    low_a = along_shard(mine[:half], 2)
    low_b = along_shard(mine[half:], 2)
    high = along_shard(mine, -2)
    across = partner(piece(jnp.where(odd == 1, r, r ^ 2)))
    across_index = jnp.where(odd == 1, r ^ 2, r)

    first, last = labels[0], labels[-1]
    head = jnp.sum((labels == first).astype(jnp.int32))
    tail = jnp.sum((labels == last).astype(jnp.int32))
    info = lax.all_gather(jnp.stack([first, last, head, tail]), "shard")

    def bounds(query_shard, key_shard, key_piece, query_offset, query_rows, enabled=True):
        valid = (query_shard < shards) & (key_shard >= 0) & enabled
        query_info = info[jnp.clip(query_shard, 0, shards - 1)]
        key_info = info[jnp.clip(key_shard, 0, shards - 1)]
        valid &= query_info[0] == key_info[1]
        first_key = jnp.clip(rows - key_info[3] - key_piece * quarter, 0, quarter)
        count = jnp.clip(query_info[2] - query_offset, 0, query_rows)
        return [first_key, jnp.where(valid & (first_key < quarter), count, 0)]

    def packed(*pairs):
        return jnp.stack([value for pair in pairs for value in pair]).astype(jnp.int32)

    own = normalize(embeddings)
    index = jnp.arange(rows, dtype=jnp.int32)
    begins = jnp.concatenate([jnp.ones((1,), jnp.bool_), labels[1:] != labels[:-1]])
    start = lax.cummax(jnp.where(begins, index, 0))
    tiles_each = rows // TILE_K // reps
    numbers = [
        r + n * reps if n % 2 == 0 else (n + 1) * reps - 1 - r for n in range(tiles_each)
    ]
    vmem, smem = pl.BlockSpec(memory_space=pltpu.VMEM), pl.BlockSpec(memory_space=pltpu.SMEM)
    best = pl.pallas_call(
        diagonal_kernel,
        out_shape=jax.ShapeDtypeStruct((1, rows), F32),
        in_specs=[smem, vmem, vmem],
        out_specs=vmem,
        compiler_params=pltpu.CompilerParams(vmem_limit_bytes=VMEM_LIMIT),
        cost_estimate=pl.CostEstimate(
            flops=rows * rows * embeddings.shape[1] // reps,
            bytes_accessed=rows * embeddings.shape[1] * 2,
            transcendentals=0,
        ),
        name="diagonal",
    )(jnp.stack(numbers).astype(jnp.int32), start[None, :], own)

    low = jnp.concatenate([low_a, low_b], axis=0)
    across_2 = other_rep(across, 1)
    a0, a1 = across_index, across_index ^ 1
    near = run_tasks(
        "near",
        [(0, 1, 0), (2, 1, 0), (0, 2, 1), (0, 3, 2), (2, 4, 3), (3, 4, 3)],
        packed(
            bounds(s, s - 2, r, 0, rows),
            bounds(s, s - 1, a0, 0, rows, odd == 1),
            bounds(s ^ 1, s - 2, r, a0 * quarter, quarter),
            bounds(s ^ 1, s - 2, r, a1 * quarter, quarter),
            bounds(s + 2, s ^ 1, a0, r * quarter, quarter),
            bounds(s + 2, s ^ 1, a1, r * quarter, quarter),
        ),
        [low, own, across, across_2, high],
        [rows, quarter, quarter, quarter],
    )
    from_partner = [partner(near[1][0]), partner(near[2][0])]

    even_only = lambda i: i % 2 == 0
    high_across = along_shard(high, 1, even_only)
    low_1 = other_rep(low, 1)
    low_2a, low_2b = other_rep(low_a, 2), other_rep(low_b, 2)
    low_2 = jnp.concatenate([low_2a, low_2b], axis=0)
    low_3 = other_rep(low_2, 1)
    far = run_tasks(
        "far",
        [(n, 4, 0) for n in range(4)] + [(n, 5, 1) for n in range(4)],
        packed(
            *[bounds(s + 2, s - 2, r ^ n, r * quarter, quarter) for n in range(4)],
            *[bounds(s + 1, s - 2, r ^ n, r * quarter, quarter, odd == 1) for n in range(4)],
        ),
        [low, low_1, low_2, low_3, high, high_across],
        [quarter, quarter],
    )

    above = along_shard(jnp.maximum(near[3][0], far[0][0]), 2)
    above = jnp.where(s >= 2, above, -1.0)
    across_above = along_shard(far[1][0], 1, lambda i: i % 2 == 1)
    across_above = jnp.where((s >= 2) & (odd == 0), across_above, -1.0)

    def placed(values, index):
        return lax.dynamic_update_slice_in_dim(
            jnp.full((rows,), -1.0, F32), values, index * quarter, 0
        )

    home = jnp.where(odd == 1, r, r ^ 2)
    best = jnp.maximum(best[0], near[0][0])
    best = jnp.maximum(best, placed(from_partner[0], home))
    best = jnp.maximum(best, placed(from_partner[1], home ^ 1))
    best = jnp.maximum(best, placed(jnp.maximum(above, across_above), r))
    return lax.pmax(best, "rep")


def solution(mesh):
    placed = (P("shard", None), P("shard"))
    return jax.shard_map(local, mesh=mesh, in_specs=placed, out_specs=P("shard"), check_vma=False)
```

```python
import functools
import math

import jax
import jax.numpy as jnp
from jax import lax
from jax.experimental import pallas as pl
from jax.experimental.pallas import tpu as pltpu
from jax.sharding import PartitionSpec as P

F32 = jnp.float32
BF16 = jnp.bfloat16
TILE = 256
WIDE = 512
INFO = 16
VMEM_LIMIT = 48 * 1024 * 1024
VMEM = pl.BlockSpec(memory_space=pltpu.VMEM)
SMEM = pl.BlockSpec(memory_space=pltpu.SMEM)


def normalize(values):
    as_float = values.astype(F32)
    inverse = lax.rsqrt(jnp.mean(as_float * as_float, axis=1, keepdims=True) + 1e-06)
    return (as_float * inverse / math.sqrt(values.shape[1])).astype(BF16)


def score(keys, queries):
    return lax.dot_general(keys, queries, (((1,), (1,)), ((), ())), preferred_element_type=F32)


def fold(values):
    rows, cols = values.shape
    return jnp.max(values.reshape(rows // 8, 8, cols), axis=0)


def prepare_kernel(index_ref, mine_ref, across_ref, labels_ref, a_out, b_out, mine_out, across_out):
    labels = labels_ref[...]
    first, last = jnp.min(labels), jnp.max(labels)
    head = jnp.sum((labels == first).astype(jnp.int32))
    tail = jnp.sum((labels == last).astype(jnp.int32))
    row = lax.broadcasted_iota(jnp.int32, (INFO, mine_ref.shape[1]), 0)
    info = jnp.zeros(row.shape, jnp.int32)
    for n, value in enumerate([first, last, head // 16, head % 16, tail // 16, tail % 16]):
        info = jnp.where(row == n, value, info)
    info = info.astype(F32).astype(BF16)
    rows = mine_ref.shape[0]
    half = rows // 2
    for n in range(rows // 128):
        part = normalize(mine_ref[pl.ds(n * 128, 128), :])
        mine_out[pl.ds(n * 128, 128), :] = part
        if n * 128 < half:
            a_out[pl.ds(n * 128, 128), :] = part
        else:
            b_out[pl.ds(n * 128 - half, 128), :] = part
        across_out[pl.ds(n * 128, 128), :] = normalize(across_ref[pl.ds(n * 128, 128), :])
    b_out[pl.ds(half, INFO), :] = info
    mine_out[pl.ds(rows, INFO), :] = info
    across_out[pl.ds(rows, INFO), :] = info


def read_info(ref):
    block = ref[pl.ds(ref.shape[0] - INFO, INFO), pl.ds(0, 128)].astype(F32)

    def scalar(values):
        return jnp.max(values).astype(jnp.int32)

    return (
        scalar(block[0:1]),
        scalar(block[1:2]),
        scalar(block[2:3] * 16 + block[3:4]),
        scalar(block[4:5] * 16 + block[5:6]),
    )


def rectangle(keys_ref, key_rows, queries_ref, query_rows, out_ref, out_at, first_key, count):
    step = min(WIDE, query_rows)
    count = jnp.where(first_key < key_rows, count, 0)

    def over_queries(j, _):
        at = pl.multiple_of(j * step, step)
        queries = queries_ref[pl.ds(at, step), :]

        scores = score(keys_ref[pl.ds(0, key_rows), :], queries)
        row = lax.broadcasted_iota(jnp.int32, scores.shape, 0)
        best = fold(jnp.where(row >= first_key, scores, -1.0))
        best = jnp.max(best, axis=0, keepdims=True)
        col = lax.broadcasted_iota(jnp.int32, best.shape, 1) + at
        cols = pl.ds(pl.multiple_of(out_at + at, TILE), step)
        out_ref[:, cols] = jnp.maximum(out_ref[:, cols], jnp.where(col < count, best, -1.0))
        return 0

    lax.fori_loop(0, (count + step - 1) // step, over_queries, 0)


def own_kernel(place_ref, emb_ref, labels_ref, row_labels_ref, own_out, best_out):
    rows = emb_ref.shape[0]
    for n in range(rows // 128):
        own_out[pl.ds(n * 128, 128), :] = normalize(emb_ref[pl.ds(n * 128, 128), :])
    best_out[...] = jnp.full(best_out.shape, -1.0, F32)
    reps = place_ref[2]
    for n in range(2):
        tile = place_ref[0] if n == 0 else rows // TILE - 1 - place_ref[0]
        at = pl.multiple_of(tile * TILE, TILE)
        keys = own_out[pl.ds(at, TILE), :]
        row_labels = row_labels_ref[pl.ds(at, TILE), :]

        def over_queries(j, _):
            cols = pl.ds(pl.multiple_of(j * WIDE, WIDE), WIDE)
            scores = score(keys, own_out[cols, :])
            row = lax.broadcasted_iota(jnp.int32, scores.shape, 0) + at
            col = lax.broadcasted_iota(jnp.int32, scores.shape, 1) + j * WIDE
            keep = (row_labels == labels_ref[:, cols]) & (row < col)
            best = jnp.max(fold(jnp.where(keep, scores, -1.0)), axis=0, keepdims=True)
            best_out[:, cols] = jnp.maximum(best_out[:, cols], best)
            return 0

        lax.fori_loop(at // WIDE, rows // WIDE, over_queries, 0)


def near_kernel(
    place_ref, own_ref, mine_ref, best_ref, low_a, low_b, low_1a, low_1b, part_a, part_b, high,
    best_out, part_out, high_out,
):
    rows = own_ref.shape[0]
    quarter = part_a.shape[0] - INFO
    half = quarter // 2
    rep, odd, _, part = [place_ref[n] for n in range(4)]
    mine, low, other, up = [read_info(ref) for ref in (mine_ref, low_b, part_a, high)]
    best_out[...] = best_ref[...]
    part_out[...] = jnp.full(part_out.shape, -1.0, F32)
    high_out[...] = jnp.full(high_out.shape, -1.0, F32)

    def reach(query, key, offset, limit):
        count = jnp.clip(query[2] - offset, 0, limit)
        return jnp.where(query[0] == key[1], count, 0)

    def first(key, at, limit):
        return jnp.clip(rows - key[3] - at, 0, limit)

    lows = [(low_a, rep * quarter), (low_b, rep * quarter + half)]
    lows_1 = [(low_1a, (rep ^ 1) * quarter), (low_1b, (rep ^ 1) * quarter + half)]
    for keys, at in lows:
        rectangle(keys, half, own_ref, rows, best_out, 0, first(low, at, half), reach(mine, low, 0, rows))
    count = jnp.where(odd == 1, reach(mine, other, 0, rows), 0)
    rectangle(part_a, quarter, own_ref, rows, best_out, 0, first(other, part * quarter, quarter), count)
    for n, queries in enumerate([part_a, part_b]):
        index = part ^ n
        for keys, at in lows:
            rectangle(
                keys, half, queries, quarter, part_out, n * quarter,
                first(low, at, half), reach(other, low, index * quarter, quarter),
            )
        rectangle(
            queries, quarter, high, quarter, high_out, 0,
            first(other, index * quarter, quarter), reach(up, other, rep * quarter, quarter),
        )
    for keys, at in lows + lows_1:
        rectangle(
            keys, half, high, quarter, high_out, 0,
            first(low, at, half), reach(up, low, rep * quarter, quarter),
        )


def far_kernel(
    place_ref, prior_ref, low_a, low_b, low_1a, low_1b, low_2a, low_2b, low_3a, low_3b,
    high, up_a, up_b, high_out, up_out,
):
    rows = place_ref[4]
    quarter = high.shape[0] - INFO
    half = quarter // 2
    rep = place_ref[0]
    low, up, side = [read_info(ref) for ref in (low_b, high, up_b)]
    high_out[...] = prior_ref[...]
    up_out[...] = jnp.full(up_out.shape, -1.0, F32)

    def reach(query, offset, limit):
        count = jnp.clip(query[2] - offset, 0, limit)
        return jnp.where(query[0] == low[1], count, 0)

    pieces = [(low_a, low_b), (low_1a, low_1b), (low_2a, low_2b), (low_3a, low_3b)]
    for n, pair in enumerate(pieces):
        for m, keys in enumerate(pair):
            at = (rep ^ n) * quarter + m * half
            first = jnp.clip(rows - low[3] - at, 0, half)
            if n >= 2:
                rectangle(keys, half, high, quarter, high_out, 0, first, reach(up, rep * quarter, quarter))
            rectangle(keys, half, up_a, half, up_out, 0, first, reach(side, (rep ^ 2) * quarter, half))
            rectangle(
                keys, half, up_b, half, up_out, half, first, reach(side, rep * quarter + half, half)
            )


def local(embeddings, labels):
    rows, width = embeddings.shape
    shards, reps = lax.axis_size("shard"), lax.axis_size("rep")
    s, r = lax.axis_index("shard"), lax.axis_index("rep")
    odd = s % 2
    quarter = rows // reps
    half = quarter // 2

    def along_shard(block, distance, keep=lambda i: True):
        route = [
            (i, i + distance) for i in range(shards) if i + distance in range(shards) and keep(i)
        ]
        return lax.ppermute(block, "shard", route)

    def partner(block):
        return lax.ppermute(block, "shard", [(i, i ^ 1) for i in range(shards)])

    def other_rep(block, flip):
        return lax.ppermute(block, "rep", [(i, i ^ flip) for i in range(reps)])

    def call(kernel, name, shapes, work, in_specs, *arrays):
        return pl.pallas_call(
            kernel,
            out_shape=[jax.ShapeDtypeStruct(shape, dtype) for shape, dtype in shapes],
            in_specs=in_specs,
            out_specs=[VMEM] * len(shapes),
            compiler_params=pltpu.CompilerParams(vmem_limit_bytes=VMEM_LIMIT),
            cost_estimate=pl.CostEstimate(
                flops=int(2 * work * rows * rows * width),
                bytes_accessed=sum(a.size * a.dtype.itemsize for a in arrays),
                transcendentals=0,
            ),
            name=name,
        )(*arrays)

    sent = jnp.where(odd == 1, r, r ^ 2)
    part = jnp.where(odd == 1, r ^ 2, r)
    place = jnp.stack([r, odd, jnp.int32(reps), part, jnp.int32(rows)]).astype(jnp.int32)
    piece_shape = jax.ShapeDtypeStruct((quarter + INFO, width), BF16)
    piece_spec = pl.BlockSpec((quarter + INFO, width), lambda i, at: (0, 0))
    half_spec = pl.BlockSpec((half, width), lambda i, at: (0, 0))
    tail_spec = pl.BlockSpec((half + INFO, width), lambda i, at: (0, 0))
    mine_a, mine_b, mine, across_mine = pl.pallas_call(
        prepare_kernel,
        out_shape=[
            jax.ShapeDtypeStruct((half, width), BF16),
            jax.ShapeDtypeStruct((half + INFO, width), BF16),
            piece_shape,
            piece_shape,
        ],
        grid_spec=pltpu.PrefetchScalarGridSpec(
            num_scalar_prefetch=1,
            grid=(1,),
            in_specs=[
                pl.BlockSpec((quarter, width), lambda i, at: (at[0], 0)),
                pl.BlockSpec((quarter, width), lambda i, at: (at[1], 0)),
                pl.BlockSpec((rows // 128, 128), lambda i, at: (0, 0)),
            ],
            out_specs=[half_spec, tail_spec, piece_spec, piece_spec],
        ),
        compiler_params=pltpu.CompilerParams(vmem_limit_bytes=VMEM_LIMIT),
        name="prepare",
    )(jnp.stack([r, sent]).astype(jnp.int32), embeddings, embeddings, labels.reshape(rows // 128, 128))

    low_a = along_shard(mine_a, 2)
    high = along_shard(mine, -2)
    across = partner(across_mine)
    low_b = along_shard(mine_b, 2)

    own, best = call(
        own_kernel, "own", [((rows, width), BF16), ((1, rows), F32)], 0.15,
        [SMEM, VMEM, VMEM, VMEM], place, embeddings, labels[None, :], labels[:, None],
    )

    odd_only, even_only = (lambda i: i % 2 == 1), (lambda i: i % 2 == 0)
    low_2a = other_rep(low_a, 2)
    low_1a = other_rep(low_a, 1)
    low_2b = other_rep(low_b, 2)
    up_b = along_shard(high[half:], 1, even_only)
    up_a = along_shard(across[:half], -2, odd_only)
    across_1 = other_rep(across, 1)
    low_1b = other_rep(low_b, 1)
    low_3a = other_rep(low_2a, 1)
    low_3b = other_rep(low_2b, 1)

    best, of_part, of_high = call(
        near_kernel, "near",
        [((1, rows), F32), ((1, 2 * quarter), F32), ((1, quarter), F32)], 0.75,
        [SMEM] + [VMEM] * 10,
        place, own, mine, best, low_a, low_b, low_1a, low_1b, across, across_1, high,
    )
    from_partner = partner(of_part)

    of_high, of_up = call(
        far_kernel, "far", [((1, quarter), F32), ((1, quarter), F32)], 0.4,
        [SMEM] + [VMEM] * 12,
        place, of_high, low_a, low_b, low_1a, low_1b, low_2a, low_2b, low_3a, low_3b,
        high, up_a, up_b,
    )

    above = jnp.where(s >= 2, along_shard(of_high, 2)[0], -1.0)
    beside = jnp.where((s >= 2) & (odd == 0), along_shard(of_up, 1, odd_only)[0], -1.0)

    def placed(values, at):
        return lax.dynamic_update_slice_in_dim(jnp.full((rows,), -1.0, F32), values, at, 0)

    home = jnp.where(odd == 1, r, r ^ 2)
    best = jnp.maximum(best[0], placed(from_partner[0, :quarter], home * quarter))
    best = jnp.maximum(best, placed(from_partner[0, quarter:], (home ^ 1) * quarter))
    best = jnp.maximum(best, placed(above, r * quarter))
    best = jnp.maximum(best, placed(beside[:half], (r ^ 2) * quarter))
    best = jnp.maximum(best, placed(beside[half:], r * quarter + half))
    return lax.pmax(best, "rep")


def solution(mesh):
    placed = (P("shard", None), P("shard"))
    return jax.shard_map(local, mesh=mesh, in_specs=placed, out_specs=P("shard"), check_vma=False)
```

```python
import functools
import math

import jax
import jax.numpy as jnp
from jax import lax
from jax.experimental import pallas as pl
from jax.experimental.pallas import tpu as pltpu
from jax.sharding import PartitionSpec as P

F32 = jnp.float32
BF16 = jnp.bfloat16
TILE = 256
WIDE = 512
INFO = 16
VMEM_LIMIT = 48 * 1024 * 1024
VMEM = pl.BlockSpec(memory_space=pltpu.VMEM)
SMEM = pl.BlockSpec(memory_space=pltpu.SMEM)


def normalize(values):
    as_float = values.astype(F32)
    inverse = lax.rsqrt(jnp.mean(as_float * as_float, axis=1, keepdims=True) + 1e-06)
    return (as_float * inverse / math.sqrt(values.shape[1])).astype(BF16)


def score(keys, queries):
    return lax.dot_general(keys, queries, (((1,), (1,)), ((), ())), preferred_element_type=F32)


def fold(values):
    rows, cols = values.shape
    return jnp.max(values.reshape(rows // 8, 8, cols), axis=0)


def prepare_kernel(index_ref, mine_ref, across_ref, labels_ref, lo_out, lo_info, hi_out, hi_info,
                   across_info, across_out):
    labels = labels_ref[...]
    first, last = jnp.min(labels), jnp.max(labels)
    head = jnp.sum((labels == first).astype(jnp.int32))
    tail = jnp.sum((labels == last).astype(jnp.int32))
    row = lax.broadcasted_iota(jnp.int32, (INFO, mine_ref.shape[1]), 0)
    info = jnp.zeros(row.shape, jnp.int32)
    for n, value in enumerate([first, last, head // 16, head % 16, tail // 16, tail % 16]):
        info = jnp.where(row == n, value, info)
    info = info.astype(F32).astype(BF16)
    half = lo_out.shape[0]
    for n in range(half // 128):
        rows, later = pl.ds(n * 128, 128), pl.ds(half + n * 128, 128)
        lo_out[rows, :] = lo_info[rows, :] = normalize(mine_ref[rows, :])
        hi_out[rows, :] = hi_info[rows, :] = normalize(mine_ref[later, :])
        across_info[rows, :] = normalize(across_ref[rows, :])
        across_out[rows, :] = normalize(across_ref[later, :])
    for ref in (lo_info, hi_info, across_info):
        ref[pl.ds(half, INFO), :] = info


def read_info(ref):
    block = ref[pl.ds(ref.shape[0] - INFO, INFO), pl.ds(0, 128)].astype(F32)

    def scalar(values):
        return jnp.max(values).astype(jnp.int32)

    return (
        scalar(block[0:1]),
        scalar(block[1:2]),
        scalar(block[2:3] * 16 + block[3:4]),
        scalar(block[4:5] * 16 + block[5:6]),
    )


def rectangle(keys_ref, key_rows, queries_ref, query_rows, out_ref, out_at, first_key, count):
    step = min(WIDE, query_rows)
    count = jnp.where(first_key < key_rows, count, 0)

    def over_queries(j, _):
        at = pl.multiple_of(j * step, step)
        queries = queries_ref[pl.ds(at, step), :]

        scores = score(keys_ref[pl.ds(0, key_rows), :], queries)
        row = lax.broadcasted_iota(jnp.int32, scores.shape, 0)
        best = fold(jnp.where(row >= first_key, scores, -1.0))
        best = jnp.max(best, axis=0, keepdims=True)
        col = lax.broadcasted_iota(jnp.int32, best.shape, 1) + at
        cols = pl.ds(pl.multiple_of(out_at + at, TILE), step)
        out_ref[:, cols] = jnp.maximum(out_ref[:, cols], jnp.where(col < count, best, -1.0))
        return 0

    lax.fori_loop(0, (count + step - 1) // step, over_queries, 0)


def own_kernel(place_ref, emb_ref, labels_ref, row_labels_ref, own_out, best_out):
    rows = emb_ref.shape[0]
    for n in range(rows // 128):
        own_out[pl.ds(n * 128, 128), :] = normalize(emb_ref[pl.ds(n * 128, 128), :])
    best_out[...] = jnp.full(best_out.shape, -1.0, F32)
    reps = place_ref[2]
    for n in range(2):
        tile = place_ref[0] if n == 0 else rows // TILE - 1 - place_ref[0]
        at = pl.multiple_of(tile * TILE, TILE)
        keys = own_out[pl.ds(at, TILE), :]
        row_labels = row_labels_ref[pl.ds(at, TILE), :]

        def over_queries(j, _):
            cols = pl.ds(pl.multiple_of(j * WIDE, WIDE), WIDE)
            scores = score(keys, own_out[cols, :])
            row = lax.broadcasted_iota(jnp.int32, scores.shape, 0) + at
            col = lax.broadcasted_iota(jnp.int32, scores.shape, 1) + j * WIDE
            keep = (row_labels == labels_ref[:, cols]) & (row < col)
            best = jnp.max(fold(jnp.where(keep, scores, -1.0)), axis=0, keepdims=True)
            best_out[:, cols] = jnp.maximum(best_out[:, cols], best)
            return 0

        lax.fori_loop(at // WIDE, rows // WIDE, over_queries, 0)


def compare_kernel(names, tasks, outs, fresh, rows, place_ref, *refs):
    count = len(names)
    pieces = dict(zip(names, refs[:count]))
    prior, results = refs[count : len(refs) - len(outs)], refs[len(refs) - len(outs) :]
    results = dict(zip(outs, results))
    for name, ref in zip([name for name in outs if name not in fresh], prior):
        results[name][...] = ref[...]
    for name in fresh:
        results[name][...] = jnp.full(results[name].shape, -1.0, F32)
    quarter = rows // 4
    half = quarter // 2
    rep, odd, _, part = [place_ref[n] for n in range(4)]
    info = {name[5:]: read_info(pieces[name]) for name in names if name.startswith("info_")}

    def where(name):
        kind, tail = name.split("_")
        if kind == "own":
            return 0
        at = half if tail[-1] == "b" else 0
        if kind == "low":
            return (rep ^ int(tail[0])) * quarter + at
        index = {"across": part, "high": rep, "up": rep ^ 2 if tail == "a" else rep}[kind]
        return index * quarter + at

    for keys, queries in tasks:
        key_info, query_info = info[keys.split("_")[0]], info[queries.split("_")[0]]
        limit = rows if queries.startswith("own") else half
        reach = jnp.clip(query_info[2] - where(queries), 0, limit)
        reach = jnp.where(query_info[0] == key_info[1], reach, 0)
        if keys.startswith("across") and queries.startswith("own"):
            reach = jnp.where(odd == 1, reach, 0)
        first = jnp.clip(rows - key_info[3] - where(keys), 0, half)
        out = results[queries.split("_")[0]]
        out_at = half if queries.endswith("_b") else 0
        rectangle(pieces[keys], half, pieces[queries], limit, out, out_at, first, reach)


def merge_kernel(place_ref, best_ref, partner_ref, above_ref, beside_ref, out_ref):
    quarter = above_ref.shape[1]
    half = quarter // 2
    rep, shard, home = [place_ref[n] for n in range(3)]
    out_ref[...] = best_ref[...]

    def raised(at, values):
        cols = pl.ds(pl.multiple_of(at, half), values.shape[1])
        out_ref[:, cols] = jnp.maximum(out_ref[:, cols], values)

    raised(home * quarter, partner_ref[...])
    raised(rep * quarter, jnp.where(shard >= 2, above_ref[...], -1.0))
    beside = jnp.where((shard >= 2) & (shard % 2 == 0), beside_ref[...], -1.0)
    raised((rep ^ 2) * quarter, beside[:, :half])
    raised(rep * quarter + half, beside[:, half:])


def local(embeddings, labels):
    rows, width = embeddings.shape
    shards, reps = lax.axis_size("shard"), lax.axis_size("rep")
    s, r = lax.axis_index("shard"), lax.axis_index("rep")
    odd = s % 2
    quarter = rows // reps
    half = quarter // 2

    def along_shard(block, distance, keep=lambda i: True):
        route = [
            (i, i + distance) for i in range(shards) if i + distance in range(shards) and keep(i)
        ]
        return lax.ppermute(block, "shard", route)

    def partner(block):
        return lax.ppermute(block, "shard", [(i, i ^ 1) for i in range(shards)])

    def other_rep(block, flip):
        return lax.ppermute(block, "rep", [(i, i ^ flip) for i in range(reps)])

    def call(kernel, name, shapes, work, in_specs, *arrays):
        return pl.pallas_call(
            kernel,
            out_shape=[jax.ShapeDtypeStruct(shape, dtype) for shape, dtype in shapes],
            in_specs=in_specs,
            out_specs=[VMEM] * len(shapes),
            compiler_params=pltpu.CompilerParams(vmem_limit_bytes=VMEM_LIMIT),
            cost_estimate=pl.CostEstimate(flops=1024, bytes_accessed=1024, transcendentals=0),
            name=name,
        )(*arrays)

    sent = jnp.where(odd == 1, r ^ 1, r ^ 2)
    part = jnp.where(odd == 1, r ^ 2, r ^ 1)
    place = jnp.stack([r, odd, jnp.int32(reps), part]).astype(jnp.int32)
    sizes = [half, half + INFO, half, half + INFO, half + INFO, half]
    lo, lo_info, hi, hi_info, across_info, across_rest = pl.pallas_call(
        prepare_kernel,
        out_shape=[jax.ShapeDtypeStruct((size, width), BF16) for size in sizes],
        grid_spec=pltpu.PrefetchScalarGridSpec(
            num_scalar_prefetch=1,
            grid=(1,),
            in_specs=[
                pl.BlockSpec((quarter, width), lambda i, at: (at[0], 0)),
                pl.BlockSpec((quarter, width), lambda i, at: (at[1], 0)),
                pl.BlockSpec((rows // 128, 128), lambda i, at: (0, 0)),
            ],
            out_specs=[pl.BlockSpec((size, width), lambda i, at: (0, 0)) for size in sizes],
        ),
        compiler_params=pltpu.CompilerParams(vmem_limit_bytes=VMEM_LIMIT),
        name="prepare",
    )(jnp.stack([r, sent]).astype(jnp.int32), embeddings, embeddings, labels.reshape(rows // 128, 128))

    odd_only, even_only = (lambda i: i % 2 == 1), (lambda i: i % 2 == 0)
    fence = lax.optimization_barrier
    piece = {}

    def compare(name, tasks, infos, prior, outs, work):
        names = sorted({n for task in tasks for n in task})
        arrays = [piece[n] for n in names] + [piece[v] for v in infos.values()]
        names = names + ["info_" + k for k in infos]
        ordered = [k for k in outs if k in prior] + [k for k in outs if k not in prior]
        fresh = [k for k in ordered if k not in prior]
        old = [prior[k] for k in ordered if k in prior]
        shapes = [((1, rows if k == "own" else quarter), F32) for k in ordered]
        given = call(
            functools.partial(compare_kernel, names, tasks, ordered, fresh, rows),
            name, shapes, work, [SMEM] + [VMEM] * (len(arrays) + len(old)),
            place, *arrays, *old,
        )
        return dict(zip(ordered, given))

    piece["low_0a"] = along_shard(lo_info, 2)
    piece["across_a"] = partner(across_info)
    piece["high_b"] = along_shard(hi_info, -2)
    piece["low_0b"] = along_shard(hi, 2)
    piece["high_a"] = along_shard(lo, -2)

    names = ["low_0a", "across_a", "high_b"]
    *fenced, across_rest, own_place = fence(tuple(piece[n] for n in names) + (across_rest, place))
    piece.update(zip(names, fenced))
    piece["across_b"] = partner(across_rest)
    piece["low_2a"] = other_rep(piece["low_0a"], 2)
    piece["up_b"] = along_shard(piece["high_b"], 1, even_only)
    piece["low_1a"] = other_rep(piece["low_0a"], 1)
    own, best = call(
        own_kernel, "own", [((rows, width), BF16), ((1, rows), F32)], 0.15,
        [SMEM, VMEM, VMEM, VMEM], own_place, embeddings, labels[None, :], labels[:, None],
    )
    piece["mine"] = lo_info

    piece["own_x"], piece["mine"] = own, lo_info
    infos = {"own": "mine", "low": "low_0a", "across": "across_a", "high": "high_b"}
    result = compare(
        "near",
        [("low_0a", "own_x"), ("across_a", "own_x"), ("low_0a", "across_a"), ("across_a", "high_b"),
         ("low_0a", "high_b"), ("low_1a", "across_a"), ("low_1a", "high_b")],
        infos, {"own": best}, ["own", "across", "high"], 0.35,
    )

    names = ["low_0b", "high_a", "across_b", "low_1a", "low_2a", "across_a"]
    fenced = fence(tuple(piece[n] for n in names) + (result["high"],))
    piece.update(zip(names, fenced))
    result["high"] = fenced[-1]
    piece["low_2b"] = other_rep(piece["low_0b"], 2)
    piece["up_a"] = along_shard(piece["across_a"], -2, odd_only)
    piece["low_1b"] = other_rep(piece["low_0b"], 1)
    piece["low_3a"] = other_rep(piece["low_2a"], 1)
    near = ["low_0a", "low_0b", "low_1a", "low_2a"]
    result = compare(
        "next",
        [("low_0b", "own_x"), ("across_b", "own_x")]
        + [(k, "across_a") for k in ("low_0b", "low_2a")] + [(k, "across_b") for k in near]
        + [("across_a", "high_a"), ("across_b", "high_a"), ("across_b", "high_b")]
        + [(k, "high_a") for k in near] + [(k, "high_b") for k in ("low_0b", "low_2a")],
        infos, result, ["own", "across", "high"], 0.6,
    )
    piece["low_2b"], result["high"] = fence((piece["low_2b"], result["high"]))
    piece["low_3b"] = other_rep(piece["low_2b"], 1)
    last = ["low_1b", "low_2b", "low_3a", "low_3b"]
    best = result["own"]
    result = compare(
        "far",
        [(k, q) for k in last[:2] for q in ("across_a", "across_b")]
        + [(k, q) for k in last for q in ("high_a", "high_b")]
        + [(k, q) for k in near + last for q in ("up_a", "up_b")],
        {"low": "low_0a", "across": "across_a", "high": "high_b", "up": "up_b"},
        result, ["across", "high", "up"], 0.45,
    )

    above = along_shard(result["high"], 2)
    beside = along_shard(result["up"], 1, odd_only)
    from_partner = partner(result["across"])
    place = jnp.stack([r, s, sent]).astype(jnp.int32)
    (best,) = call(
        merge_kernel, "merge", [((1, rows), F32)], 0.0, [SMEM] + [VMEM] * 4,
        place, best, from_partner, above, beside,
    )
    return lax.pmax(best[0], "rep")


def solution(mesh):
    placed = (P("shard", None), P("shard"))
    return jax.shard_map(local, mesh=mesh, in_specs=placed, out_specs=P("shard"), check_vma=False)
```

```python
import functools
import math

import jax
import jax.numpy as jnp
from jax import lax
from jax.experimental import pallas as pl
from jax.experimental.pallas import tpu as pltpu
from jax.sharding import PartitionSpec as P

F32 = jnp.float32
BF16 = jnp.bfloat16
LOOK = 4
TILE = 256
WIDE = 512
INFO = 16
VMEM_LIMIT = 32 * 1024 * 1024
VMEM = pl.BlockSpec(memory_space=pltpu.VMEM)
SMEM = pl.BlockSpec(memory_space=pltpu.SMEM)


def normalize(values):
    as_float = values.astype(F32)
    inverse = lax.rsqrt(jnp.mean(as_float * as_float, axis=1, keepdims=True) + 1e-06)
    return (as_float * inverse / math.sqrt(values.shape[1])).astype(BF16)


def score(keys, queries):
    return lax.dot_general(keys, queries, (((1,), (1,)), ((), ())), preferred_element_type=F32)


def fold(values):
    rows, cols = values.shape
    return jnp.max(values.reshape(rows // 8, 8, cols), axis=0)


def prepare_kernel(index_ref, mine_ref, labels_ref, lo_out, hi_out):
    labels = labels_ref[...]
    first, last = jnp.min(labels), jnp.max(labels)
    head = jnp.sum((labels == first).astype(jnp.int32))
    tail = jnp.sum((labels == last).astype(jnp.int32))
    row = lax.broadcasted_iota(jnp.int32, (INFO, mine_ref.shape[1]), 0)
    info = jnp.zeros(row.shape, jnp.int32)
    for n, value in enumerate([first, head // 16, head % 16, last, tail // 16, tail % 16]):
        info = jnp.where(row == n, value, info)
    half = hi_out.shape[0]
    for n in range(half // 128):
        at = pl.ds(n * 128, 128)
        lo_out[at, :] = normalize(mine_ref[at, :])
        hi_out[at, :] = normalize(mine_ref[pl.ds(half + n * 128, 128), :])
    lo_out[pl.ds(half, INFO), :] = info.astype(F32).astype(BF16)


def read_reach(ref, at):
    block = ref[pl.ds(ref.shape[0] - INFO, INFO), pl.ds(0, 128)].astype(F32)
    packed = block[at : at + 1] + 256.0 * (16.0 * block[at + 1 : at + 2] + block[at + 2 : at + 3])
    packed = jnp.max(packed).astype(jnp.int32)
    return packed % 256, packed // 256


def own_kernel(place_ref, emb_ref, labels_ref, row_labels_ref, own_out, best_out, reach_out):
    rows = emb_ref.shape[0]
    labels = labels_ref[...]
    first = jnp.min(labels)
    reach_out[0] = first
    reach_out[1] = jnp.sum((labels == first).astype(jnp.int32))
    for n in range(rows // 128):
        own_out[pl.ds(n * 128, 128), :] = normalize(emb_ref[pl.ds(n * 128, 128), :])
    best_out[...] = jnp.full(best_out.shape, -1.0, F32)
    for n in range(2):
        tile = place_ref[0] if n == 0 else rows // TILE - 1 - place_ref[0]
        at = pl.multiple_of(tile * TILE, TILE)
        keys = own_out[pl.ds(at, TILE), :]
        row_labels = row_labels_ref[pl.ds(at, TILE), :]

        def over_queries(j, _):
            cols = pl.ds(pl.multiple_of(j * WIDE, WIDE), WIDE)
            scores = score(keys, own_out[cols, :])
            row = lax.broadcasted_iota(jnp.int32, scores.shape, 0) + at
            col = lax.broadcasted_iota(jnp.int32, scores.shape, 1) + j * WIDE
            keep = (row_labels == labels_ref[:, cols]) & (row < col)
            best = jnp.max(fold(jnp.where(keep, scores, -1.0)), axis=0, keepdims=True)
            best_out[:, cols] = jnp.maximum(best_out[:, cols], best)
            return 0

        lax.fori_loop(at // WIDE, rows // WIDE, over_queries, 0)


def earlier_kernel(fresh, base, place_ref, own_reach, own_ref, best_ref, keys_ref, *refs):
    reach_in, (best_out, reach_out) = (None, refs) if fresh else (refs[0], refs[1:])
    step = pl.program_id(0)
    rows, half = own_ref.shape[0], TILE

    @pl.when(step == 0)
    def _():
        best_out[...] = best_ref[...]

    if fresh:
        label, tail = read_reach(keys_ref, 3)
        reach_out[2 * step], reach_out[2 * step + 1] = label, tail
    else:
        label, tail = reach_in[2 * step], reach_in[2 * step + 1]
        reach_out[2 * step], reach_out[2 * step + 1] = label, tail
    count = jnp.where((place_ref[step] >= 0) & (label == own_reach[0]), own_reach[1], 0)
    first = rows - tail - place_ref[LOOK] * 2 * half - base
    count = jnp.where(first < half, count, 0)

    def over_queries(j, _):
        at = pl.multiple_of(j * WIDE, WIDE)
        scores = score(keys_ref[pl.ds(0, half), :], own_ref[pl.ds(at, WIDE), :])
        index = lax.broadcasted_iota(jnp.int32, scores.shape, 0)
        best = jnp.max(fold(jnp.where(index >= first, scores, -1.0)), axis=0, keepdims=True)
        col = lax.broadcasted_iota(jnp.int32, best.shape, 1) + at
        cols = pl.ds(at, WIDE)
        best_out[:, cols] = jnp.maximum(best_out[:, cols], jnp.where(col < count, best, -1.0))
        return 0

    lax.fori_loop(0, (count + WIDE - 1) // WIDE, over_queries, 0)


def local(embeddings, labels):
    rows, width = embeddings.shape
    shards, reps = lax.axis_size("shard"), lax.axis_size("rep")
    s, r = lax.axis_index("shard"), lax.axis_index("rep")
    quarter = rows // reps
    half = quarter // 2
    params = pltpu.CompilerParams(vmem_limit_bytes=VMEM_LIMIT)
    streamed = pltpu.CompilerParams(vmem_limit_bytes=60 * 1024 * 1024)
    small = pl.CostEstimate(flops=1024, bytes_accessed=1024, transcendentals=0)

    sizes = [half + INFO, half]
    lo, hi = pl.pallas_call(
        prepare_kernel,
        out_shape=[jax.ShapeDtypeStruct((size, width), BF16) for size in sizes],
        grid_spec=pltpu.PrefetchScalarGridSpec(
            num_scalar_prefetch=1,
            grid=(1,),
            in_specs=[
                pl.BlockSpec((quarter, width), lambda i, at: (at[0], 0)),
                pl.BlockSpec((rows // 128, 128), lambda i, at: (0, 0)),
            ],
            out_specs=[pl.BlockSpec((size, width), lambda i, at: (0, 0)) for size in sizes],
        ),
        compiler_params=streamed,
        name="prepare",
    )(r[None].astype(jnp.int32), embeddings, labels.reshape(rows // 128, 128))

    whole = shards <= 2 * LOOK

    def earlier(piece):
        if whole:
            return lax.all_gather(piece, "shard")
        pieces = [
            lax.ppermute(piece, "shard", [(i, i + n) for i in range(shards - n)])
            for n in range(1, LOOK + 1)
        ]
        return jnp.stack(pieces)

    lo_all, hi_all = earlier(lo), earlier(hi)

    own, best, own_reach = pl.pallas_call(
        own_kernel,
        out_shape=[
            jax.ShapeDtypeStruct((rows, width), BF16),
            jax.ShapeDtypeStruct((1, rows), F32),
            jax.ShapeDtypeStruct((2,), jnp.int32),
        ],
        in_specs=[SMEM, VMEM, VMEM, VMEM],
        out_specs=[VMEM, VMEM, SMEM],
        compiler_params=params,
        cost_estimate=small,
        name="own",
    )(r[None].astype(jnp.int32), embeddings, labels[None, :], labels[:, None])

    shard_of = s - 1 - jnp.arange(LOOK, dtype=jnp.int32)
    place = jnp.concatenate([shard_of, r[None]]).astype(jnp.int32)

    def against(pieces, best, reach):
        size = pieces.shape[1]
        which = lambda i, at: (jnp.maximum(at[i], 0) if whole else i, 0, 0)
        full = pl.BlockSpec((rows, width), lambda i, at: (0, 0))
        line = pl.BlockSpec((1, rows), lambda i, at: (0, 0))
        fresh = reach is None
        return pl.pallas_call(
            functools.partial(earlier_kernel, fresh, 0 if fresh else half),
            out_shape=[
                jax.ShapeDtypeStruct((1, rows), F32),
                jax.ShapeDtypeStruct((2 * LOOK,), jnp.int32),
            ],
            grid_spec=pltpu.PrefetchScalarGridSpec(
                num_scalar_prefetch=1,
                grid=(LOOK,),
                in_specs=[SMEM, full, line, pl.BlockSpec((None, size, width), which)]
                + ([] if fresh else [SMEM]),
                out_specs=[line, SMEM],
            ),
            compiler_params=streamed,
            cost_estimate=small,
            name="earlier",
        )(place, own_reach, own, best, pieces, *([] if fresh else [reach]))

    best, reach = against(lo_all, best, None)
    best, _ = against(hi_all, best, reach)
    return lax.pmax(best[0], "rep")


def solution(mesh):
    placed = (P("shard", None), P("shard"))
    return jax.shard_map(local, mesh=mesh, in_specs=placed, out_specs=P("shard"), check_vma=False)
```

```python
import functools
import math

import jax
import jax.numpy as jnp
from jax import lax
from jax.experimental import pallas as pl
from jax.experimental.pallas import tpu as pltpu
from jax.sharding import PartitionSpec as P

F32 = jnp.float32
BF16 = jnp.bfloat16
TILE = 256
WIDE = 512
INFO = 16
VMEM_LIMIT = 32 * 1024 * 1024
VMEM = pl.BlockSpec(memory_space=pltpu.VMEM)
SMEM = pl.BlockSpec(memory_space=pltpu.SMEM)


def normalize(values):
    as_float = values.astype(F32)
    inverse = lax.rsqrt(jnp.mean(as_float * as_float, axis=1, keepdims=True) + 1e-06)
    return (as_float * inverse / math.sqrt(values.shape[1])).astype(BF16)


def score(keys, queries):
    return lax.dot_general(keys, queries, (((1,), (1,)), ((), ())), preferred_element_type=F32)


def fold(values):
    rows, cols = values.shape
    return jnp.max(values.reshape(rows // 8, 8, cols), axis=0)


def prepare_kernel(index_ref, mine_ref, across_ref, labels_ref, lo_out, hi_out, mine_out, across_out):
    labels = labels_ref[...]
    first, last = jnp.min(labels), jnp.max(labels)
    head = jnp.sum((labels == first).astype(jnp.int32))
    tail = jnp.sum((labels == last).astype(jnp.int32))
    row = lax.broadcasted_iota(jnp.int32, (INFO, mine_ref.shape[1]), 0)
    info = jnp.zeros(row.shape, jnp.int32)
    for n, value in enumerate([first, head // 16, head % 16, last, tail // 16, tail % 16]):
        info = jnp.where(row == n, value, info)
    info = info.astype(F32).astype(BF16)
    rows = mine_ref.shape[0]
    half = lo_out.shape[0]
    for n in range(rows // 128):
        at = pl.ds(n * 128, 128)
        values = normalize(mine_ref[at, :])
        mine_out[at, :] = values
        if n * 128 < half:
            lo_out[at, :] = values
        else:
            hi_out[pl.ds(n * 128 - half, 128), :] = values
        across_out[at, :] = normalize(across_ref[at, :])
    hi_out[pl.ds(half, INFO), :] = info
    mine_out[pl.ds(rows, INFO), :] = info
    across_out[pl.ds(rows, INFO), :] = info


def read_reach(ref, at):
    block = ref[pl.ds(ref.shape[0] - INFO, INFO), pl.ds(0, 128)].astype(F32)
    packed = block[at : at + 1] + 256.0 * (16.0 * block[at + 1 : at + 2] + block[at + 2 : at + 3])
    packed = jnp.max(packed).astype(jnp.int32)
    return packed % 256, packed // 256


def group(keys, queries_ref, query_rows, out_ref, out_at, count):
    step = min(WIDE, query_rows)

    def over_queries(j, _):
        at = pl.multiple_of(j * step, step)
        queries = queries_ref[pl.ds(at, step), :]
        best = None
        for ref, row, rows, first in keys:
            scores = score(ref[pl.ds(row, rows), :], queries)
            index = lax.broadcasted_iota(jnp.int32, scores.shape, 0)
            top = fold(jnp.where(index >= first, scores, -1.0))
            best = top if best is None else jnp.maximum(best, top)
        best = jnp.max(best, axis=0, keepdims=True)
        col = lax.broadcasted_iota(jnp.int32, best.shape, 1) + at
        cols = pl.ds(pl.multiple_of(out_at + at, TILE), step)
        out_ref[:, cols] = jnp.maximum(out_ref[:, cols], jnp.where(col < count, best, -1.0))
        return 0

    lax.fori_loop(0, (count + step - 1) // step, over_queries, 0)


def own_kernel(place_ref, emb_ref, labels_ref, row_labels_ref, own_out, best_out, reach_out):
    rows = emb_ref.shape[0]
    labels = labels_ref[...]
    first = jnp.min(labels)
    reach_out[0] = first
    reach_out[1] = jnp.sum((labels == first).astype(jnp.int32))
    for n in range(rows // 128):
        own_out[pl.ds(n * 128, 128), :] = normalize(emb_ref[pl.ds(n * 128, 128), :])
    best_out[...] = jnp.full(best_out.shape, -1.0, F32)
    for n in range(2):
        tile = place_ref[0] if n == 0 else rows // TILE - 1 - place_ref[0]
        at = pl.multiple_of(tile * TILE, TILE)
        keys = own_out[pl.ds(at, TILE), :]
        row_labels = row_labels_ref[pl.ds(at, TILE), :]

        def over_queries(j, _):
            cols = pl.ds(pl.multiple_of(j * WIDE, WIDE), WIDE)
            scores = score(keys, own_out[cols, :])
            row = lax.broadcasted_iota(jnp.int32, scores.shape, 0) + at
            col = lax.broadcasted_iota(jnp.int32, scores.shape, 1) + j * WIDE
            keep = (row_labels == labels_ref[:, cols]) & (row < col)
            best = jnp.max(fold(jnp.where(keep, scores, -1.0)), axis=0, keepdims=True)
            best_out[:, cols] = jnp.maximum(best_out[:, cols], best)
            return 0

        lax.fori_loop(at // WIDE, rows // WIDE, over_queries, 0)


def reached(query, key, offset, limit):
    count = jnp.clip(query[1] - offset, 0, limit)
    return jnp.where(query[0] == key[0], count, 0)


def lower_keys(rep, tail, rows, pieces):
    half = rows // 8
    return [
        (ref, 0, half, jnp.clip(rows - tail - (rep ^ flip) * 2 * half - part * half, 0, half))
        for ref, flip, part in pieces
    ]


def near_kernel(place_ref, own_reach, own_ref, best_ref, low_0a, low_0b, low_1a, low_2a, across, high,
                best_out, across_out, high_out, reach_out):
    rows = own_ref.shape[0]
    quarter = across.shape[0] - INFO
    rep, odd, part = [place_ref[n] for n in range(3)]
    mine = (own_reach[0], own_reach[1])
    low, beside_head = read_reach(low_0b, 3), read_reach(across, 0)
    beside_tail, up = read_reach(across, 3), read_reach(high, 0)
    for n, value in enumerate(low + beside_head + up):
        reach_out[n] = value
    best_out[...] = best_ref[...]
    across_out[...] = jnp.full(across_out.shape, -1.0, F32)
    high_out[...] = jnp.full(high_out.shape, -1.0, F32)

    lows = lower_keys(
        rep, low[1], rows, [(low_0a, 0, 0), (low_0b, 0, 1), (low_1a, 1, 0), (low_2a, 2, 0)]
    )
    besides = [
        (across, 0, quarter, jnp.clip(rows - beside_tail[1] - part * quarter, 0, quarter))
    ]
    group(lows[:2], own_ref, rows, best_out, 0, reached(mine, low, 0, rows))
    count = jnp.where(odd == 1, reached(mine, beside_tail, 0, rows), 0)
    group(besides, own_ref, rows, best_out, 0, count)
    group(lows, across, quarter, across_out, 0, reached(beside_head, low, part * quarter, quarter))
    group(besides, high, quarter, high_out, 0, reached(up, beside_tail, rep * quarter, quarter))
    group(lows, high, quarter, high_out, 0, reached(up, low, rep * quarter, quarter))


def far_kernel(place_ref, reach_ref, across_ref, high_ref, low_0a, low_0b, low_1a, low_1b, low_2a,
               low_2b, low_3a, across, high, up_a, up_b, across_out, high_out, up_out, side_out):
    quarter = across.shape[0] - INFO
    half = quarter // 2
    rep, _, part = [place_ref[n] for n in range(3)]
    low, beside, up = [(reach_ref[2 * n], reach_ref[2 * n + 1]) for n in range(3)]
    side = read_reach(up_b, 0)
    side_out[0], side_out[1] = side
    across_out[...] = across_ref[...]
    high_out[...] = high_ref[...]
    up_out[...] = jnp.full(up_out.shape, -1.0, F32)

    lows = lower_keys(
        rep, low[1], 4 * quarter,
        [(low_1b, 1, 1), (low_2b, 2, 1), (low_3a, 3, 0), (low_0a, 0, 0), (low_0b, 0, 1), (low_1a, 1, 0), (low_2a, 2, 0)],
    )
    group(lows[:2], across, quarter, across_out, 0, reached(beside, low, part * quarter, quarter))
    group(lows[:3], high, quarter, high_out, 0, reached(up, low, rep * quarter, quarter))
    group(lows, up_a, half, up_out, 0, reached(side, low, (rep ^ 2) * quarter, half))
    group(lows, up_b, half, up_out, half, reached(side, low, rep * quarter + half, half))


def last_kernel(place_ref, reach_ref, side_ref, high_ref, up_ref, low_3b, high, up_a, up_b,
                high_out, up_out):
    half = up_a.shape[0]
    quarter = 2 * half
    rep = place_ref[0]
    low, up = (reach_ref[0], reach_ref[1]), (reach_ref[4], reach_ref[5])
    side = (side_ref[0], side_ref[1])
    high_out[...], up_out[...] = high_ref[...], up_ref[...]
    lows = lower_keys(rep, low[1], 4 * quarter, [(low_3b, 3, 1)])
    group(lows, high, quarter, high_out, 0, reached(up, low, rep * quarter, quarter))
    group(lows, up_a, half, up_out, 0, reached(side, low, (rep ^ 2) * quarter, half))
    group(lows, up_b, half, up_out, half, reached(side, low, rep * quarter + half, half))


def merge_kernel(place_ref, best_ref, partner_ref, above_ref, beside_ref, out_ref):
    quarter = above_ref.shape[1]
    half = quarter // 2
    rep, shard, home = [place_ref[n] for n in range(3)]
    out_ref[...] = best_ref[...]

    def raised(at, values):
        cols = pl.ds(pl.multiple_of(at, half), values.shape[1])
        out_ref[:, cols] = jnp.maximum(out_ref[:, cols], values)

    raised(home * quarter, partner_ref[...])
    raised(rep * quarter, jnp.where(shard >= 2, above_ref[...], -1.0))
    beside = jnp.where((shard >= 2) & (shard % 2 == 0), beside_ref[...], -1.0)
    raised((rep ^ 2) * quarter, beside[:, :half])
    raised(rep * quarter + half, beside[:, half:])


def local(embeddings, labels):
    rows, width = embeddings.shape
    shards, reps = lax.axis_size("shard"), lax.axis_size("rep")
    s, r = lax.axis_index("shard"), lax.axis_index("rep")
    odd = s % 2
    quarter = rows // reps
    half = quarter // 2

    def along_shard(block, distance, keep=lambda i: True):
        route = [
            (i, i + distance) for i in range(shards) if i + distance in range(shards) and keep(i)
        ]
        return lax.ppermute(block, "shard", route)

    def partner(block):
        return lax.ppermute(block, "shard", [(i, i ^ 1) for i in range(shards)])

    def other_rep(block, flip):
        return lax.ppermute(block, "rep", [(i, i ^ flip) for i in range(reps)])

    def call(kernel, name, shapes, specs, *arrays):
        return pl.pallas_call(
            kernel,
            out_shape=[jax.ShapeDtypeStruct(shape, dtype) for shape, dtype in shapes],
            in_specs=specs[: len(arrays)],
            out_specs=specs[len(arrays) :],
            compiler_params=pltpu.CompilerParams(vmem_limit_bytes=VMEM_LIMIT),
            cost_estimate=pl.CostEstimate(flops=1024, bytes_accessed=1024, transcendentals=0),
            name=name,
        )(*arrays)

    sent = jnp.where(odd == 1, r ^ 1, r ^ 2)
    part = jnp.where(odd == 1, r ^ 2, r ^ 1)
    place = jnp.stack([r, odd, part]).astype(jnp.int32)
    sizes = [half, half + INFO, quarter + INFO, quarter + INFO]
    lo, hi, whole, across = pl.pallas_call(
        prepare_kernel,
        out_shape=[jax.ShapeDtypeStruct((size, width), BF16) for size in sizes],
        grid_spec=pltpu.PrefetchScalarGridSpec(
            num_scalar_prefetch=1,
            grid=(1,),
            in_specs=[
                pl.BlockSpec((quarter, width), lambda i, at: (at[0], 0)),
                pl.BlockSpec((quarter, width), lambda i, at: (at[1], 0)),
                pl.BlockSpec((rows // 128, 128), lambda i, at: (0, 0)),
            ],
            out_specs=[pl.BlockSpec((size, width), lambda i, at: (0, 0)) for size in sizes],
        ),
        compiler_params=pltpu.CompilerParams(vmem_limit_bytes=60 * 1024 * 1024),
        name="prepare",
    )(jnp.stack([r, sent]).astype(jnp.int32), embeddings, embeddings, labels.reshape(rows // 128, 128))

    odd_only, even_only = (lambda i: i % 2 == 1), (lambda i: i % 2 == 0)
    fence = lax.optimization_barrier

    low_0a = along_shard(lo, 2)
    across = partner(across)
    high = along_shard(whole, -2)
    low_0b = along_shard(hi, 2)

    own, best, own_reach = call(
        own_kernel, "own", [((rows, width), BF16), ((1, rows), F32), ((2,), jnp.int32)],
        [SMEM] + [VMEM] * 5 + [SMEM],
        place, embeddings, labels[None, :], labels[:, None],
    )

    low_0a, own, best = fence((low_0a, own, best))
    low_2a = other_rep(low_0a, 2)
    low_1a = other_rep(low_0a, 1)
    across, high, low_0b, low_1a, low_2a = fence((across, high, low_0b, low_1a, low_2a))
    low_2b = other_rep(low_0b, 2)
    up_b = along_shard(high[half:], 1, even_only)
    up_a = along_shard(across[:half], -2, odd_only)
    low_1b = other_rep(low_0b, 1)
    low_3a = other_rep(low_2a, 1)
    results = [((1, quarter), F32)] * 2
    best, of_across, of_high, reach = call(
        near_kernel, "near", [((1, rows), F32)] + results + [((6,), jnp.int32)],
        [SMEM] * 2 + [VMEM] * 11 + [SMEM],
        place, own_reach, own, best, low_0a, low_0b, low_1a, low_2a, across, high,
    )
    low_2b, up_a, up_b, low_1b, low_3a, of_across = fence(
        (low_2b, up_a, up_b, low_1b, low_3a, of_across)
    )
    low_3b = other_rep(low_2b, 1)
    of_across, of_high, of_up, side = call(
        far_kernel, "far", results + [((1, quarter), F32), ((2,), jnp.int32)],
        [SMEM] * 2 + [VMEM] * 16 + [SMEM],
        place, reach, of_across, of_high, low_0a, low_0b, low_1a, low_1b, low_2a, low_2b,
        low_3a, across, high, up_a, up_b,
    )
    of_high, of_up = call(
        last_kernel, "last", results, [SMEM] * 3 + [VMEM] * 8,
        place, reach, side, of_high, of_up, low_3b, high, up_a, up_b,
    )

    above = along_shard(of_high, 2)
    beside = along_shard(of_up, 1, odd_only)
    from_partner = partner(of_across)
    place = jnp.stack([r, s, sent]).astype(jnp.int32)
    (best,) = call(
        merge_kernel, "merge", [((1, rows), F32)], [SMEM] + [VMEM] * 5,
        place, best, from_partner, above, beside,
    )
    return lax.pmax(best[0], "rep")


def solution(mesh):
    placed = (P("shard", None), P("shard"))
    return jax.shard_map(local, mesh=mesh, in_specs=placed, out_specs=P("shard"), check_vma=False)
```

```python
import functools
import math

import jax
import jax.numpy as jnp
from jax import lax
from jax.experimental import pallas as pl
from jax.experimental.pallas import tpu as pltpu
from jax.sharding import PartitionSpec as P

F32 = jnp.float32
BF16 = jnp.bfloat16
TILE = 256
WIDE = 512
INFO = 16
VMEM_LIMIT = 32 * 1024 * 1024
PREPARE_LIMIT = 60 * 1024 * 1024
VMEM = pl.BlockSpec(memory_space=pltpu.VMEM)
SMEM = pl.BlockSpec(memory_space=pltpu.SMEM)


def normalize(values):
    as_float = values.astype(F32)
    inverse = lax.rsqrt(jnp.mean(as_float * as_float, axis=1, keepdims=True) + 1e-06)
    return (as_float * inverse / math.sqrt(values.shape[1])).astype(BF16)


def score(keys, queries):
    return lax.dot_general(keys, queries, (((1,), (1,)), ((), ())), preferred_element_type=F32)


def fold(values):
    rows, cols = values.shape
    return jnp.max(values.reshape(rows // 8, 8, cols), axis=0)


def position():
    rep, odd = lax.axis_index("rep"), lax.axis_index("shard") % 2
    return rep, odd, rep ^ (1 + odd)


def prepare_kernel(emb_ref, labels_ref, mine_out, across_out, raw, sems):
    rep, odd, _ = position()
    quarter = mine_out.shape[0] - INFO
    part = quarter // 2
    copies = []
    for n in range(4):
        piece = rep if n < 2 else rep ^ (2 - odd)
        at = pl.multiple_of(piece * quarter + (n % 2) * part, part)
        copies.append(pltpu.make_async_copy(emb_ref.at[pl.ds(at, part), :], raw.at[n], sems.at[n]))
        copies[-1].start()
    labels = labels_ref[...]
    first, last = jnp.min(labels), jnp.max(labels)
    head = jnp.sum((labels == first).astype(jnp.int32))
    tail = jnp.sum((labels == last).astype(jnp.int32))
    row = lax.broadcasted_iota(jnp.int32, (INFO, mine_out.shape[1]), 0)
    info = jnp.zeros(row.shape, jnp.int32)
    for n, value in enumerate([first, head // 16, head % 16, last, tail // 16, tail % 16]):
        info = jnp.where(row == n, value, info)
    info = info.astype(F32).astype(BF16)
    for n, copy in enumerate(copies):
        copy.wait()
        out = mine_out if n < 2 else across_out
        for m in range(part // 128):
            rows = pl.ds((n % 2) * part + m * 128, 128)
            out[rows, :] = normalize(raw[n, pl.ds(m * 128, 128), :])
    mine_out[pl.ds(quarter, INFO), :] = info
    across_out[pl.ds(quarter, INFO), :] = info


def read_reach(ref, at):
    block = ref[pl.ds(ref.shape[0] - INFO, INFO), pl.ds(0, 128)].astype(F32)
    packed = block[at : at + 1] + 256.0 * (16.0 * block[at + 1 : at + 2] + block[at + 2 : at + 3])
    packed = jnp.max(packed).astype(jnp.int32)
    return packed % 256, packed // 256


def group(keys, queries_ref, query_rows, out_ref, out_at, count):
    step = min(WIDE, query_rows)

    def over_queries(j, _):
        at = pl.multiple_of(j * step, step)
        queries = queries_ref[pl.ds(at, step), :]
        best = None
        for ref, row, rows, first in keys:
            scores = score(ref[pl.ds(row, rows), :], queries)
            index = lax.broadcasted_iota(jnp.int32, scores.shape, 0)
            top = fold(jnp.where(index >= first, scores, -1.0))
            best = top if best is None else jnp.maximum(best, top)
        best = jnp.max(best, axis=0, keepdims=True)
        col = lax.broadcasted_iota(jnp.int32, best.shape, 1) + at
        cols = pl.ds(pl.multiple_of(out_at + at, TILE), step)
        out_ref[:, cols] = jnp.maximum(out_ref[:, cols], jnp.where(col < count, best, -1.0))
        return 0

    lax.fori_loop(0, (count + step - 1) // step, over_queries, 0)


def own_kernel(emb_ref, labels_ref, row_labels_ref, own_out, best_out, reach_out):
    rows = emb_ref.shape[0]
    rep = lax.axis_index("rep")
    labels = labels_ref[...]
    first = jnp.min(labels)
    reach_out[0] = first
    reach_out[1] = jnp.sum((labels == first).astype(jnp.int32))
    for n in range(rows // 128):
        own_out[pl.ds(n * 128, 128), :] = normalize(emb_ref[pl.ds(n * 128, 128), :])
    best_out[...] = jnp.full(best_out.shape, -1.0, F32)
    for n in range(2):
        tile = rep if n == 0 else rows // TILE - 1 - rep
        at = pl.multiple_of(tile * TILE, TILE)
        keys = own_out[pl.ds(at, TILE), :]
        row_labels = row_labels_ref[pl.ds(at, TILE), :]

        def over_queries(j, _):
            cols = pl.ds(pl.multiple_of(j * WIDE, WIDE), WIDE)
            scores = score(keys, own_out[cols, :])
            row = lax.broadcasted_iota(jnp.int32, scores.shape, 0) + at
            col = lax.broadcasted_iota(jnp.int32, scores.shape, 1) + j * WIDE
            keep = (row_labels == labels_ref[:, cols]) & (row < col)
            best = jnp.max(fold(jnp.where(keep, scores, -1.0)), axis=0, keepdims=True)
            best_out[:, cols] = jnp.maximum(best_out[:, cols], best)
            return 0

        lax.fori_loop(at // WIDE, rows // WIDE, over_queries, 0)


def reached(query, key, offset, limit):
    count = jnp.clip(query[1] - offset, 0, limit)
    return jnp.where(query[0] == key[0], count, 0)


def lower_keys(rep, tail, quarter, pieces):
    return [
        (ref, 0, quarter, jnp.clip(4 * quarter - tail - (rep ^ flip) * quarter, 0, quarter))
        for ref, flip in pieces
    ]


def near_kernel(own_reach, own_ref, best_ref, low_0, low_1, across, high,
                best_out, across_out, high_out, reach_out):
    rows = own_ref.shape[0]
    quarter = across.shape[0] - INFO
    rep, odd, part = position()
    mine = (own_reach[0], own_reach[1])
    low, beside_head = read_reach(low_0, 3), read_reach(across, 0)
    beside_tail, up = read_reach(across, 3), read_reach(high, 0)
    for n, value in enumerate(low + beside_head + up):
        reach_out[n] = value
    best_out[...] = best_ref[...]
    across_out[...] = jnp.full(across_out.shape, -1.0, F32)
    high_out[...] = jnp.full(high_out.shape, -1.0, F32)

    lows = lower_keys(rep, low[1], quarter, [(low_0, 0), (low_1, 1)])
    besides = [
        (across, 0, quarter, jnp.clip(rows - beside_tail[1] - part * quarter, 0, quarter))
    ]
    group(lows[:1], own_ref, rows, best_out, 0, reached(mine, low, 0, rows))
    count = jnp.where(odd == 1, reached(mine, beside_tail, 0, rows), 0)
    group(besides, own_ref, rows, best_out, 0, count)
    group(lows, across, quarter, across_out, 0, reached(beside_head, low, part * quarter, quarter))
    group(besides, high, quarter, high_out, 0, reached(up, beside_tail, rep * quarter, quarter))
    group(lows, high, quarter, high_out, 0, reached(up, low, rep * quarter, quarter))


def far_kernel(reach_ref, across_ref, high_ref, low_0, low_1, low_2, across, high, up_a, up_b,
               across_out, high_out, up_out, side_out):
    quarter = across.shape[0] - INFO
    half = quarter // 2
    rep, _, part = position()
    low, beside, up = [(reach_ref[2 * n], reach_ref[2 * n + 1]) for n in range(3)]
    side = read_reach(up_b, 0)
    side_out[0], side_out[1] = side
    across_out[...] = across_ref[...]
    high_out[...] = high_ref[...]
    up_out[...] = jnp.full(up_out.shape, -1.0, F32)
    lows = lower_keys(rep, low[1], quarter, [(low_2, 2), (low_0, 0), (low_1, 1)])
    group(lows[:1], across, quarter, across_out, 0, reached(beside, low, part * quarter, quarter))
    group(lows[:1], high, quarter, high_out, 0, reached(up, low, rep * quarter, quarter))
    group(lows, up_a, half, up_out, 0, reached(side, low, (rep ^ 2) * quarter, half))
    group(lows, up_b, half, up_out, half, reached(side, low, rep * quarter + half, half))


def last_kernel(reach_ref, side_ref, high_ref, up_ref, low_3, high, up_a, up_b, high_out, up_out):
    half = up_a.shape[0]
    quarter = 2 * half
    rep = lax.axis_index("rep")
    low, up = (reach_ref[0], reach_ref[1]), (reach_ref[4], reach_ref[5])
    side = (side_ref[0], side_ref[1])
    high_out[...], up_out[...] = high_ref[...], up_ref[...]
    lows = lower_keys(rep, low[1], quarter, [(low_3, 3)])
    group(lows, high, quarter, high_out, 0, reached(up, low, rep * quarter, quarter))
    group(lows, up_a, half, up_out, 0, reached(side, low, (rep ^ 2) * quarter, half))
    group(lows, up_b, half, up_out, half, reached(side, low, rep * quarter + half, half))


def merge_kernel(best_ref, partner_ref, above_ref, beside_ref, out_ref):
    quarter = above_ref.shape[1]
    half = quarter // 2
    rep, odd, _ = position()
    inside = lax.axis_index("shard") >= 2
    out_ref[...] = best_ref[...]

    def raised(at, values):
        cols = pl.ds(pl.multiple_of(at, half), values.shape[1])
        out_ref[:, cols] = jnp.maximum(out_ref[:, cols], values)

    raised((rep ^ (2 - odd)) * quarter, partner_ref[...])
    raised(rep * quarter, jnp.where(inside, above_ref[...], -1.0))
    beside = jnp.where(inside & (odd == 0), beside_ref[...], -1.0)
    raised((rep ^ 2) * quarter, beside[:, :half])
    raised(rep * quarter + half, beside[:, half:])


def local(embeddings, labels):
    rows, width = embeddings.shape
    shards, reps = lax.axis_size("shard"), lax.axis_size("rep")
    quarter = rows // reps
    half = quarter // 2

    def along_shard(block, distance, keep=lambda i: True):
        route = [
            (i, i + distance) for i in range(shards) if i + distance in range(shards) and keep(i)
        ]
        return lax.ppermute(block, "shard", route)

    def partner(block):
        return lax.ppermute(block, "shard", [(i, i ^ 1) for i in range(shards)])

    def other_rep(block, flip):
        return lax.ppermute(block, "rep", [(i, i ^ flip) for i in range(reps)])

    def call(kernel, name, shapes, specs, *arrays):
        return pl.pallas_call(
            kernel,
            out_shape=[jax.ShapeDtypeStruct(shape, dtype) for shape, dtype in shapes],
            in_specs=specs[: len(arrays)],
            out_specs=specs[len(arrays) :],
            compiler_params=pltpu.CompilerParams(vmem_limit_bytes=VMEM_LIMIT),
            cost_estimate=pl.CostEstimate(flops=1024, bytes_accessed=1024, transcendentals=0),
            name=name,
        )(*arrays)

    mine, across = pl.pallas_call(
        prepare_kernel,
        out_shape=[jax.ShapeDtypeStruct((quarter + INFO, width), BF16)] * 2,
        in_specs=[pl.BlockSpec(memory_space=pl.ANY), VMEM],
        out_specs=[VMEM] * 2,
        scratch_shapes=[pltpu.VMEM((4, half, width), BF16), pltpu.SemaphoreType.DMA((4,))],
        compiler_params=pltpu.CompilerParams(vmem_limit_bytes=PREPARE_LIMIT),
        name="prepare",
    )(embeddings, labels.reshape(rows // 128, 128))

    odd_only, even_only = (lambda i: i % 2 == 1), (lambda i: i % 2 == 0)
    fence = lax.optimization_barrier

    low_0 = along_shard(mine, 2)
    high = along_shard(mine, -2)
    across = partner(across)

    own, best, own_reach = call(
        own_kernel, "own", [((rows, width), BF16), ((1, rows), F32), ((2,), jnp.int32)],
        [VMEM] * 5 + [SMEM], embeddings, labels[None, :], labels[:, None],
    )

    low_0, own, best = fence((low_0, own, best))
    low_2 = other_rep(low_0, 2)
    low_1 = other_rep(low_0, 1)
    across, high, low_1 = fence((across, high, low_1))
    up_b = along_shard(high[half:], 1, even_only)
    up_a = along_shard(across[:half], -2, odd_only)
    results = [((1, quarter), F32)] * 2
    best, of_across, of_high, reach = call(
        near_kernel, "near", [((1, rows), F32)] + results + [((6,), jnp.int32)],
        [SMEM] + [VMEM] * 9 + [SMEM], own_reach, own, best, low_0, low_1, across, high,
    )
    low_2, up_a, up_b, of_across = fence((low_2, up_a, up_b, of_across))
    low_3 = other_rep(low_2, 1)
    of_across, of_high, of_up, side = call(
        far_kernel, "far", results + [((1, quarter), F32), ((2,), jnp.int32)],
        [SMEM] + [VMEM] * 12 + [SMEM],
        reach, of_across, of_high, low_0, low_1, low_2, across, high, up_a, up_b,
    )
    of_high, of_up = call(
        last_kernel, "last", results, [SMEM] * 2 + [VMEM] * 8,
        reach, side, of_high, of_up, low_3, high, up_a, up_b,
    )

    above = along_shard(of_high, 2)
    beside = along_shard(of_up, 1, odd_only)
    from_partner = partner(of_across)
    (best,) = call(
        merge_kernel, "merge", [((1, rows), F32)], [VMEM] * 5, best, from_partner, above, beside
    )
    return lax.pmax(best[0], "rep")


def solution(mesh):
    placed = (P("shard", None), P("shard"))
    return jax.shard_map(local, mesh=mesh, in_specs=placed, out_specs=P("shard"), check_vma=False)
```

```python
import functools
import math

import jax
import jax.numpy as jnp
from jax import lax
from jax.experimental import pallas as pl
from jax.experimental.pallas import tpu as pltpu
from jax.sharding import PartitionSpec as P

F32 = jnp.float32
BF16 = jnp.bfloat16
TILE = 256
WIDE = 512
INFO = 16
VMEM_LIMIT = 32 * 1024 * 1024
OWN_LIMIT = 46 * 1024 * 1024
PREPARE_LIMIT = 60 * 1024 * 1024
VMEM = pl.BlockSpec(memory_space=pltpu.VMEM)
SMEM = pl.BlockSpec(memory_space=pltpu.SMEM)


def normalize(values):
    as_float = values.astype(F32)
    width = values.shape[1]
    inverse = lax.rsqrt(jnp.sum(as_float * as_float, axis=1, keepdims=True) * (1 / width) + 1e-06)
    return (as_float * (inverse * (1 / math.sqrt(width)))).astype(BF16)


def score(keys, queries):
    return lax.dot_general(keys, queries, (((1,), (1,)), ((), ())), preferred_element_type=F32)


def fold(values):
    rows, cols = values.shape
    return jnp.max(values.reshape(rows // 8, 8, cols), axis=0)


def position():
    rep, odd = lax.axis_index("rep"), lax.axis_index("shard") % 2
    return rep, odd, rep ^ (1 + odd)


def prepare_kernel(emb_ref, labels_ref, lo_out, hi_out, mine_out, across_out, raw, sems):
    rep, odd, _ = position()
    quarter = mine_out.shape[0] - INFO
    part = quarter // 2
    copies = []
    for n in range(4):
        piece = rep if n < 2 else rep ^ (2 - odd)
        at = pl.multiple_of(piece * quarter + (n % 2) * part, part)
        copies.append(pltpu.make_async_copy(emb_ref.at[pl.ds(at, part), :], raw.at[n], sems.at[n]))
        copies[-1].start()
    labels = labels_ref[...]
    first, last = jnp.min(labels), jnp.max(labels)
    head = jnp.sum((labels == first).astype(jnp.int32))
    tail = jnp.sum((labels == last).astype(jnp.int32))
    row = lax.broadcasted_iota(jnp.int32, (INFO, mine_out.shape[1]), 0)
    info = jnp.zeros(row.shape, jnp.int32)
    for n, value in enumerate([first, head // 16, head % 16, last, tail // 16, tail % 16]):
        info = jnp.where(row == n, value, info)
    info = info.astype(F32).astype(BF16)
    for n, copy in enumerate(copies):
        copy.wait()
        out = mine_out if n < 2 else across_out
        for m in range(part // 128):
            rows = pl.ds(m * 128, 128)
            values = normalize(raw[n, rows, :])
            out[pl.ds((n % 2) * part + m * 128, 128), :] = values
            if n < 2:
                (lo_out, hi_out)[n][rows, :] = values
    hi_out[pl.ds(part, INFO), :] = info
    mine_out[pl.ds(quarter, INFO), :] = info
    across_out[pl.ds(quarter, INFO), :] = info


def read_reach(ref, at):
    block = ref[pl.ds(ref.shape[0] - INFO, INFO), pl.ds(0, 128)].astype(F32)
    packed = block[at : at + 1] + 256.0 * (16.0 * block[at + 1 : at + 2] + block[at + 2 : at + 3])
    packed = jnp.max(packed).astype(jnp.int32)
    return packed % 256, packed // 256


def group(keys, queries_ref, query_rows, out_ref, out_at, count):
    step = min(WIDE, query_rows)

    def over_queries(j, _):
        at = pl.multiple_of(j * step, step)
        queries = queries_ref[pl.ds(at, step), :]
        best = None
        for ref, row, rows, first in keys:
            scores = score(ref[pl.ds(row, rows), :], queries)
            index = lax.broadcasted_iota(jnp.int32, scores.shape, 0)
            top = fold(jnp.where(index >= first, scores, -1.0))
            best = top if best is None else jnp.maximum(best, top)
        best = jnp.max(best, axis=0, keepdims=True)
        col = lax.broadcasted_iota(jnp.int32, best.shape, 1) + at
        cols = pl.ds(pl.multiple_of(out_at + at, TILE), step)
        out_ref[:, cols] = jnp.maximum(out_ref[:, cols], jnp.where(col < count, best, -1.0))
        return 0

    lax.fori_loop(0, (count + step - 1) // step, over_queries, 0)


def own_kernel(emb_ref, labels_ref, own_out, best_out, reach_out, start, raw, sems):
    rows = emb_ref.shape[0]
    rep = lax.axis_index("rep")
    parts = raw.shape[0]
    size = rows // parts
    copies = [
        pltpu.make_async_copy(emb_ref.at[pl.ds(n * size, size), :], raw.at[n], sems.at[n])
        for n in range(parts)
    ]
    for copy in copies:
        copy.start()
    labels = jnp.broadcast_to(labels_ref[...], start.shape)
    first = jnp.min(labels)
    reach_out[0] = first
    reach_out[1] = jnp.sum((labels == first).astype(jnp.int32)) // start.shape[0]
    lane = lax.broadcasted_iota(jnp.int32, labels.shape, 1)
    begin = jnp.where((lane == 0) | (labels != pltpu.roll(labels, 1, 1)), lane, 0)
    shift = 1
    while shift < rows:
        begin = jnp.maximum(begin, jnp.where(lane >= shift, pltpu.roll(begin, shift, 1), 0))
        shift *= 2
    start[...] = begin
    best_out[...] = jnp.full(best_out.shape, -1.0, F32)
    for n, copy in enumerate(copies):
        copy.wait()
        for m in range(size // 128):
            values = normalize(raw[n, pl.ds(m * 128, 128), :])
            own_out[pl.ds(n * size + m * 128, 128), :] = values
    for n in range(2):
        tile = rep if n == 0 else rows // TILE - 1 - rep
        at = pl.multiple_of(tile * TILE, TILE)
        keys = own_out[pl.ds(at, TILE), :]

        def over_queries(j, _):
            cols = pl.ds(pl.multiple_of(j * WIDE, WIDE), WIDE)
            scores = score(keys, own_out[cols, :])
            row = lax.broadcasted_iota(jnp.int32, scores.shape, 0) + at
            col = lax.broadcasted_iota(jnp.int32, scores.shape, 1) + j * WIDE
            keep = (row >= start[0:1, cols]) & (row < col)
            best = jnp.max(fold(jnp.where(keep, scores, -1.0)), axis=0, keepdims=True)
            best_out[:, cols] = jnp.maximum(best_out[:, cols], best)
            return 0

        lax.fori_loop(at // WIDE, rows // WIDE, over_queries, 0)


def reached(query, key, offset, limit):
    count = jnp.clip(query[1] - offset, 0, limit)
    return jnp.where(query[0] == key[0], count, 0)


def lower_keys(rep, tail, rows, pieces):
    half = rows // 8
    return [
        (ref, 0, half, jnp.clip(rows - tail - (rep ^ flip) * 2 * half - part * half, 0, half))
        for ref, flip, part in pieces
    ]


def near_kernel(own_reach, own_ref, best_ref, low_0a, low_0b, low_1a, low_2a, across, high,
                best_out, across_out, high_out, reach_out):
    rows = own_ref.shape[0]
    quarter = across.shape[0] - INFO
    rep, odd, part = position()
    mine = (own_reach[0], own_reach[1])
    low, beside_head = read_reach(low_0b, 3), read_reach(across, 0)
    beside_tail, up = read_reach(across, 3), read_reach(high, 0)
    for n, value in enumerate(low + beside_head + up):
        reach_out[n] = value
    best_out[...] = best_ref[...]
    across_out[...] = jnp.full(across_out.shape, -1.0, F32)
    high_out[...] = jnp.full(high_out.shape, -1.0, F32)

    lows = lower_keys(
        rep, low[1], rows, [(low_0a, 0, 0), (low_0b, 0, 1), (low_1a, 1, 0), (low_2a, 2, 0)]
    )
    besides = [
        (across, 0, quarter, jnp.clip(rows - beside_tail[1] - part * quarter, 0, quarter))
    ]
    group(lows[:2], own_ref, rows, best_out, 0, reached(mine, low, 0, rows))
    count = jnp.where(odd == 1, reached(mine, beside_tail, 0, rows), 0)
    group(besides, own_ref, rows, best_out, 0, count)
    group(lows, across, quarter, across_out, 0, reached(beside_head, low, part * quarter, quarter))
    group(besides, high, quarter, high_out, 0, reached(up, beside_tail, rep * quarter, quarter))
    group(lows, high, quarter, high_out, 0, reached(up, low, rep * quarter, quarter))


def far_kernel(reach_ref, across_ref, high_ref, low_0a, low_0b, low_1a, low_1b, low_2a,
               low_2b, low_3a, across, high, up_a, up_b, across_out, high_out, up_out, side_out):
    quarter = across.shape[0] - INFO
    half = quarter // 2
    rep, _, part = position()
    low, beside, up = [(reach_ref[2 * n], reach_ref[2 * n + 1]) for n in range(3)]
    side = read_reach(up_b, 0)
    side_out[0], side_out[1] = side
    across_out[...] = across_ref[...]
    high_out[...] = high_ref[...]
    up_out[...] = jnp.full(up_out.shape, -1.0, F32)

    lows = lower_keys(
        rep, low[1], 4 * quarter,
        [(low_1b, 1, 1), (low_2b, 2, 1), (low_3a, 3, 0), (low_0a, 0, 0), (low_0b, 0, 1), (low_1a, 1, 0), (low_2a, 2, 0)],
    )
    group(lows[:2], across, quarter, across_out, 0, reached(beside, low, part * quarter, quarter))
    group(lows[:3], high, quarter, high_out, 0, reached(up, low, rep * quarter, quarter))
    group(lows, up_a, half, up_out, 0, reached(side, low, (rep ^ 2) * quarter, half))
    group(lows, up_b, half, up_out, half, reached(side, low, rep * quarter + half, half))


def last_kernel(reach_ref, side_ref, high_ref, up_ref, low_3b, high, up_a, up_b,
                high_out, up_out):
    half = up_a.shape[0]
    quarter = 2 * half
    rep = lax.axis_index("rep")
    low, up = (reach_ref[0], reach_ref[1]), (reach_ref[4], reach_ref[5])
    side = (side_ref[0], side_ref[1])
    high_out[...], up_out[...] = high_ref[...], up_ref[...]
    lows = lower_keys(rep, low[1], 4 * quarter, [(low_3b, 3, 1)])
    group(lows, high, quarter, high_out, 0, reached(up, low, rep * quarter, quarter))
    group(lows, up_a, half, up_out, 0, reached(side, low, (rep ^ 2) * quarter, half))
    group(lows, up_b, half, up_out, half, reached(side, low, rep * quarter + half, half))


def merge_kernel(best_ref, partner_ref, above_ref, beside_ref, out_ref):
    quarter = above_ref.shape[1]
    half = quarter // 2
    rep, odd, _ = position()
    inside = lax.axis_index("shard") >= 2
    out_ref[...] = best_ref[...]

    def raised(at, values):
        cols = pl.ds(pl.multiple_of(at, half), values.shape[1])
        out_ref[:, cols] = jnp.maximum(out_ref[:, cols], values)

    raised((rep ^ (2 - odd)) * quarter, partner_ref[...])
    raised(rep * quarter, jnp.where(inside, above_ref[...], -1.0))
    beside = jnp.where(inside & (odd == 0), beside_ref[...], -1.0)
    raised((rep ^ 2) * quarter, beside[:, :half])
    raised(rep * quarter + half, beside[:, half:])


def local(embeddings, labels):
    rows, width = embeddings.shape
    shards, reps = lax.axis_size("shard"), lax.axis_size("rep")
    quarter = rows // reps
    half = quarter // 2

    def along_shard(block, distance, keep=lambda i: True):
        route = [
            (i, i + distance) for i in range(shards) if i + distance in range(shards) and keep(i)
        ]
        return lax.ppermute(block, "shard", route)

    def partner(block):
        return lax.ppermute(block, "shard", [(i, i ^ 1) for i in range(shards)])

    def other_rep(block, flip):
        return lax.ppermute(block, "rep", [(i, i ^ flip) for i in range(reps)])

    def call(kernel, name, shapes, specs, *arrays):
        return pl.pallas_call(
            kernel,
            out_shape=[jax.ShapeDtypeStruct(shape, dtype) for shape, dtype in shapes],
            in_specs=specs[: len(arrays)],
            out_specs=specs[len(arrays) :],
            compiler_params=pltpu.CompilerParams(vmem_limit_bytes=VMEM_LIMIT),
            cost_estimate=pl.CostEstimate(flops=1024, bytes_accessed=1024, transcendentals=0),
            name=name,
        )(*arrays)

    sizes = [half, half + INFO, quarter + INFO, quarter + INFO]
    lo, hi, mine, across = pl.pallas_call(
        prepare_kernel,
        out_shape=[jax.ShapeDtypeStruct((size, width), BF16) for size in sizes],
        in_specs=[pl.BlockSpec(memory_space=pltpu.HBM), VMEM],
        out_specs=[VMEM] * 4,
        scratch_shapes=[pltpu.VMEM((4, half, width), BF16), pltpu.SemaphoreType.DMA((4,))],
        compiler_params=pltpu.CompilerParams(vmem_limit_bytes=PREPARE_LIMIT),
        name="prepare",
    )(embeddings, labels.reshape(rows // 128, 128))

    odd_only, even_only = (lambda i: i % 2 == 1), (lambda i: i % 2 == 0)
    fence = lax.optimization_barrier

    low_0a = along_shard(lo, 2)
    high = along_shard(mine, -2)
    across = partner(across)
    low_0b = along_shard(hi, 2)

    low_0a, own_labels = fence((low_0a, labels))
    low_2a = other_rep(low_0a, 2)
    low_1a = other_rep(low_0a, 1)
    own, best, own_reach = pl.pallas_call(
        own_kernel,
        out_shape=[
            jax.ShapeDtypeStruct((rows, width), BF16),
            jax.ShapeDtypeStruct((1, rows), F32),
            jax.ShapeDtypeStruct((2,), jnp.int32),
        ],
        in_specs=[pl.BlockSpec(memory_space=pltpu.HBM), VMEM],
        out_specs=[VMEM, VMEM, SMEM],
        scratch_shapes=[
            pltpu.VMEM((8, rows), jnp.int32),
            pltpu.VMEM((4, quarter, width), BF16),
            pltpu.SemaphoreType.DMA((4,)),
        ],
        compiler_params=pltpu.CompilerParams(vmem_limit_bytes=OWN_LIMIT),
        cost_estimate=pl.CostEstimate(flops=1024, bytes_accessed=1024, transcendentals=0),
        name="own",
    )(embeddings, own_labels[None, :])

    across, high, low_0b, low_1a, low_2a, own, best = fence(
        (across, high, low_0b, low_1a, low_2a, own, best)
    )
    low_2b = other_rep(low_0b, 2)
    up_b = along_shard(high[half:], 1, even_only)
    up_a = along_shard(across[:half], -2, odd_only)
    low_1b = other_rep(low_0b, 1)
    low_3a = other_rep(low_2a, 1)
    results = [((1, quarter), F32)] * 2
    best, of_across, of_high, reach = call(
        near_kernel, "near", [((1, rows), F32)] + results + [((6,), jnp.int32)],
        [SMEM] + [VMEM] * 11 + [SMEM],
        own_reach, own, best, low_0a, low_0b, low_1a, low_2a, across, high,
    )
    low_2b, up_a, up_b, low_1b, low_3a, of_across = fence(
        (low_2b, up_a, up_b, low_1b, low_3a, of_across)
    )
    low_3b = other_rep(low_2b, 1)
    of_across, of_high, of_up, side = call(
        far_kernel, "far", results + [((1, quarter), F32), ((2,), jnp.int32)],
        [SMEM] + [VMEM] * 16 + [SMEM],
        reach, of_across, of_high, low_0a, low_0b, low_1a, low_1b, low_2a, low_2b,
        low_3a, across, high, up_a, up_b,
    )
    of_high, of_up = call(
        last_kernel, "last", results, [SMEM] * 2 + [VMEM] * 8,
        reach, side, of_high, of_up, low_3b, high, up_a, up_b,
    )

    above = along_shard(of_high, 2)
    beside = along_shard(of_up, 1, odd_only)
    from_partner = partner(of_across)
    (best,) = call(
        merge_kernel, "merge", [((1, rows), F32)], [VMEM] * 5, best, from_partner, above, beside
    )
    return lax.pmax(best[0], "rep")


def solution(mesh):
    placed = (P("shard", None), P("shard"))
    return jax.shard_map(local, mesh=mesh, in_specs=placed, out_specs=P("shard"), check_vma=False)
```

```python
import functools
import math

import jax
import jax.numpy as jnp
from jax import lax
from jax.experimental import pallas as pl
from jax.experimental.pallas import tpu as pltpu
from jax.sharding import PartitionSpec as P

F32 = jnp.float32
BF16 = jnp.bfloat16
TILE = 256
WIDE = 512
INFO = 16
VMEM_LIMIT = 32 * 1024 * 1024
OWN_LIMIT = 46 * 1024 * 1024
PREPARE_LIMIT = 50 * 1024 * 1024
VMEM = pl.BlockSpec(memory_space=pltpu.VMEM)
SMEM = pl.BlockSpec(memory_space=pltpu.SMEM)


def normalize(values):
    as_float = values.astype(F32)
    width = values.shape[1]
    inverse = lax.rsqrt(jnp.sum(as_float * as_float, axis=1, keepdims=True) * (1 / width) + 1e-06)
    return (as_float * (inverse * (1 / math.sqrt(width)))).astype(BF16)


def score(keys, queries):
    return lax.dot_general(keys, queries, (((1,), (1,)), ((), ())), preferred_element_type=F32)


def fold(values):
    rows, cols = values.shape
    return jnp.max(values.reshape(rows // 8, 8, cols), axis=0)


def position():
    rep, odd = lax.axis_index("rep"), lax.axis_index("shard") % 2
    return rep, odd, rep ^ (1 + odd)


def prepare_kernel(emb_ref, labels_hbm, lo_out, hi_out, mine_out, across_out, raw, labels_ref, sems):
    rep, odd, _ = position()
    quarter = mine_out.shape[0] - INFO
    part = quarter // 2
    copies = []
    for n in range(4):
        piece = rep if n < 2 else rep ^ (2 - odd)
        at = pl.multiple_of(piece * quarter + (n % 2) * part, part)
        copies.append(pltpu.make_async_copy(emb_ref.at[pl.ds(at, part), :], raw.at[n], sems.at[n]))
        copies[-1].start()
    fetch = pltpu.make_async_copy(labels_hbm, labels_ref, sems.at[4])
    fetch.start()
    fetch.wait()
    labels = labels_ref[...]
    first, last = jnp.min(labels), jnp.max(labels)
    head = jnp.sum((labels == first).astype(jnp.int32))
    tail = jnp.sum((labels == last).astype(jnp.int32))
    row = lax.broadcasted_iota(jnp.int32, (INFO, mine_out.shape[1]), 0)
    info = jnp.zeros(row.shape, jnp.int32)
    for n, value in enumerate([first, head // 16, head % 16, last, tail // 16, tail % 16]):
        info = jnp.where(row == n, value, info)
    info = info.astype(F32).astype(BF16)
    for n, copy in enumerate(copies):
        copy.wait()
        out = mine_out if n < 2 else across_out
        for m in range(part // 128):
            rows = pl.ds(m * 128, 128)
            values = normalize(raw[n, rows, :])
            out[pl.ds((n % 2) * part + m * 128, 128), :] = values
            if n < 2:
                (lo_out, hi_out)[n][rows, :] = values
    hi_out[pl.ds(part, INFO), :] = info
    mine_out[pl.ds(quarter, INFO), :] = info
    across_out[pl.ds(quarter, INFO), :] = info


def read_reach(ref, at):
    block = ref[pl.ds(ref.shape[0] - INFO, INFO), pl.ds(0, 128)].astype(F32)
    packed = block[at : at + 1] + 256.0 * (16.0 * block[at + 1 : at + 2] + block[at + 2 : at + 3])
    packed = jnp.max(packed).astype(jnp.int32)
    return packed % 256, packed // 256


def group(keys, queries_ref, query_rows, out_ref, out_at, count):
    step = min(WIDE, query_rows)

    def over_queries(j, _):
        at = pl.multiple_of(j * step, step)
        queries = queries_ref[pl.ds(at, step), :]
        best = None
        for ref, row, rows, first in keys:
            scores = score(ref[pl.ds(row, rows), :], queries)
            index = lax.broadcasted_iota(jnp.int32, scores.shape, 0)
            top = fold(jnp.where(index >= first, scores, -1.0))
            best = top if best is None else jnp.maximum(best, top)
        best = jnp.max(best, axis=0, keepdims=True)
        col = lax.broadcasted_iota(jnp.int32, best.shape, 1) + at
        cols = pl.ds(pl.multiple_of(out_at + at, TILE), step)
        out_ref[:, cols] = jnp.maximum(out_ref[:, cols], jnp.where(col < count, best, -1.0))
        return 0

    lax.fori_loop(0, (count + step - 1) // step, over_queries, 0)


def own_kernel(emb_ref, labels_ref, own_out, best_out, reach_out, start, raw, sems):
    rows = emb_ref.shape[0]
    rep = lax.axis_index("rep")
    parts = raw.shape[0]
    size = rows // parts
    copies = [
        pltpu.make_async_copy(emb_ref.at[pl.ds(n * size, size), :], raw.at[n], sems.at[n])
        for n in range(parts)
    ]
    for copy in copies:
        copy.start()
    labels = jnp.broadcast_to(labels_ref[...], start.shape)
    first = jnp.min(labels)
    reach_out[0] = first
    reach_out[1] = jnp.sum((labels == first).astype(jnp.int32)) // start.shape[0]
    lane = lax.broadcasted_iota(jnp.int32, labels.shape, 1)
    begin = jnp.where((lane == 0) | (labels != pltpu.roll(labels, 1, 1)), lane, 0)
    shift = 1
    while shift < rows:
        begin = jnp.maximum(begin, jnp.where(lane >= shift, pltpu.roll(begin, shift, 1), 0))
        shift *= 2
    start[...] = begin
    best_out[...] = jnp.full(best_out.shape, -1.0, F32)
    for n, copy in enumerate(copies):
        copy.wait()
        for m in range(size // 128):
            values = normalize(raw[n, pl.ds(m * 128, 128), :])
            own_out[pl.ds(n * size + m * 128, 128), :] = values
    for n in range(2):
        tile = rep if n == 0 else rows // TILE - 1 - rep
        at = pl.multiple_of(tile * TILE, TILE)
        keys = own_out[pl.ds(at, TILE), :]

        def over_queries(j, _):
            cols = pl.ds(pl.multiple_of(j * WIDE, WIDE), WIDE)
            scores = score(keys, own_out[cols, :])
            row = lax.broadcasted_iota(jnp.int32, scores.shape, 0) + at
            col = lax.broadcasted_iota(jnp.int32, scores.shape, 1) + j * WIDE
            keep = (row >= start[0:1, cols]) & (row < col)
            best = jnp.max(fold(jnp.where(keep, scores, -1.0)), axis=0, keepdims=True)
            best_out[:, cols] = jnp.maximum(best_out[:, cols], best)
            return 0

        lax.fori_loop(at // WIDE, rows // WIDE, over_queries, 0)


def reached(query, key, offset, limit):
    count = jnp.clip(query[1] - offset, 0, limit)
    return jnp.where(query[0] == key[0], count, 0)


def lower_keys(rep, tail, rows, pieces):
    half = rows // 8
    return [
        (ref, 0, half, jnp.clip(rows - tail - (rep ^ flip) * 2 * half - part * half, 0, half))
        for ref, flip, part in pieces
    ]


def near_kernel(own_reach, own_ref, best_ref, low_0a, low_0b, low_1a, low_2a, across, high,
                best_out, across_out, high_out, reach_out):
    rows = own_ref.shape[0]
    quarter = across.shape[0] - INFO
    rep, odd, part = position()
    mine = (own_reach[0], own_reach[1])
    low, beside_head = read_reach(low_0b, 3), read_reach(across, 0)
    beside_tail, up = read_reach(across, 3), read_reach(high, 0)
    for n, value in enumerate(low + beside_head + up):
        reach_out[n] = value
    best_out[...] = best_ref[...]
    across_out[...] = jnp.full(across_out.shape, -1.0, F32)
    high_out[...] = jnp.full(high_out.shape, -1.0, F32)

    lows = lower_keys(
        rep, low[1], rows, [(low_0a, 0, 0), (low_0b, 0, 1), (low_1a, 1, 0), (low_2a, 2, 0)]
    )
    besides = [
        (across, 0, quarter, jnp.clip(rows - beside_tail[1] - part * quarter, 0, quarter))
    ]
    group(lows[:2], own_ref, rows, best_out, 0, reached(mine, low, 0, rows))
    count = jnp.where(odd == 1, reached(mine, beside_tail, 0, rows), 0)
    group(besides, own_ref, rows, best_out, 0, count)
    group(lows, across, quarter, across_out, 0, reached(beside_head, low, part * quarter, quarter))
    group(besides, high, quarter, high_out, 0, reached(up, beside_tail, rep * quarter, quarter))
    group(lows, high, quarter, high_out, 0, reached(up, low, rep * quarter, quarter))


def far_kernel(reach_ref, across_ref, high_ref, low_0a, low_0b, low_1a, low_1b, low_2a,
               low_2b, low_3a, across, high, up_a, up_b, across_out, high_out, up_out, side_out):
    quarter = across.shape[0] - INFO
    half = quarter // 2
    rep, _, part = position()
    low, beside, up = [(reach_ref[2 * n], reach_ref[2 * n + 1]) for n in range(3)]
    side = read_reach(up_b, 0)
    side_out[0], side_out[1] = side
    across_out[...] = across_ref[...]
    high_out[...] = high_ref[...]
    up_out[...] = jnp.full(up_out.shape, -1.0, F32)

    lows = lower_keys(
        rep, low[1], 4 * quarter,
        [(low_1b, 1, 1), (low_2b, 2, 1), (low_3a, 3, 0), (low_0a, 0, 0), (low_0b, 0, 1), (low_1a, 1, 0), (low_2a, 2, 0)],
    )
    group(lows[:2], across, quarter, across_out, 0, reached(beside, low, part * quarter, quarter))
    group(lows[:3], high, quarter, high_out, 0, reached(up, low, rep * quarter, quarter))
    group(lows, up_a, half, up_out, 0, reached(side, low, (rep ^ 2) * quarter, half))
    group(lows, up_b, half, up_out, half, reached(side, low, rep * quarter + half, half))


def last_kernel(reach_ref, side_ref, high_ref, up_ref, low_3b, high, up_a, up_b,
                high_out, up_out):
    half = up_a.shape[0]
    quarter = 2 * half
    rep = lax.axis_index("rep")
    low, up = (reach_ref[0], reach_ref[1]), (reach_ref[4], reach_ref[5])
    side = (side_ref[0], side_ref[1])
    high_out[...], up_out[...] = high_ref[...], up_ref[...]
    lows = lower_keys(rep, low[1], 4 * quarter, [(low_3b, 3, 1)])
    group(lows, high, quarter, high_out, 0, reached(up, low, rep * quarter, quarter))
    group(lows, up_a, half, up_out, 0, reached(side, low, (rep ^ 2) * quarter, half))
    group(lows, up_b, half, up_out, half, reached(side, low, rep * quarter + half, half))


def merge_kernel(best_ref, partner_ref, above_ref, beside_ref, out_ref):
    quarter = above_ref.shape[1]
    half = quarter // 2
    rep, odd, _ = position()
    inside = lax.axis_index("shard") >= 2
    out_ref[...] = best_ref[...]

    def raised(at, values):
        cols = pl.ds(pl.multiple_of(at, half), values.shape[1])
        out_ref[:, cols] = jnp.maximum(out_ref[:, cols], values)

    raised((rep ^ (2 - odd)) * quarter, partner_ref[...])
    raised(rep * quarter, jnp.where(inside, above_ref[...], -1.0))
    beside = jnp.where(inside & (odd == 0), beside_ref[...], -1.0)
    raised((rep ^ 2) * quarter, beside[:, :half])
    raised(rep * quarter + half, beside[:, half:])


def local(embeddings, labels):
    rows, width = embeddings.shape
    shards, reps = lax.axis_size("shard"), lax.axis_size("rep")
    quarter = rows // reps
    half = quarter // 2

    def along_shard(block, distance, keep=lambda i: True):
        route = [
            (i, i + distance) for i in range(shards) if i + distance in range(shards) and keep(i)
        ]
        return lax.ppermute(block, "shard", route)

    def partner(block):
        return lax.ppermute(block, "shard", [(i, i ^ 1) for i in range(shards)])

    def other_rep(block, flip):
        return lax.ppermute(block, "rep", [(i, i ^ flip) for i in range(reps)])

    def call(kernel, name, shapes, specs, *arrays):
        return pl.pallas_call(
            kernel,
            out_shape=[jax.ShapeDtypeStruct(shape, dtype) for shape, dtype in shapes],
            in_specs=specs[: len(arrays)],
            out_specs=specs[len(arrays) :],
            compiler_params=pltpu.CompilerParams(vmem_limit_bytes=VMEM_LIMIT),
            cost_estimate=pl.CostEstimate(flops=1024, bytes_accessed=1024, transcendentals=0),
            name=name,
        )(*arrays)

    sizes = [half, half + INFO, quarter + INFO, quarter + INFO]
    lo, hi, mine, across = pl.pallas_call(
        prepare_kernel,
        out_shape=[jax.ShapeDtypeStruct((size, width), BF16) for size in sizes],
        in_specs=[pl.BlockSpec(memory_space=pltpu.HBM)] * 2,
        out_specs=[VMEM] * 4,
        scratch_shapes=[
            pltpu.VMEM((4, half, width), BF16),
            pltpu.VMEM((rows // 128, 128), jnp.int32),
            pltpu.SemaphoreType.DMA((5,)),
        ],
        compiler_params=pltpu.CompilerParams(vmem_limit_bytes=PREPARE_LIMIT),
        name="prepare",
    )(embeddings, labels.reshape(rows // 128, 128))

    odd_only, even_only = (lambda i: i % 2 == 1), (lambda i: i % 2 == 0)
    fence = lax.optimization_barrier

    low_0a = along_shard(lo, 2)
    high = along_shard(mine, -2)
    across = partner(across)
    low_0b = along_shard(hi, 2)

    low_0a, own_labels = fence((low_0a, labels))
    low_2a = other_rep(low_0a, 2)
    low_1a = other_rep(low_0a, 1)
    own, best, own_reach = pl.pallas_call(
        own_kernel,
        out_shape=[
            jax.ShapeDtypeStruct((rows, width), BF16),
            jax.ShapeDtypeStruct((1, rows), F32),
            jax.ShapeDtypeStruct((2,), jnp.int32),
        ],
        in_specs=[pl.BlockSpec(memory_space=pltpu.HBM), VMEM],
        out_specs=[VMEM, VMEM, SMEM],
        scratch_shapes=[
            pltpu.VMEM((8, rows), jnp.int32),
            pltpu.VMEM((4, quarter, width), BF16),
            pltpu.SemaphoreType.DMA((4,)),
        ],
        compiler_params=pltpu.CompilerParams(vmem_limit_bytes=OWN_LIMIT),
        cost_estimate=pl.CostEstimate(flops=1024, bytes_accessed=1024, transcendentals=0),
        name="own",
    )(embeddings, own_labels[None, :])

    across, high, own, best = fence((across, high, own, best))
    up_a = along_shard(across[:half], -2, odd_only)
    up_b = along_shard(high[half:], 1, even_only)
    low_0b, low_1a, low_2a, across, high = fence((low_0b, low_1a, low_2a, across, high))
    low_2b = other_rep(low_0b, 2)
    low_1b = other_rep(low_0b, 1)
    low_3a = other_rep(low_2a, 1)
    results = [((1, quarter), F32)] * 2
    best, of_across, of_high, reach = call(
        near_kernel, "near", [((1, rows), F32)] + results + [((6,), jnp.int32)],
        [SMEM] + [VMEM] * 11 + [SMEM],
        own_reach, own, best, low_0a, low_0b, low_1a, low_2a, across, high,
    )
    low_2b, up_a, up_b, low_1b, low_3a, of_across = fence(
        (low_2b, up_a, up_b, low_1b, low_3a, of_across)
    )
    low_3b = other_rep(low_2b, 1)
    of_across, of_high, of_up, side = call(
        far_kernel, "far", results + [((1, quarter), F32), ((2,), jnp.int32)],
        [SMEM] + [VMEM] * 16 + [SMEM],
        reach, of_across, of_high, low_0a, low_0b, low_1a, low_1b, low_2a, low_2b,
        low_3a, across, high, up_a, up_b,
    )
    of_high, of_up = call(
        last_kernel, "last", results, [SMEM] * 2 + [VMEM] * 8,
        reach, side, of_high, of_up, low_3b, high, up_a, up_b,
    )

    above = along_shard(of_high, 2)
    beside = along_shard(of_up, 1, odd_only)
    from_partner = partner(of_across)
    (best,) = call(
        merge_kernel, "merge", [((1, rows), F32)], [VMEM] * 5, best, from_partner, above, beside
    )
    return lax.pmax(best[0], "rep")


def solution(mesh):
    placed = (P("shard", None), P("shard"))
    return jax.shard_map(local, mesh=mesh, in_specs=placed, out_specs=P("shard"), check_vma=False)
```

```python
import functools
import math

import jax
import jax.numpy as jnp
from jax import lax
from jax.experimental import pallas as pl
from jax.experimental.pallas import tpu as pltpu
from jax.sharding import PartitionSpec as P

F32 = jnp.float32
BF16 = jnp.bfloat16
TILE = 256
WIDE = 512
INFO = 16
VMEM_LIMIT = 32 * 1024 * 1024
OWN_LIMIT = 46 * 1024 * 1024
PREPARE_LIMIT = 50 * 1024 * 1024
VMEM = pl.BlockSpec(memory_space=pltpu.VMEM)
SMEM = pl.BlockSpec(memory_space=pltpu.SMEM)


def normalize(values):
    as_float = values.astype(F32)
    width = values.shape[1]
    inverse = lax.rsqrt(jnp.sum(as_float * as_float, axis=1, keepdims=True) * (1 / width) + 1e-06)
    return (as_float * (inverse * (1 / math.sqrt(width)))).astype(BF16)


def score(keys, queries):
    return lax.dot_general(keys, queries, (((1,), (1,)), ((), ())), preferred_element_type=F32)


def fold(values):
    rows, cols = values.shape
    return jnp.max(values.reshape(rows // 8, 8, cols), axis=0)


def position():
    rep, odd = lax.axis_index("rep"), lax.axis_index("shard") % 2
    return rep, odd, rep ^ (1 + odd)


def prepare_kernel(emb_ref, labels_hbm, lo_out, hi_out, mine_out, across_out, raw, labels_ref, sems):
    rep, odd, _ = position()
    quarter = mine_out.shape[0] - INFO
    part = quarter // 2
    copies = []
    for n in range(4):
        piece = rep if n < 2 else rep ^ (2 - odd)
        at = pl.multiple_of(piece * quarter + (n % 2) * part, part)
        copies.append(pltpu.make_async_copy(emb_ref.at[pl.ds(at, part), :], raw.at[n], sems.at[n]))
        copies[-1].start()
    fetch = pltpu.make_async_copy(labels_hbm, labels_ref, sems.at[4])
    fetch.start()
    fetch.wait()
    labels = labels_ref[...]
    first, last = jnp.min(labels), jnp.max(labels)
    head = jnp.sum((labels == first).astype(jnp.int32))
    tail = jnp.sum((labels == last).astype(jnp.int32))
    row = lax.broadcasted_iota(jnp.int32, (INFO, mine_out.shape[1]), 0)
    info = jnp.zeros(row.shape, jnp.int32)
    for n, value in enumerate([first, head // 16, head % 16, last, tail // 16, tail % 16]):
        info = jnp.where(row == n, value, info)
    info = info.astype(F32).astype(BF16)
    for n, copy in enumerate(copies):
        copy.wait()
        out = mine_out if n < 2 else across_out
        for m in range(part // 128):
            rows = pl.ds(m * 128, 128)
            values = normalize(raw[n, rows, :])
            out[pl.ds((n % 2) * part + m * 128, 128), :] = values
            if n < 2:
                (lo_out, hi_out)[n][rows, :] = values
    hi_out[pl.ds(part, INFO), :] = info
    mine_out[pl.ds(quarter, INFO), :] = info
    across_out[pl.ds(quarter, INFO), :] = info


def read_reach(ref, at):
    block = ref[pl.ds(ref.shape[0] - INFO, INFO), pl.ds(0, 128)].astype(F32)
    packed = block[at : at + 1] + 256.0 * (16.0 * block[at + 1 : at + 2] + block[at + 2 : at + 3])
    packed = jnp.max(packed).astype(jnp.int32)
    return packed % 256, packed // 256


def group(keys, queries_ref, query_rows, out_ref, out_at, count):
    step = min(2 * WIDE, query_rows)

    def over_queries(j, _):
        at = pl.multiple_of(j * step, step)
        queries = queries_ref[pl.ds(at, step), :]
        best = None
        for ref, row, rows, first in keys:
            scores = score(queries, ref[pl.ds(row, rows), :])
            for n in range(0, rows, 128):
                part = scores[:, n : n + 128]
                lane = lax.broadcasted_iota(jnp.int32, part.shape, 1) + n
                part = jnp.where(lane >= first, part, -1.0)
                best = part if best is None else jnp.maximum(best, part)
        best = jnp.max(jnp.transpose(best), axis=0, keepdims=True)
        col = lax.broadcasted_iota(jnp.int32, best.shape, 1) + at
        cols = pl.ds(pl.multiple_of(out_at + at, TILE), step)
        out_ref[:, cols] = jnp.maximum(out_ref[:, cols], jnp.where(col < count, best, -1.0))
        return 0

    lax.fori_loop(0, (count + step - 1) // step, over_queries, 0)


def own_kernel(emb_ref, labels_ref, own_out, best_out, reach_out, start, raw, sems):
    rows = emb_ref.shape[0]
    rep = lax.axis_index("rep")
    parts = raw.shape[0]
    size = rows // parts
    copies = [
        pltpu.make_async_copy(emb_ref.at[pl.ds(n * size, size), :], raw.at[n], sems.at[n])
        for n in range(parts)
    ]
    for copy in copies:
        copy.start()
    labels = jnp.broadcast_to(labels_ref[...], start.shape)
    first = jnp.min(labels)
    reach_out[0] = first
    reach_out[1] = jnp.sum((labels == first).astype(jnp.int32)) // start.shape[0]
    lane = lax.broadcasted_iota(jnp.int32, labels.shape, 1)
    begin = jnp.where((lane == 0) | (labels != pltpu.roll(labels, 1, 1)), lane, 0)
    shift = 1
    while shift < rows:
        begin = jnp.maximum(begin, jnp.where(lane >= shift, pltpu.roll(begin, shift, 1), 0))
        shift *= 2
    start[...] = begin
    best_out[...] = jnp.full(best_out.shape, -1.0, F32)
    for n, copy in enumerate(copies):
        copy.wait()
        for m in range(size // 128):
            values = normalize(raw[n, pl.ds(m * 128, 128), :])
            own_out[pl.ds(n * size + m * 128, 128), :] = values
    for n in range(2):
        tile = rep if n == 0 else rows // TILE - 1 - rep
        at = pl.multiple_of(tile * TILE, TILE)
        keys = own_out[pl.ds(at, TILE), :]

        def over_queries(j, _):
            cols = pl.ds(pl.multiple_of(j * WIDE, WIDE), WIDE)
            scores = score(keys, own_out[cols, :])
            row = lax.broadcasted_iota(jnp.int32, scores.shape, 0) + at
            col = lax.broadcasted_iota(jnp.int32, scores.shape, 1) + j * WIDE
            keep = (row >= start[0:1, cols]) & (row < col)
            best = jnp.max(fold(jnp.where(keep, scores, -1.0)), axis=0, keepdims=True)
            best_out[:, cols] = jnp.maximum(best_out[:, cols], best)
            return 0

        lax.fori_loop(at // WIDE, rows // WIDE, over_queries, 0)


def reached(query, key, offset, limit):
    count = jnp.clip(query[1] - offset, 0, limit)
    return jnp.where(query[0] == key[0], count, 0)


def lower_keys(rep, tail, rows, pieces):
    half = rows // 8
    return [
        (ref, 0, half, jnp.clip(rows - tail - (rep ^ flip) * 2 * half - part * half, 0, half))
        for ref, flip, part in pieces
    ]


def near_kernel(own_reach, own_ref, best_ref, low_0a, low_0b, low_1a, low_2a, across, high,
                best_out, across_out, high_out, reach_out):
    rows = own_ref.shape[0]
    quarter = across.shape[0] - INFO
    rep, odd, part = position()
    mine = (own_reach[0], own_reach[1])
    low, beside_head = read_reach(low_0b, 3), read_reach(across, 0)
    beside_tail, up = read_reach(across, 3), read_reach(high, 0)
    for n, value in enumerate(low + beside_head + up):
        reach_out[n] = value
    best_out[...] = best_ref[...]
    across_out[...] = jnp.full(across_out.shape, -1.0, F32)
    high_out[...] = jnp.full(high_out.shape, -1.0, F32)

    lows = lower_keys(
        rep, low[1], rows, [(low_0a, 0, 0), (low_0b, 0, 1), (low_1a, 1, 0), (low_2a, 2, 0)]
    )
    besides = [
        (across, 0, quarter, jnp.clip(rows - beside_tail[1] - part * quarter, 0, quarter))
    ]
    group(lows[:2], own_ref, rows, best_out, 0, reached(mine, low, 0, rows))
    count = jnp.where(odd == 1, reached(mine, beside_tail, 0, rows), 0)
    group(besides, own_ref, rows, best_out, 0, count)
    group(lows, across, quarter, across_out, 0, reached(beside_head, low, part * quarter, quarter))
    group(besides, high, quarter, high_out, 0, reached(up, beside_tail, rep * quarter, quarter))
    group(lows, high, quarter, high_out, 0, reached(up, low, rep * quarter, quarter))


def far_kernel(reach_ref, across_ref, high_ref, low_0a, low_0b, low_1a, low_1b, low_2a,
               low_2b, low_3a, across, high, up_a, up_b, across_out, high_out, up_out, side_out):
    quarter = across.shape[0] - INFO
    half = quarter // 2
    rep, _, part = position()
    low, beside, up = [(reach_ref[2 * n], reach_ref[2 * n + 1]) for n in range(3)]
    side = read_reach(up_b, 0)
    side_out[0], side_out[1] = side
    across_out[...] = across_ref[...]
    high_out[...] = high_ref[...]
    up_out[...] = jnp.full(up_out.shape, -1.0, F32)

    lows = lower_keys(
        rep, low[1], 4 * quarter,
        [(low_1b, 1, 1), (low_2b, 2, 1), (low_3a, 3, 0), (low_0a, 0, 0), (low_0b, 0, 1), (low_1a, 1, 0), (low_2a, 2, 0)],
    )
    group(lows[:2], across, quarter, across_out, 0, reached(beside, low, part * quarter, quarter))
    group(lows[:3], high, quarter, high_out, 0, reached(up, low, rep * quarter, quarter))
    group(lows, up_a, half, up_out, 0, reached(side, low, (rep ^ 2) * quarter, half))
    group(lows, up_b, half, up_out, half, reached(side, low, rep * quarter + half, half))


def last_kernel(reach_ref, side_ref, high_ref, up_ref, low_3b, high, up_a, up_b,
                high_out, up_out):
    half = up_a.shape[0]
    quarter = 2 * half
    rep = lax.axis_index("rep")
    low, up = (reach_ref[0], reach_ref[1]), (reach_ref[4], reach_ref[5])
    side = (side_ref[0], side_ref[1])
    high_out[...], up_out[...] = high_ref[...], up_ref[...]
    lows = lower_keys(rep, low[1], 4 * quarter, [(low_3b, 3, 1)])
    group(lows, high, quarter, high_out, 0, reached(up, low, rep * quarter, quarter))
    group(lows, up_a, half, up_out, 0, reached(side, low, (rep ^ 2) * quarter, half))
    group(lows, up_b, half, up_out, half, reached(side, low, rep * quarter + half, half))


def merge_kernel(best_ref, partner_ref, above_ref, beside_ref, out_ref):
    quarter = above_ref.shape[1]
    half = quarter // 2
    rep, odd, _ = position()
    inside = lax.axis_index("shard") >= 2
    out_ref[...] = best_ref[...]

    def raised(at, values):
        cols = pl.ds(pl.multiple_of(at, half), values.shape[1])
        out_ref[:, cols] = jnp.maximum(out_ref[:, cols], values)

    raised((rep ^ (2 - odd)) * quarter, partner_ref[...])
    raised(rep * quarter, jnp.where(inside, above_ref[...], -1.0))
    beside = jnp.where(inside & (odd == 0), beside_ref[...], -1.0)
    raised((rep ^ 2) * quarter, beside[:, :half])
    raised(rep * quarter + half, beside[:, half:])


def local(embeddings, labels):
    rows, width = embeddings.shape
    shards, reps = lax.axis_size("shard"), lax.axis_size("rep")
    quarter = rows // reps
    half = quarter // 2

    def along_shard(block, distance, keep=lambda i: True):
        route = [
            (i, i + distance) for i in range(shards) if i + distance in range(shards) and keep(i)
        ]
        return lax.ppermute(block, "shard", route)

    def partner(block):
        return lax.ppermute(block, "shard", [(i, i ^ 1) for i in range(shards)])

    def other_rep(block, flip):
        return lax.ppermute(block, "rep", [(i, i ^ flip) for i in range(reps)])

    def call(kernel, name, shapes, specs, *arrays):
        return pl.pallas_call(
            kernel,
            out_shape=[jax.ShapeDtypeStruct(shape, dtype) for shape, dtype in shapes],
            in_specs=specs[: len(arrays)],
            out_specs=specs[len(arrays) :],
            compiler_params=pltpu.CompilerParams(vmem_limit_bytes=VMEM_LIMIT),
            cost_estimate=pl.CostEstimate(flops=1024, bytes_accessed=1024, transcendentals=0),
            name=name,
        )(*arrays)

    sizes = [half, half + INFO, quarter + INFO, quarter + INFO]
    lo, hi, mine, across = pl.pallas_call(
        prepare_kernel,
        out_shape=[jax.ShapeDtypeStruct((size, width), BF16) for size in sizes],
        in_specs=[pl.BlockSpec(memory_space=pltpu.HBM)] * 2,
        out_specs=[VMEM] * 4,
        scratch_shapes=[
            pltpu.VMEM((4, half, width), BF16),
            pltpu.VMEM((rows // 128, 128), jnp.int32),
            pltpu.SemaphoreType.DMA((5,)),
        ],
        compiler_params=pltpu.CompilerParams(vmem_limit_bytes=PREPARE_LIMIT),
        name="prepare",
    )(embeddings, labels.reshape(rows // 128, 128))

    odd_only, even_only = (lambda i: i % 2 == 1), (lambda i: i % 2 == 0)
    fence = lax.optimization_barrier

    low_0a = along_shard(lo, 2)
    high = along_shard(mine, -2)
    across = partner(across)
    low_0b = along_shard(hi, 2)

    low_0a, own_labels = fence((low_0a, labels))
    low_2a = other_rep(low_0a, 2)
    low_1a = other_rep(low_0a, 1)
    own, best, own_reach = pl.pallas_call(
        own_kernel,
        out_shape=[
            jax.ShapeDtypeStruct((rows, width), BF16),
            jax.ShapeDtypeStruct((1, rows), F32),
            jax.ShapeDtypeStruct((2,), jnp.int32),
        ],
        in_specs=[pl.BlockSpec(memory_space=pltpu.HBM), VMEM],
        out_specs=[VMEM, VMEM, SMEM],
        scratch_shapes=[
            pltpu.VMEM((8, rows), jnp.int32),
            pltpu.VMEM((4, quarter, width), BF16),
            pltpu.SemaphoreType.DMA((4,)),
        ],
        compiler_params=pltpu.CompilerParams(vmem_limit_bytes=OWN_LIMIT),
        cost_estimate=pl.CostEstimate(flops=1024, bytes_accessed=1024, transcendentals=0),
        name="own",
    )(embeddings, own_labels[None, :])

    across, high, own, best = fence((across, high, own, best))
    up_a = along_shard(across[:half], -2, odd_only)
    up_b = along_shard(high[half:], 1, even_only)
    low_0b, low_1a, low_2a, across, high = fence((low_0b, low_1a, low_2a, across, high))
    low_2b = other_rep(low_0b, 2)
    low_1b = other_rep(low_0b, 1)
    low_3a = other_rep(low_2a, 1)
    results = [((1, quarter), F32)] * 2
    best, of_across, of_high, reach = call(
        near_kernel, "near", [((1, rows), F32)] + results + [((6,), jnp.int32)],
        [SMEM] + [VMEM] * 11 + [SMEM],
        own_reach, own, best, low_0a, low_0b, low_1a, low_2a, across, high,
    )
    low_2b, up_a, up_b, low_1b, low_3a, of_across = fence(
        (low_2b, up_a, up_b, low_1b, low_3a, of_across)
    )
    low_3b = other_rep(low_2b, 1)
    of_across, of_high, of_up, side = call(
        far_kernel, "far", results + [((1, quarter), F32), ((2,), jnp.int32)],
        [SMEM] + [VMEM] * 16 + [SMEM],
        reach, of_across, of_high, low_0a, low_0b, low_1a, low_1b, low_2a, low_2b,
        low_3a, across, high, up_a, up_b,
    )
    of_high, of_up = call(
        last_kernel, "last", results, [SMEM] * 2 + [VMEM] * 8,
        reach, side, of_high, of_up, low_3b, high, up_a, up_b,
    )

    above = along_shard(of_high, 2)
    beside = along_shard(of_up, 1, odd_only)
    from_partner = partner(of_across)
    (best,) = call(
        merge_kernel, "merge", [((1, rows), F32)], [VMEM] * 5, best, from_partner, above, beside
    )
    return lax.pmax(best[0], "rep")


def solution(mesh):
    placed = (P("shard", None), P("shard"))
    return jax.shard_map(local, mesh=mesh, in_specs=placed, out_specs=P("shard"), check_vma=False)
```

```python
import functools
import math

import jax
import jax.numpy as jnp
from jax import lax
from jax.experimental import pallas as pl
from jax.experimental.pallas import tpu as pltpu
from jax.sharding import PartitionSpec as P

F32 = jnp.float32
BF16 = jnp.bfloat16
TILE = 256
WIDE = 512
INFO = 16
VMEM_LIMIT = 32 * 1024 * 1024
OWN_LIMIT = 46 * 1024 * 1024
PREPARE_LIMIT = 50 * 1024 * 1024
VMEM = pl.BlockSpec(memory_space=pltpu.VMEM)
SMEM = pl.BlockSpec(memory_space=pltpu.SMEM)


def normalize(values):
    as_float = values.astype(F32)
    width = values.shape[1]
    inverse = lax.rsqrt(jnp.sum(as_float * as_float, axis=1, keepdims=True) * (1 / width) + 1e-06)
    return (as_float * (inverse * (1 / math.sqrt(width)))).astype(BF16)


def score(keys, queries):
    return lax.dot_general(keys, queries, (((1,), (1,)), ((), ())), preferred_element_type=F32)


def fold(values):
    rows, cols = values.shape
    return jnp.max(values.reshape(rows // 8, 8, cols), axis=0)


def position():
    rep, odd = lax.axis_index("rep"), lax.axis_index("shard") % 2
    return rep, odd, rep ^ (1 + odd)


def prepare_kernel(emb_ref, labels_hbm, lo_out, hi_out, mine_out, across_out, raw, labels_ref, sems):
    rep, odd, _ = position()
    quarter = mine_out.shape[0] - INFO
    part = quarter // 2
    copies = []
    for n in range(4):
        piece = rep if n < 2 else rep ^ (2 - odd)
        at = pl.multiple_of(piece * quarter + (n % 2) * part, part)
        copies.append(pltpu.make_async_copy(emb_ref.at[pl.ds(at, part), :], raw.at[n], sems.at[n]))
        copies[-1].start()
    fetch = pltpu.make_async_copy(labels_hbm, labels_ref, sems.at[4])
    fetch.start()
    fetch.wait()
    labels = labels_ref[...]
    first, last = jnp.min(labels), jnp.max(labels)
    head = jnp.sum((labels == first).astype(jnp.int32))
    tail = jnp.sum((labels == last).astype(jnp.int32))
    row = lax.broadcasted_iota(jnp.int32, (INFO, mine_out.shape[1]), 0)
    info = jnp.zeros(row.shape, jnp.int32)
    for n, value in enumerate([first, head // 16, head % 16, last, tail // 16, tail % 16]):
        info = jnp.where(row == n, value, info)
    info = info.astype(F32).astype(BF16)
    for n, copy in enumerate(copies):
        copy.wait()
        out = mine_out if n < 2 else across_out
        for m in range(part // 128):
            rows = pl.ds(m * 128, 128)
            values = normalize(raw[n, rows, :])
            out[pl.ds((n % 2) * part + m * 128, 128), :] = values
            if n < 2:
                (lo_out, hi_out)[n][rows, :] = values
    hi_out[pl.ds(part, INFO), :] = info
    mine_out[pl.ds(quarter, INFO), :] = info
    across_out[pl.ds(quarter, INFO), :] = info


def read_reach(ref, at):
    block = ref[pl.ds(ref.shape[0] - INFO, INFO), pl.ds(0, 128)].astype(F32)
    packed = block[at : at + 1] + 256.0 * (16.0 * block[at + 1 : at + 2] + block[at + 2 : at + 3])
    packed = jnp.max(packed).astype(jnp.int32)
    return packed % 256, packed // 256


def group(keys, queries_ref, query_rows, out_ref, out_at, count):
    step = min(WIDE, query_rows)

    def over_queries(j, _):
        at = pl.multiple_of(j * step, step)
        queries = queries_ref[pl.ds(at, step), :]
        best = None
        for ref, row, rows, first in keys:
            scores = score(ref[pl.ds(row, rows), :], queries)
            index = lax.broadcasted_iota(jnp.int32, scores.shape, 0)
            top = fold(jnp.where(index >= first, scores, -1.0))
            best = top if best is None else jnp.maximum(best, top)
        best = jnp.max(best, axis=0, keepdims=True)
        col = lax.broadcasted_iota(jnp.int32, best.shape, 1) + at
        cols = pl.ds(pl.multiple_of(out_at + at, TILE), step)
        out_ref[:, cols] = jnp.maximum(out_ref[:, cols], jnp.where(col < count, best, -1.0))
        return 0

    lax.fori_loop(0, (count + step - 1) // step, over_queries, 0)


def own_kernel(emb_ref, labels_ref, own_out, best_out, reach_out, start, raw, sems):
    rows = emb_ref.shape[0]
    rep = lax.axis_index("rep")
    parts = raw.shape[0]
    size = rows // parts
    copies = [
        pltpu.make_async_copy(emb_ref.at[pl.ds(n * size, size), :], raw.at[n], sems.at[n])
        for n in range(parts)
    ]
    for copy in copies:
        copy.start()
    labels = jnp.broadcast_to(labels_ref[...], start.shape)
    first = jnp.min(labels)
    reach_out[0] = first
    reach_out[1] = jnp.sum((labels == first).astype(jnp.int32)) // start.shape[0]
    lane = lax.broadcasted_iota(jnp.int32, labels.shape, 1)
    begin = jnp.where((lane == 0) | (labels != pltpu.roll(labels, 1, 1)), lane, 0)
    shift = 1
    while shift < rows:
        begin = jnp.maximum(begin, jnp.where(lane >= shift, pltpu.roll(begin, shift, 1), 0))
        shift *= 2
    start[...] = begin
    best_out[...] = jnp.full(best_out.shape, -1.0, F32)
    for n, copy in enumerate(copies):
        copy.wait()
        for m in range(size // 128):
            values = normalize(raw[n, pl.ds(m * 128, 128), :])
            own_out[pl.ds(n * size + m * 128, 128), :] = values
    for n in range(2):
        tile = rep if n == 0 else rows // TILE - 1 - rep
        at = pl.multiple_of(tile * TILE, TILE)
        keys = own_out[pl.ds(at, TILE), :]

        def over_queries(j, _):
            cols = pl.ds(pl.multiple_of(j * WIDE, WIDE), WIDE)
            scores = score(keys, own_out[cols, :])
            row = lax.broadcasted_iota(jnp.int32, scores.shape, 0) + at
            col = lax.broadcasted_iota(jnp.int32, scores.shape, 1) + j * WIDE
            keep = (row >= start[0:1, cols]) & (row < col)
            best = jnp.max(fold(jnp.where(keep, scores, -1.0)), axis=0, keepdims=True)
            best_out[:, cols] = jnp.maximum(best_out[:, cols], best)
            return 0

        lax.fori_loop(at // WIDE, rows // WIDE, over_queries, 0)


def reached(query, key, offset, limit):
    count = jnp.clip(query[1] - offset, 0, limit)
    return jnp.where(query[0] == key[0], count, 0)


def lower_keys(rep, tail, rows, pieces):
    half = rows // 8
    return [
        (ref, 0, half, jnp.clip(rows - tail - (rep ^ flip) * 2 * half - part * half, 0, half))
        for ref, flip, part in pieces
    ]


def near_kernel(own_reach, own_ref, best_ref, low_0a, low_0b, low_1a, low_2a, across, high,
                best_out, across_out, high_out, reach_out):
    rows = own_ref.shape[0]
    quarter = across.shape[0] - INFO
    rep, odd, part = position()
    mine = (own_reach[0], own_reach[1])
    low, beside_head = read_reach(low_0b, 3), read_reach(across, 0)
    beside_tail, up = read_reach(across, 3), read_reach(high, 0)
    for n, value in enumerate(low + beside_head + up):
        reach_out[n] = value
    best_out[...] = best_ref[...]
    across_out[...] = jnp.full(across_out.shape, -1.0, F32)
    high_out[...] = jnp.full(high_out.shape, -1.0, F32)

    lows = lower_keys(
        rep, low[1], rows, [(low_0a, 0, 0), (low_0b, 0, 1), (low_1a, 1, 0), (low_2a, 2, 0)]
    )
    besides = [
        (across, 0, quarter, jnp.clip(rows - beside_tail[1] - part * quarter, 0, quarter))
    ]
    group(lows[:2], own_ref, rows, best_out, 0, reached(mine, low, 0, rows))
    count = jnp.where(odd == 1, reached(mine, beside_tail, 0, rows), 0)
    group(besides, own_ref, rows, best_out, 0, count)
    group(lows, across, quarter, across_out, 0, reached(beside_head, low, part * quarter, quarter))
    group(besides, high, quarter, high_out, 0, reached(up, beside_tail, rep * quarter, quarter))
    group(lows, high, quarter, high_out, 0, reached(up, low, rep * quarter, quarter))


def far_kernel(reach_ref, across_ref, high_ref, low_0a, low_0b, low_1a, low_1b, low_2a,
               low_2b, low_3a, across, high, up_a, up_b, across_out, high_out, up_out, side_out):
    quarter = across.shape[0] - INFO
    half = quarter // 2
    rep, _, part = position()
    low, beside, up = [(reach_ref[2 * n], reach_ref[2 * n + 1]) for n in range(3)]
    side = read_reach(up_b, 0)
    side_out[0], side_out[1] = side
    across_out[...] = across_ref[...]
    high_out[...] = high_ref[...]
    up_out[...] = jnp.full(up_out.shape, -1.0, F32)

    lows = lower_keys(
        rep, low[1], 4 * quarter,
        [(low_1b, 1, 1), (low_2b, 2, 1), (low_3a, 3, 0), (low_0a, 0, 0), (low_0b, 0, 1), (low_1a, 1, 0), (low_2a, 2, 0)],
    )
    group(lows[:2], across, quarter, across_out, 0, reached(beside, low, part * quarter, quarter))
    group(lows[:3], high, quarter, high_out, 0, reached(up, low, rep * quarter, quarter))
    group(lows, up_a, half, up_out, 0, reached(side, low, (rep ^ 2) * quarter, half))
    group(lows, up_b, half, up_out, half, reached(side, low, rep * quarter + half, half))


def last_kernel(reach_ref, side_ref, high_ref, up_ref, low_3b, high, up_a, up_b,
                high_out, up_out):
    half = up_a.shape[0]
    quarter = 2 * half
    rep = lax.axis_index("rep")
    low, up = (reach_ref[0], reach_ref[1]), (reach_ref[4], reach_ref[5])
    side = (side_ref[0], side_ref[1])
    high_out[...], up_out[...] = high_ref[...], up_ref[...]
    lows = lower_keys(rep, low[1], 4 * quarter, [(low_3b, 3, 1)])
    group(lows, high, quarter, high_out, 0, reached(up, low, rep * quarter, quarter))
    group(lows, up_a, half, up_out, 0, reached(side, low, (rep ^ 2) * quarter, half))
    group(lows, up_b, half, up_out, half, reached(side, low, rep * quarter + half, half))


def merge_kernel(best_ref, across_ref, high_ref, up_ref, out_ref):
    rows, quarter = best_ref.shape[1], high_ref.shape[1]
    half = quarter // 2
    shards = out_ref.shape[1] // rows
    rep, odd, part = position()
    shard = lax.axis_index("shard")
    out_ref[...] = jnp.full(out_ref.shape, -1.0, F32)

    def put(at, values):
        out_ref[:, pl.ds(pl.multiple_of(at, half), values.shape[1])] = values

    put(shard * rows, best_ref[...])
    put((shard ^ 1) * rows + part * quarter, across_ref[...])

    @pl.when(shard + 2 < shards)
    def _():
        put((shard + 2) * rows + rep * quarter, high_ref[...])

    @pl.when((odd == 1) & (shard + 1 < shards))
    def _():
        put((shard + 1) * rows + (rep ^ 2) * quarter, up_ref[:, :half])
        put((shard + 1) * rows + rep * quarter + half, up_ref[:, half:])


def local(embeddings, labels):
    rows, width = embeddings.shape
    shards, reps = lax.axis_size("shard"), lax.axis_size("rep")
    quarter = rows // reps
    half = quarter // 2

    def along_shard(block, distance, keep=lambda i: True):
        route = [
            (i, i + distance) for i in range(shards) if i + distance in range(shards) and keep(i)
        ]
        return lax.ppermute(block, "shard", route)

    def partner(block):
        return lax.ppermute(block, "shard", [(i, i ^ 1) for i in range(shards)])

    def other_rep(block, flip):
        return lax.ppermute(block, "rep", [(i, i ^ flip) for i in range(reps)])

    def call(kernel, name, shapes, specs, *arrays):
        return pl.pallas_call(
            kernel,
            out_shape=[jax.ShapeDtypeStruct(shape, dtype) for shape, dtype in shapes],
            in_specs=specs[: len(arrays)],
            out_specs=specs[len(arrays) :],
            compiler_params=pltpu.CompilerParams(vmem_limit_bytes=VMEM_LIMIT),
            cost_estimate=pl.CostEstimate(flops=1024, bytes_accessed=1024, transcendentals=0),
            name=name,
        )(*arrays)

    sizes = [half, half + INFO, quarter + INFO, quarter + INFO]
    lo, hi, mine, across = pl.pallas_call(
        prepare_kernel,
        out_shape=[jax.ShapeDtypeStruct((size, width), BF16) for size in sizes],
        in_specs=[pl.BlockSpec(memory_space=pltpu.HBM)] * 2,
        out_specs=[VMEM] * 4,
        scratch_shapes=[
            pltpu.VMEM((4, half, width), BF16),
            pltpu.VMEM((rows // 128, 128), jnp.int32),
            pltpu.SemaphoreType.DMA((5,)),
        ],
        compiler_params=pltpu.CompilerParams(vmem_limit_bytes=PREPARE_LIMIT),
        name="prepare",
    )(embeddings, labels.reshape(rows // 128, 128))

    odd_only, even_only = (lambda i: i % 2 == 1), (lambda i: i % 2 == 0)
    fence = lax.optimization_barrier

    low_0a = along_shard(lo, 2)
    high = along_shard(mine, -2)
    across = partner(across)
    low_0b = along_shard(hi, 2)

    low_0a, own_labels = fence((low_0a, labels))
    low_2a = other_rep(low_0a, 2)
    low_1a = other_rep(low_0a, 1)
    own, best, own_reach = pl.pallas_call(
        own_kernel,
        out_shape=[
            jax.ShapeDtypeStruct((rows, width), BF16),
            jax.ShapeDtypeStruct((1, rows), F32),
            jax.ShapeDtypeStruct((2,), jnp.int32),
        ],
        in_specs=[pl.BlockSpec(memory_space=pltpu.HBM), VMEM],
        out_specs=[VMEM, VMEM, SMEM],
        scratch_shapes=[
            pltpu.VMEM((8, rows), jnp.int32),
            pltpu.VMEM((4, quarter, width), BF16),
            pltpu.SemaphoreType.DMA((4,)),
        ],
        compiler_params=pltpu.CompilerParams(vmem_limit_bytes=OWN_LIMIT),
        cost_estimate=pl.CostEstimate(flops=1024, bytes_accessed=1024, transcendentals=0),
        name="own",
    )(embeddings, own_labels[None, :])

    across, high, own, best = fence((across, high, own, best))
    up_a = along_shard(across[:half], -2, odd_only)
    up_b = along_shard(high[half:], 1, even_only)
    low_0b, low_1a, low_2a, across, high = fence((low_0b, low_1a, low_2a, across, high))
    low_2b = other_rep(low_0b, 2)
    low_1b = other_rep(low_0b, 1)
    low_3a = other_rep(low_2a, 1)
    results = [((1, quarter), F32)] * 2
    best, of_across, of_high, reach = call(
        near_kernel, "near", [((1, rows), F32)] + results + [((6,), jnp.int32)],
        [SMEM] + [VMEM] * 11 + [SMEM],
        own_reach, own, best, low_0a, low_0b, low_1a, low_2a, across, high,
    )
    low_2b, up_a, up_b, low_1b, low_3a, of_across = fence(
        (low_2b, up_a, up_b, low_1b, low_3a, of_across)
    )
    low_3b = other_rep(low_2b, 1)
    of_across, of_high, of_up, side = call(
        far_kernel, "far", results + [((1, quarter), F32), ((2,), jnp.int32)],
        [SMEM] + [VMEM] * 16 + [SMEM],
        reach, of_across, of_high, low_0a, low_0b, low_1a, low_1b, low_2a, low_2b,
        low_3a, across, high, up_a, up_b,
    )
    of_high, of_up = call(
        last_kernel, "last", results, [SMEM] * 2 + [VMEM] * 8,
        reach, side, of_high, of_up, low_3b, high, up_a, up_b,
    )

    (best,) = call(
        merge_kernel, "merge", [((1, shards * rows), F32)], [VMEM] * 5, best, of_across, of_high, of_up
    )
    best = lax.pmax(best[0], ("shard", "rep"))
    return lax.dynamic_slice_in_dim(best, lax.axis_index("shard") * rows, rows, 0)


def solution(mesh):
    placed = (P("shard", None), P("shard"))
    return jax.shard_map(local, mesh=mesh, in_specs=placed, out_specs=P("shard"), check_vma=False)
```

```python
import functools
import math

import jax
import jax.numpy as jnp
from jax import lax
from jax.experimental import pallas as pl
from jax.experimental.pallas import tpu as pltpu
from jax.sharding import PartitionSpec as P

F32 = jnp.float32
BF16 = jnp.bfloat16
TILE = 256
WIDE = 512
INFO = 16
VMEM_LIMIT = 32 * 1024 * 1024
OWN_LIMIT = 46 * 1024 * 1024
PREPARE_LIMIT = 50 * 1024 * 1024
VMEM = pl.BlockSpec(memory_space=pltpu.VMEM)
SMEM = pl.BlockSpec(memory_space=pltpu.SMEM)


def normalize(values):
    as_float = values.astype(F32)
    width = values.shape[1]
    inverse = lax.rsqrt(jnp.sum(as_float * as_float, axis=1, keepdims=True) * (1 / width) + 1e-06)
    return (as_float * (inverse * (1 / math.sqrt(width)))).astype(BF16)


def score(keys, queries):
    return lax.dot_general(keys, queries, (((1,), (1,)), ((), ())), preferred_element_type=F32)


def fold(values):
    rows, cols = values.shape
    return jnp.max(values.reshape(rows // 8, 8, cols), axis=0)


def prepare_kernel(emb_ref, labels_hbm, lo_out, hi_out, mine_out, raw, labels_ref, sems):
    rep = lax.axis_index("rep")
    quarter = mine_out.shape[0] - INFO
    part = quarter // 2
    copies = []
    for n in range(2):
        at = pl.multiple_of(rep * quarter + n * part, part)
        copies.append(pltpu.make_async_copy(emb_ref.at[pl.ds(at, part), :], raw.at[n], sems.at[n]))
        copies[-1].start()
    fetch = pltpu.make_async_copy(labels_hbm, labels_ref, sems.at[2])
    fetch.start()
    fetch.wait()
    labels = labels_ref[...]
    first, last = jnp.min(labels), jnp.max(labels)
    head = jnp.sum((labels == first).astype(jnp.int32))
    tail = jnp.sum((labels == last).astype(jnp.int32))
    row = lax.broadcasted_iota(jnp.int32, (INFO, mine_out.shape[1]), 0)
    info = jnp.zeros(row.shape, jnp.int32)
    for n, value in enumerate([first, head // 16, head % 16, last, tail // 16, tail % 16]):
        info = jnp.where(row == n, value, info)
    info = info.astype(F32).astype(BF16)
    for n, copy in enumerate(copies):
        copy.wait()
        for m in range(part // 128):
            rows = pl.ds(m * 128, 128)
            values = normalize(raw[n, rows, :])
            mine_out[pl.ds(n * part + m * 128, 128), :] = values
            (lo_out, hi_out)[n][rows, :] = values
    hi_out[pl.ds(part, INFO), :] = info
    mine_out[pl.ds(quarter, INFO), :] = info


def read_reach(ref, at):
    block = ref[pl.ds(ref.shape[0] - INFO, INFO), pl.ds(0, 128)].astype(F32)
    packed = block[at : at + 1] + 256.0 * (16.0 * block[at + 1 : at + 2] + block[at + 2 : at + 3])
    packed = jnp.max(packed).astype(jnp.int32)
    return packed % 256, packed // 256


def group(keys, queries_ref, query_rows, out_ref, out_at, count):
    step = min(WIDE, query_rows)

    def over_queries(j, _):
        at = pl.multiple_of(j * step, step)
        queries = queries_ref[pl.ds(at, step), :]
        best = None
        for ref, row, rows, first in keys:
            scores = score(ref[pl.ds(row, rows), :], queries)
            index = lax.broadcasted_iota(jnp.int32, scores.shape, 0)
            top = fold(jnp.where(index >= first, scores, -1.0))
            best = top if best is None else jnp.maximum(best, top)
        best = jnp.max(best, axis=0, keepdims=True)
        col = lax.broadcasted_iota(jnp.int32, best.shape, 1) + at
        cols = pl.ds(pl.multiple_of(out_at + at, TILE), step)
        out_ref[:, cols] = jnp.maximum(out_ref[:, cols], jnp.where(col < count, best, -1.0))
        return 0

    lax.fori_loop(0, (count + step - 1) // step, over_queries, 0)


def own_kernel(emb_ref, labels_ref, own_out, best_out, reach_out, start, raw, sems):
    rows = emb_ref.shape[0]
    rep = lax.axis_index("rep")
    parts = raw.shape[0]
    size = rows // parts
    copies = [
        pltpu.make_async_copy(emb_ref.at[pl.ds(n * size, size), :], raw.at[n], sems.at[n])
        for n in range(parts)
    ]
    for copy in copies:
        copy.start()
    labels = jnp.broadcast_to(labels_ref[...], start.shape)
    first = jnp.min(labels)
    reach_out[0] = first
    reach_out[1] = jnp.sum((labels == first).astype(jnp.int32)) // start.shape[0]
    lane = lax.broadcasted_iota(jnp.int32, labels.shape, 1)
    begin = jnp.where((lane == 0) | (labels != pltpu.roll(labels, 1, 1)), lane, 0)
    shift = 1
    while shift < rows:
        begin = jnp.maximum(begin, jnp.where(lane >= shift, pltpu.roll(begin, shift, 1), 0))
        shift *= 2
    start[...] = begin
    best_out[...] = jnp.full(best_out.shape, -1.0, F32)
    for n, copy in enumerate(copies):
        copy.wait()
        for m in range(size // 128):
            values = normalize(raw[n, pl.ds(m * 128, 128), :])
            own_out[pl.ds(n * size + m * 128, 128), :] = values
    for n in range(2):
        tile = rep if n == 0 else rows // TILE - 1 - rep
        at = pl.multiple_of(tile * TILE, TILE)
        keys = own_out[pl.ds(at, TILE), :]

        def over_queries(j, _):
            cols = pl.ds(pl.multiple_of(j * WIDE, WIDE), WIDE)
            scores = score(keys, own_out[cols, :])
            row = lax.broadcasted_iota(jnp.int32, scores.shape, 0) + at
            col = lax.broadcasted_iota(jnp.int32, scores.shape, 1) + j * WIDE
            keep = (row >= start[0:1, cols]) & (row < col)
            best = jnp.max(fold(jnp.where(keep, scores, -1.0)), axis=0, keepdims=True)
            best_out[:, cols] = jnp.maximum(best_out[:, cols], best)
            return 0

        lax.fori_loop(at // WIDE, rows // WIDE, over_queries, 0)


def reached(query, key, offset, limit):
    count = jnp.clip(query[1] - offset, 0, limit)
    return jnp.where(query[0] == key[0], count, 0)


def key_piece(ref, tail, rows, at, size):
    return (ref, 0, size, jnp.clip(rows - tail - at, 0, size))


def upper(pieces, keys, up, rep, out_ref, enabled=True):
    half = TILE
    for ref, flip, part in pieces:
        at = (rep ^ flip) * 2 * half + part * half
        for last, several in keys:
            count = jnp.where(enabled, reached(up, last, at, half), 0)
            group(several, ref, half, out_ref, at, count)


def near_kernel(own_reach, own_ref, best_ref, low, across, high_0a, high_0b, high_1a, high_2a,
                best_out, high_out, reach_out):
    rows = own_ref.shape[0]
    quarter = across.shape[0] - INFO
    rep, odd = lax.axis_index("rep"), lax.axis_index("shard") % 2
    mine = (own_reach[0], own_reach[1])
    lower, beside, up = read_reach(low, 3), read_reach(across, 3), read_reach(high_0b, 0)
    for n, value in enumerate(lower + beside + up):
        reach_out[n] = value
    best_out[...] = best_ref[...]
    high_out[...] = jnp.full(high_out.shape, -1.0, F32)
    lows = [key_piece(low, lower[1], rows, rep * quarter, quarter)]
    besides = [key_piece(across, beside[1], rows, rep * quarter, quarter)]
    group(lows, own_ref, rows, best_out, 0, reached(mine, lower, 0, rows))
    count = jnp.where(odd == 1, reached(mine, beside, 0, rows), 0)
    group(besides, own_ref, rows, best_out, 0, count)
    pieces = [(high_0a, 0, 0), (high_0b, 0, 1), (high_1a, 1, 0), (high_2a, 2, 0)]
    upper(pieces, [(beside, besides), (lower, lows)], up, rep, high_out)


def far_parts(reach_ref, side, low, across, side_a, side_b):
    half = TILE
    quarter, rows = 2 * half, 8 * half
    rep, odd = lax.axis_index("rep"), lax.axis_index("shard") % 2
    lower, beside, up = [(reach_ref[2 * n], reach_ref[2 * n + 1]) for n in range(3)]
    at = rep * quarter
    both = [
        (beside, [key_piece(across, beside[1], rows, at, quarter)]),
        (lower, [key_piece(low, lower[1], rows, at, quarter)]),
    ]
    sides = [
        key_piece(side_a, side[1], rows, at + half, half),
        key_piece(side_b, side[1], rows, at, half),
    ]
    return rep, odd == 0, up, both, [(side, sides)]


def far_kernel(reach_ref, prior_ref, low, across, high_0a, high_0b, high_1a, high_1b, high_2a,
               high_2b, high_3a, side_a, side_b, high_out, side_out):
    side = read_reach(side_a, 3)
    side_out[0], side_out[1] = side
    rep, even, up, both, sides = far_parts(reach_ref, side, low, across, side_a, side_b)
    high_out[...] = prior_ref[...]
    late = [(high_1b, 1, 1), (high_2b, 2, 1), (high_3a, 3, 0)]
    upper(late, both, up, rep, high_out)
    early = [(high_0a, 0, 0), (high_0b, 0, 1), (high_1a, 1, 0), (high_2a, 2, 0)]
    upper(early + late, sides, up, rep, high_out, even)


def last_kernel(reach_ref, side_ref, prior_ref, low, across, high_3b, side_a, side_b, high_out):
    side = (side_ref[0], side_ref[1])
    rep, even, up, both, sides = far_parts(reach_ref, side, low, across, side_a, side_b)
    high_out[...] = prior_ref[...]
    upper([(high_3b, 3, 1)], both, up, rep, high_out)
    upper([(high_3b, 3, 1)], sides, up, rep, high_out, even)


def local(embeddings, labels):
    rows, width = embeddings.shape
    shards, reps = lax.axis_size("shard"), lax.axis_size("rep")
    quarter = rows // reps
    half = quarter // 2

    def along_shard(block, distance, keep=lambda i: True):
        route = [
            (i, i + distance) for i in range(shards) if i + distance in range(shards) and keep(i)
        ]
        return lax.ppermute(block, "shard", route)

    def partner(block):
        return lax.ppermute(block, "shard", [(i, i ^ 1) for i in range(shards)])

    def other_rep(block, flip):
        return lax.ppermute(block, "rep", [(i, i ^ flip) for i in range(reps)])

    def call(kernel, name, shapes, specs, *arrays):
        return pl.pallas_call(
            kernel,
            out_shape=[jax.ShapeDtypeStruct(shape, dtype) for shape, dtype in shapes],
            in_specs=specs[: len(arrays)],
            out_specs=specs[len(arrays) :],
            compiler_params=pltpu.CompilerParams(vmem_limit_bytes=VMEM_LIMIT),
            cost_estimate=pl.CostEstimate(flops=1024, bytes_accessed=1024, transcendentals=0),
            name=name,
        )(*arrays)

    sizes = [half, half + INFO, quarter + INFO]
    lo, hi, mine = pl.pallas_call(
        prepare_kernel,
        out_shape=[jax.ShapeDtypeStruct((size, width), BF16) for size in sizes],
        in_specs=[pl.BlockSpec(memory_space=pltpu.HBM)] * 2,
        out_specs=[VMEM] * 3,
        scratch_shapes=[
            pltpu.VMEM((2, half, width), BF16),
            pltpu.VMEM((rows // 128, 128), jnp.int32),
            pltpu.SemaphoreType.DMA((3,)),
        ],
        compiler_params=pltpu.CompilerParams(vmem_limit_bytes=PREPARE_LIMIT),
        name="prepare",
    )(embeddings, labels.reshape(rows // 128, 128))

    odd_only, even_only = (lambda i: i % 2 == 1), (lambda i: i % 2 == 0)
    fence = lax.optimization_barrier

    high_0a = along_shard(lo, -2)
    low = along_shard(mine, 2)
    across = partner(mine)
    high_0b = along_shard(hi, -2)

    high_0a, own_labels = fence((high_0a, labels))
    high_2a = other_rep(high_0a, 2)
    high_1a = other_rep(high_0a, 1)
    own, best, own_reach = pl.pallas_call(
        own_kernel,
        out_shape=[
            jax.ShapeDtypeStruct((rows, width), BF16),
            jax.ShapeDtypeStruct((1, rows), F32),
            jax.ShapeDtypeStruct((2,), jnp.int32),
        ],
        in_specs=[pl.BlockSpec(memory_space=pltpu.HBM), VMEM],
        out_specs=[VMEM, VMEM, SMEM],
        scratch_shapes=[
            pltpu.VMEM((8, rows), jnp.int32),
            pltpu.VMEM((4, quarter, width), BF16),
            pltpu.SemaphoreType.DMA((4,)),
        ],
        compiler_params=pltpu.CompilerParams(vmem_limit_bytes=OWN_LIMIT),
        cost_estimate=pl.CostEstimate(flops=1024, bytes_accessed=1024, transcendentals=0),
        name="own",
    )(embeddings, own_labels[None, :])

    across, low, own, best = fence((across, low, own, best))
    side_b = along_shard(across[:half], 2, even_only)
    side_a = along_shard(low[half:], -1, odd_only)
    high_0b, high_1a, high_2a, across, low = fence((high_0b, high_1a, high_2a, across, low))
    high_2b = other_rep(high_0b, 2)
    high_1b = other_rep(high_0b, 1)
    high_3a = other_rep(high_2a, 1)
    line = ((1, rows), F32)
    best, of_high, reach = call(
        near_kernel, "near", [line, line, ((6,), jnp.int32)],
        [SMEM] + [VMEM] * 10 + [SMEM],
        own_reach, own, best, low, across, high_0a, high_0b, high_1a, high_2a,
    )
    high_2b, side_a, side_b, high_1b, high_3a, of_high = fence(
        (high_2b, side_a, side_b, high_1b, high_3a, of_high)
    )
    high_3b = other_rep(high_2b, 1)
    of_high, side = call(
        far_kernel, "far", [line, ((2,), jnp.int32)], [SMEM] + [VMEM] * 13 + [SMEM],
        reach, of_high, low, across, high_0a, high_0b, high_1a, high_1b, high_2a, high_2b,
        high_3a, side_a, side_b,
    )
    (of_high,) = call(
        last_kernel, "last", [line], [SMEM] * 2 + [VMEM] * 7,
        reach, side, of_high, low, across, high_3b, side_a, side_b,
    )

    above = along_shard(of_high, 2)[0]
    above = jnp.where(lax.axis_index("shard") >= 2, above, -1.0)
    return lax.pmax(jnp.maximum(best[0], above), "rep")


def solution(mesh):
    placed = (P("shard", None), P("shard"))
    return jax.shard_map(local, mesh=mesh, in_specs=placed, out_specs=P("shard"), check_vma=False)
```

```python
import functools
import math

import jax
import jax.numpy as jnp
from jax import lax
from jax.experimental import pallas as pl
from jax.experimental.pallas import tpu as pltpu
from jax.sharding import PartitionSpec as P

F32 = jnp.float32
BF16 = jnp.bfloat16
TILE = 256
WIDE = 512
INFO = 16
VMEM_LIMIT = 32 * 1024 * 1024
OWN_LIMIT = 46 * 1024 * 1024
PREPARE_LIMIT = 50 * 1024 * 1024
VMEM = pl.BlockSpec(memory_space=pltpu.VMEM)
SMEM = pl.BlockSpec(memory_space=pltpu.SMEM)


def normalize(values):
    as_float = values.astype(F32)
    width = values.shape[1]
    inverse = lax.rsqrt(jnp.sum(as_float * as_float, axis=1, keepdims=True) * (1 / width) + 1e-06)
    return (as_float * (inverse * (1 / math.sqrt(width)))).astype(BF16)


def score(keys, queries):
    return lax.dot_general(keys, queries, (((1,), (1,)), ((), ())), preferred_element_type=F32)


def fold(values):
    rows, cols = values.shape
    return jnp.max(values.reshape(rows // 8, 8, cols), axis=0)


def prepare_kernel(emb_ref, labels_hbm, lo_out, hi_out, mine_out, raw, labels_ref, sems):
    rep = lax.axis_index("rep")
    quarter = mine_out.shape[0] - INFO
    part = quarter // 2
    copies = []
    for n in range(2):
        at = pl.multiple_of(rep * quarter + n * part, part)
        copies.append(pltpu.make_async_copy(emb_ref.at[pl.ds(at, part), :], raw.at[n], sems.at[n]))
        copies[-1].start()
    fetch = pltpu.make_async_copy(labels_hbm, labels_ref, sems.at[2])
    fetch.start()
    fetch.wait()
    labels = labels_ref[...]
    first, last = jnp.min(labels), jnp.max(labels)
    head = jnp.sum((labels == first).astype(jnp.int32))
    tail = jnp.sum((labels == last).astype(jnp.int32))
    row = lax.broadcasted_iota(jnp.int32, (INFO, mine_out.shape[1]), 0)
    info = jnp.zeros(row.shape, jnp.int32)
    for n, value in enumerate([first, head // 16, head % 16, last, tail // 16, tail % 16]):
        info = jnp.where(row == n, value, info)
    info = info.astype(F32).astype(BF16)
    for n, copy in enumerate(copies):
        copy.wait()
        for m in range(part // 128):
            rows = pl.ds(m * 128, 128)
            values = normalize(raw[n, rows, :])
            mine_out[pl.ds(n * part + m * 128, 128), :] = values
            (lo_out, hi_out)[n][rows, :] = values
    hi_out[pl.ds(part, INFO), :] = info
    mine_out[pl.ds(quarter, INFO), :] = info


def read_reach(ref, at):
    block = ref[pl.ds(ref.shape[0] - INFO, INFO), pl.ds(0, 128)].astype(F32)
    packed = block[at : at + 1] + 256.0 * (16.0 * block[at + 1 : at + 2] + block[at + 2 : at + 3])
    packed = jnp.max(packed).astype(jnp.int32)
    return packed % 256, packed // 256


def group(keys, queries_ref, query_rows, out_ref, out_at, count):
    step = min(WIDE, query_rows)

    def over_queries(j, _):
        at = pl.multiple_of(j * step, step)
        queries = queries_ref[pl.ds(at, step), :]
        best = None
        for ref, row, rows, first in keys:
            scores = score(ref[pl.ds(row, rows), :], queries)
            index = lax.broadcasted_iota(jnp.int32, scores.shape, 0)
            top = fold(jnp.where(index >= first, scores, -1.0))
            best = top if best is None else jnp.maximum(best, top)
        best = jnp.max(best, axis=0, keepdims=True)
        col = lax.broadcasted_iota(jnp.int32, best.shape, 1) + at
        cols = pl.ds(pl.multiple_of(out_at + at, TILE), step)
        out_ref[:, cols] = jnp.maximum(out_ref[:, cols], jnp.where(col < count, best, -1.0))
        return 0

    lax.fori_loop(0, (count + step - 1) // step, over_queries, 0)


def own_kernel(emb_ref, labels_ref, own_out, best_out, reach_out, start, raw, sems):
    rows = emb_ref.shape[0]
    rep = lax.axis_index("rep")
    parts = raw.shape[0]
    size = rows // parts
    copies = [
        pltpu.make_async_copy(emb_ref.at[pl.ds(n * size, size), :], raw.at[n], sems.at[n])
        for n in range(parts)
    ]
    for copy in copies:
        copy.start()
    labels = jnp.broadcast_to(labels_ref[...], start.shape)
    first = jnp.min(labels)
    reach_out[0] = first
    reach_out[1] = jnp.sum((labels == first).astype(jnp.int32)) // start.shape[0]
    lane = lax.broadcasted_iota(jnp.int32, labels.shape, 1)
    begin = jnp.where((lane == 0) | (labels != pltpu.roll(labels, 1, 1)), lane, 0)
    shift = 1
    while shift < rows:
        begin = jnp.maximum(begin, jnp.where(lane >= shift, pltpu.roll(begin, shift, 1), 0))
        shift *= 2
    start[...] = begin
    best_out[...] = jnp.full(best_out.shape, -1.0, F32)
    for n, copy in enumerate(copies):
        copy.wait()
        for m in range(size // 128):
            values = normalize(raw[n, pl.ds(m * 128, 128), :])
            own_out[pl.ds(n * size + m * 128, 128), :] = values
    for n in range(2):
        tile = rep if n == 0 else rows // TILE - 1 - rep
        at = pl.multiple_of(tile * TILE, TILE)
        keys = own_out[pl.ds(at, TILE), :]

        def over_queries(j, _):
            cols = pl.ds(pl.multiple_of(j * WIDE, WIDE), WIDE)
            scores = score(keys, own_out[cols, :])
            row = lax.broadcasted_iota(jnp.int32, scores.shape, 0) + at
            col = lax.broadcasted_iota(jnp.int32, scores.shape, 1) + j * WIDE
            keep = (row >= start[0:1, cols]) & (row < col)
            best = jnp.max(fold(jnp.where(keep, scores, -1.0)), axis=0, keepdims=True)
            best_out[:, cols] = jnp.maximum(best_out[:, cols], best)
            return 0

        lax.fori_loop(at // WIDE, rows // WIDE, over_queries, 0)


def reached(query, key, offset, limit):
    count = jnp.clip(query[1] - offset, 0, limit)
    return jnp.where(query[0] == key[0], count, 0)


def key_piece(ref, tail, rows, at, size):
    return (ref, 0, size, jnp.clip(rows - tail - at, 0, size))


def upper(pieces, keys, up, rep, out_ref, enabled=True):
    half = TILE
    for ref, flip, part in pieces:
        at = (rep ^ flip) * 2 * half + part * half
        for last, several in keys:
            count = jnp.where(enabled, reached(up, last, at, half), 0)
            group(several, ref, half, out_ref, at, count)


def near_kernel(own_reach, own_ref, best_ref, low, across, high_0a, high_0b, high_1a, high_2a,
                best_out, high_out, reach_out):
    rows = own_ref.shape[0]
    quarter = across.shape[0] - INFO
    rep, odd = lax.axis_index("rep"), lax.axis_index("shard") % 2
    mine = (own_reach[0], own_reach[1])
    lower, beside, up = read_reach(low, 3), read_reach(across, 3), read_reach(high_0b, 0)
    for n, value in enumerate(lower + beside + up):
        reach_out[n] = value
    best_out[...] = best_ref[...]
    high_out[...] = jnp.full(high_out.shape, -1.0, F32)
    lows = [key_piece(low, lower[1], rows, rep * quarter, quarter)]
    besides = [key_piece(across, beside[1], rows, rep * quarter, quarter)]
    group(lows, own_ref, rows, best_out, 0, reached(mine, lower, 0, rows))
    count = jnp.where(odd == 1, reached(mine, beside, 0, rows), 0)
    group(besides, own_ref, rows, best_out, 0, count)
    pieces = [(high_0a, 0, 0), (high_0b, 0, 1), (high_1a, 1, 0), (high_2a, 2, 0)]
    upper(pieces, [(beside, besides), (lower, lows)], up, rep, high_out)


def both_keys(reach_ref, low, across):
    quarter, rows = 2 * TILE, 8 * TILE
    rep = lax.axis_index("rep")
    lower, beside, up = [(reach_ref[2 * n], reach_ref[2 * n + 1]) for n in range(3)]
    at = rep * quarter
    both = [
        (beside, [key_piece(across, beside[1], rows, at, quarter)]),
        (lower, [key_piece(low, lower[1], rows, at, quarter)]),
    ]
    return rep, up, both


def middle_kernel(reach_ref, prior_ref, low, across, high_1b, high_3a, high_out):
    rep, up, both = both_keys(reach_ref, low, across)
    high_out[...] = prior_ref[...]
    upper([(high_1b, 1, 1), (high_3a, 3, 0)], both, up, rep, high_out)


def far_parts(reach_ref, side, low, across, side_a, side_b):
    half, rows = TILE, 8 * TILE
    rep, up, both = both_keys(reach_ref, low, across)
    at = rep * 2 * half
    sides = [
        key_piece(side_a, side[1], rows, at + half, half),
        key_piece(side_b, side[1], rows, at, half),
    ]
    return rep, lax.axis_index("shard") % 2 == 0, up, both, [(side, sides)]


def far_kernel(reach_ref, prior_ref, low, across, high_0a, high_0b, high_1a, high_1b, high_2a,
               high_2b, high_3a, side_a, side_b, high_out, side_out):
    side = read_reach(side_a, 3)
    side_out[0], side_out[1] = side
    rep, even, up, both, sides = far_parts(reach_ref, side, low, across, side_a, side_b)
    high_out[...] = prior_ref[...]
    upper([(high_2b, 2, 1)], both, up, rep, high_out)
    pieces = [(high_0a, 0, 0), (high_0b, 0, 1), (high_1a, 1, 0), (high_1b, 1, 1), (high_2a, 2, 0)]
    pieces += [(high_2b, 2, 1), (high_3a, 3, 0)]
    upper(pieces, sides, up, rep, high_out, even)


def last_kernel(reach_ref, side_ref, prior_ref, low, across, high_3b, side_a, side_b, high_out):
    side = (side_ref[0], side_ref[1])
    rep, even, up, both, sides = far_parts(reach_ref, side, low, across, side_a, side_b)
    high_out[...] = prior_ref[...]
    upper([(high_3b, 3, 1)], both, up, rep, high_out)
    upper([(high_3b, 3, 1)], sides, up, rep, high_out, even)


def local(embeddings, labels):
    rows, width = embeddings.shape
    shards, reps = lax.axis_size("shard"), lax.axis_size("rep")
    quarter = rows // reps
    half = quarter // 2

    def along_shard(block, distance, keep=lambda i: True):
        route = [
            (i, i + distance) for i in range(shards) if i + distance in range(shards) and keep(i)
        ]
        return lax.ppermute(block, "shard", route)

    def partner(block):
        return lax.ppermute(block, "shard", [(i, i ^ 1) for i in range(shards)])

    def other_rep(block, flip):
        return lax.ppermute(block, "rep", [(i, i ^ flip) for i in range(reps)])

    def call(kernel, name, shapes, specs, *arrays):
        return pl.pallas_call(
            kernel,
            out_shape=[jax.ShapeDtypeStruct(shape, dtype) for shape, dtype in shapes],
            in_specs=specs[: len(arrays)],
            out_specs=specs[len(arrays) :],
            compiler_params=pltpu.CompilerParams(vmem_limit_bytes=VMEM_LIMIT),
            cost_estimate=pl.CostEstimate(flops=1024, bytes_accessed=1024, transcendentals=0),
            name=name,
        )(*arrays)

    sizes = [half, half + INFO, quarter + INFO]
    lo, hi, mine = pl.pallas_call(
        prepare_kernel,
        out_shape=[jax.ShapeDtypeStruct((size, width), BF16) for size in sizes],
        in_specs=[pl.BlockSpec(memory_space=pltpu.HBM)] * 2,
        out_specs=[VMEM] * 3,
        scratch_shapes=[
            pltpu.VMEM((2, half, width), BF16),
            pltpu.VMEM((rows // 128, 128), jnp.int32),
            pltpu.SemaphoreType.DMA((3,)),
        ],
        compiler_params=pltpu.CompilerParams(vmem_limit_bytes=PREPARE_LIMIT),
        name="prepare",
    )(embeddings, labels.reshape(rows // 128, 128))

    odd_only, even_only = (lambda i: i % 2 == 1), (lambda i: i % 2 == 0)
    fence = lax.optimization_barrier

    high_0a = along_shard(lo, -2)
    low = along_shard(mine, 2)
    across = partner(mine)
    high_0b = along_shard(hi, -2)

    high_0a, own_labels = fence((high_0a, labels))
    high_2a = other_rep(high_0a, 2)
    high_1a = other_rep(high_0a, 1)
    own, best, own_reach = pl.pallas_call(
        own_kernel,
        out_shape=[
            jax.ShapeDtypeStruct((rows, width), BF16),
            jax.ShapeDtypeStruct((1, rows), F32),
            jax.ShapeDtypeStruct((2,), jnp.int32),
        ],
        in_specs=[pl.BlockSpec(memory_space=pltpu.HBM), VMEM],
        out_specs=[VMEM, VMEM, SMEM],
        scratch_shapes=[
            pltpu.VMEM((8, rows), jnp.int32),
            pltpu.VMEM((4, quarter, width), BF16),
            pltpu.SemaphoreType.DMA((4,)),
        ],
        compiler_params=pltpu.CompilerParams(vmem_limit_bytes=OWN_LIMIT),
        cost_estimate=pl.CostEstimate(flops=1024, bytes_accessed=1024, transcendentals=0),
        name="own",
    )(embeddings, own_labels[None, :])

    across, low, own, best = fence((across, low, own, best))
    side_b = along_shard(across[:half], 2, even_only)
    side_a = along_shard(low[half:], -1, odd_only)
    high_0b, high_1a, high_2a, across, low = fence((high_0b, high_1a, high_2a, across, low))
    high_2b = other_rep(high_0b, 2)
    high_1b = other_rep(high_0b, 1)
    high_3a = other_rep(high_2a, 1)
    line = ((1, rows), F32)
    best, of_high, reach = call(
        near_kernel, "near", [line, line, ((6,), jnp.int32)],
        [SMEM] + [VMEM] * 10 + [SMEM],
        own_reach, own, best, low, across, high_0a, high_0b, high_1a, high_2a,
    )
    (of_high,) = call(
        middle_kernel, "middle", [line], [SMEM] + [VMEM] * 6,
        reach, of_high, low, across, high_1b, high_3a,
    )
    high_2b, side_a, side_b, of_high = fence((high_2b, side_a, side_b, of_high))
    high_3b = other_rep(high_2b, 1)
    of_high, side = call(
        far_kernel, "far", [line, ((2,), jnp.int32)], [SMEM] + [VMEM] * 13 + [SMEM],
        reach, of_high, low, across, high_0a, high_0b, high_1a, high_1b, high_2a, high_2b,
        high_3a, side_a, side_b,
    )
    (of_high,) = call(
        last_kernel, "last", [line], [SMEM] * 2 + [VMEM] * 7,
        reach, side, of_high, low, across, high_3b, side_a, side_b,
    )

    above = along_shard(of_high, 2)
    best = jnp.maximum(best, jnp.where(lax.axis_index("shard") >= 2, above, -1.0))
    others = [other_rep(best, flip) for flip in range(1, reps)]
    return functools.reduce(jnp.maximum, others, best)[0]


def solution(mesh):
    placed = (P("shard", None), P("shard"))
    return jax.shard_map(local, mesh=mesh, in_specs=placed, out_specs=P("shard"), check_vma=False)
```

```python
import functools
import math

import jax
import jax.numpy as jnp
from jax import lax
from jax.experimental import pallas as pl
from jax.experimental.pallas import tpu as pltpu
from jax.sharding import PartitionSpec as P

F32 = jnp.float32
BF16 = jnp.bfloat16
TILE = 256
WIDE = 512
INFO = 16
VMEM_LIMIT = 32 * 1024 * 1024
OWN_LIMIT = 46 * 1024 * 1024
PREPARE_LIMIT = 50 * 1024 * 1024
VMEM = pl.BlockSpec(memory_space=pltpu.VMEM)
SMEM = pl.BlockSpec(memory_space=pltpu.SMEM)


def normalize(values):
    as_float = values.astype(F32)
    width = values.shape[1]
    inverse = lax.rsqrt(jnp.sum(as_float * as_float, axis=1, keepdims=True) * (1 / width) + 1e-06)
    return (as_float * (inverse * (1 / math.sqrt(width)))).astype(BF16)


def score(keys, queries):
    return lax.dot_general(keys, queries, (((1,), (1,)), ((), ())), preferred_element_type=F32)


def fold(values):
    rows, cols = values.shape
    return jnp.max(values.reshape(rows // 8, 8, cols), axis=0)


def prepare_kernel(emb_ref, labels_hbm, lo_out, hi_out, mine_out, raw, labels_ref, sems):
    rep = lax.axis_index("rep")
    quarter = mine_out.shape[0] - INFO
    part = quarter // 2
    copies = []
    for n in range(2):
        at = pl.multiple_of(rep * quarter + n * part, part)
        copies.append(pltpu.make_async_copy(emb_ref.at[pl.ds(at, part), :], raw.at[n], sems.at[n]))
        copies[-1].start()
    fetch = pltpu.make_async_copy(labels_hbm, labels_ref, sems.at[2])
    fetch.start()
    fetch.wait()
    labels = labels_ref[...]
    first, last = jnp.min(labels), jnp.max(labels)
    head = jnp.sum((labels == first).astype(jnp.int32))
    tail = jnp.sum((labels == last).astype(jnp.int32))
    row = lax.broadcasted_iota(jnp.int32, (INFO, mine_out.shape[1]), 0)
    info = jnp.zeros(row.shape, jnp.int32)
    for n, value in enumerate([first, head // 16, head % 16, last, tail // 16, tail % 16]):
        info = jnp.where(row == n, value, info)
    info = info.astype(F32).astype(BF16)
    for n, copy in enumerate(copies):
        copy.wait()
        for m in range(part // 128):
            rows = pl.ds(m * 128, 128)
            values = normalize(raw[n, rows, :])
            mine_out[pl.ds(n * part + m * 128, 128), :] = values
            (lo_out, hi_out)[n][rows, :] = values
    hi_out[pl.ds(part, INFO), :] = info
    mine_out[pl.ds(quarter, INFO), :] = info


def read_reach(ref, at):
    block = ref[pl.ds(ref.shape[0] - INFO, INFO), pl.ds(0, 128)].astype(F32)
    packed = block[at : at + 1] + 256.0 * (16.0 * block[at + 1 : at + 2] + block[at + 2 : at + 3])
    packed = jnp.max(packed).astype(jnp.int32)
    return packed % 256, packed // 256


def group(keys, queries_ref, query_rows, out_ref, out_at, count):
    step = min(WIDE, query_rows)
    clear = functools.reduce(jnp.logical_and, [first <= 0 for *_, first in keys])
    trips = (count + step - 1) // step

    def over_queries(masked, j, _):
        at = pl.multiple_of(j * step, step)
        queries = queries_ref[pl.ds(at, step), :]
        best = None
        for ref, row, rows, first in keys:
            scores = score(ref[pl.ds(row, rows), :], queries)
            if masked:
                index = lax.broadcasted_iota(jnp.int32, scores.shape, 0)
                scores = jnp.where(index >= first, scores, -1.0)
            top = fold(scores)
            best = top if best is None else jnp.maximum(best, top)
        best = jnp.max(best, axis=0, keepdims=True)
        col = lax.broadcasted_iota(jnp.int32, best.shape, 1) + at
        cols = pl.ds(pl.multiple_of(out_at + at, TILE), step)
        out_ref[:, cols] = jnp.maximum(out_ref[:, cols], jnp.where(col < count, best, -1.0))
        return 0

    lax.fori_loop(0, jnp.where(clear, trips, 0), functools.partial(over_queries, False), 0)
    lax.fori_loop(0, jnp.where(clear, 0, trips), functools.partial(over_queries, True), 0)


def own_kernel(emb_ref, labels_ref, own_out, best_out, reach_out, start, raw, sems):
    rows = emb_ref.shape[0]
    rep = lax.axis_index("rep")
    parts = raw.shape[0]
    size = rows // parts
    copies = [
        pltpu.make_async_copy(emb_ref.at[pl.ds(n * size, size), :], raw.at[n], sems.at[n])
        for n in range(parts)
    ]
    for copy in copies:
        copy.start()
    labels = jnp.broadcast_to(labels_ref[...], start.shape)
    first = jnp.min(labels)
    reach_out[0] = first
    reach_out[1] = jnp.sum((labels == first).astype(jnp.int32)) // start.shape[0]
    lane = lax.broadcasted_iota(jnp.int32, labels.shape, 1)
    begin = jnp.where((lane == 0) | (labels != pltpu.roll(labels, 1, 1)), lane, 0)
    shift = 1
    while shift < rows:
        begin = jnp.maximum(begin, jnp.where(lane >= shift, pltpu.roll(begin, shift, 1), 0))
        shift *= 2
    start[...] = begin
    best_out[...] = jnp.full(best_out.shape, -1.0, F32)
    for n, copy in enumerate(copies):
        copy.wait()
        for m in range(size // 128):
            values = normalize(raw[n, pl.ds(m * 128, 128), :])
            own_out[pl.ds(n * size + m * 128, 128), :] = values
    for n in range(2):
        tile = rep if n == 0 else rows // TILE - 1 - rep
        at = pl.multiple_of(tile * TILE, TILE)
        keys = own_out[pl.ds(at, TILE), :]

        def over_queries(j, _):
            cols = pl.ds(pl.multiple_of(j * WIDE, WIDE), WIDE)
            scores = score(keys, own_out[cols, :])
            row = lax.broadcasted_iota(jnp.int32, scores.shape, 0) + at
            col = lax.broadcasted_iota(jnp.int32, scores.shape, 1) + j * WIDE
            keep = (row >= start[0:1, cols]) & (row < col)
            best = jnp.max(fold(jnp.where(keep, scores, -1.0)), axis=0, keepdims=True)
            best_out[:, cols] = jnp.maximum(best_out[:, cols], best)
            return 0

        lax.fori_loop(at // WIDE, rows // WIDE, over_queries, 0)


def reached(query, key, offset, limit):
    count = jnp.clip(query[1] - offset, 0, limit)
    return jnp.where(query[0] == key[0], count, 0)


def key_piece(ref, tail, rows, at, size):
    return (ref, 0, size, jnp.clip(rows - tail - at, 0, size))


def upper(pieces, keys, up, rep, out_ref, enabled=True):
    half = TILE
    for ref, flip, part in pieces:
        at = (rep ^ flip) * 2 * half + part * half
        for last, several in keys:
            count = jnp.where(enabled, reached(up, last, at, half), 0)
            group(several, ref, half, out_ref, at, count)


def near_kernel(own_reach, own_ref, best_ref, low, across, high_0a, high_0b, high_1a, high_2a,
                best_out, high_out, reach_out):
    rows = own_ref.shape[0]
    quarter = across.shape[0] - INFO
    rep, odd = lax.axis_index("rep"), lax.axis_index("shard") % 2
    mine = (own_reach[0], own_reach[1])
    lower, beside, up = read_reach(low, 3), read_reach(across, 3), read_reach(high_0b, 0)
    for n, value in enumerate(lower + beside + up):
        reach_out[n] = value
    best_out[...] = best_ref[...]
    high_out[...] = jnp.full(high_out.shape, -1.0, F32)
    lows = [key_piece(low, lower[1], rows, rep * quarter, quarter)]
    besides = [key_piece(across, beside[1], rows, rep * quarter, quarter)]
    group(lows, own_ref, rows, best_out, 0, reached(mine, lower, 0, rows))
    count = jnp.where(odd == 1, reached(mine, beside, 0, rows), 0)
    group(besides, own_ref, rows, best_out, 0, count)
    pieces = [(high_0a, 0, 0), (high_0b, 0, 1), (high_1a, 1, 0), (high_2a, 2, 0)]
    upper(pieces, [(beside, besides), (lower, lows)], up, rep, high_out)


def both_keys(reach_ref, low, across):
    quarter, rows = 2 * TILE, 8 * TILE
    rep = lax.axis_index("rep")
    lower, beside, up = [(reach_ref[2 * n], reach_ref[2 * n + 1]) for n in range(3)]
    at = rep * quarter
    both = [
        (beside, [key_piece(across, beside[1], rows, at, quarter)]),
        (lower, [key_piece(low, lower[1], rows, at, quarter)]),
    ]
    return rep, up, both


def middle_kernel(reach_ref, prior_ref, low, across, high_1b, high_3a, high_out):
    rep, up, both = both_keys(reach_ref, low, across)
    high_out[...] = prior_ref[...]
    upper([(high_1b, 1, 1), (high_3a, 3, 0)], both, up, rep, high_out)


def side_keys(side, sides_ref):
    quarter, rows = 2 * TILE, 8 * TILE
    at = lax.axis_index("rep") * quarter
    return [(side, [key_piece(sides_ref, side[1], rows, at, quarter)])]


def far_kernel(reach_ref, prior_ref, low, across, high_0a, high_0b, high_1a, high_1b, high_2a,
               high_2b, high_3a, side_a, side_b, high_out, side_out, sides_out):
    half = TILE
    even = lax.axis_index("shard") % 2 == 0
    side = read_reach(side_a, 3)
    side_out[0], side_out[1] = side

    @pl.when(even)
    def _():
        sides_out[pl.ds(0, half), :] = side_b[pl.ds(0, half), :]
        sides_out[pl.ds(half, half), :] = side_a[pl.ds(0, half), :]

    rep, up, both = both_keys(reach_ref, low, across)
    high_out[...] = prior_ref[...]
    upper([(high_2b, 2, 1)], both, up, rep, high_out)
    pieces = [(high_0a, 0, 0), (high_0b, 0, 1), (high_1a, 1, 0), (high_1b, 1, 1), (high_2a, 2, 0)]
    pieces += [(high_2b, 2, 1), (high_3a, 3, 0)]
    upper(pieces, side_keys(side, sides_out), up, rep, high_out, even)


def last_kernel(reach_ref, side_ref, prior_ref, low, across, high_3b, sides, high_out):
    side = (side_ref[0], side_ref[1])
    even = lax.axis_index("shard") % 2 == 0
    rep, up, both = both_keys(reach_ref, low, across)
    high_out[...] = prior_ref[...]
    upper([(high_3b, 3, 1)], both, up, rep, high_out)
    upper([(high_3b, 3, 1)], side_keys(side, sides), up, rep, high_out, even)


def local(embeddings, labels):
    rows, width = embeddings.shape
    shards, reps = lax.axis_size("shard"), lax.axis_size("rep")
    quarter = rows // reps
    half = quarter // 2

    def along_shard(block, distance, keep=lambda i: True):
        route = [
            (i, i + distance) for i in range(shards) if i + distance in range(shards) and keep(i)
        ]
        return lax.ppermute(block, "shard", route)

    def partner(block):
        return lax.ppermute(block, "shard", [(i, i ^ 1) for i in range(shards)])

    def other_rep(block, flip):
        return lax.ppermute(block, "rep", [(i, i ^ flip) for i in range(reps)])

    def call(kernel, name, shapes, specs, *arrays):
        return pl.pallas_call(
            kernel,
            out_shape=[jax.ShapeDtypeStruct(shape, dtype) for shape, dtype in shapes],
            in_specs=specs[: len(arrays)],
            out_specs=specs[len(arrays) :],
            compiler_params=pltpu.CompilerParams(vmem_limit_bytes=VMEM_LIMIT),
            cost_estimate=pl.CostEstimate(flops=1024, bytes_accessed=1024, transcendentals=0),
            name=name,
        )(*arrays)

    sizes = [half, half + INFO, quarter + INFO]
    lo, hi, mine = pl.pallas_call(
        prepare_kernel,
        out_shape=[jax.ShapeDtypeStruct((size, width), BF16) for size in sizes],
        in_specs=[pl.BlockSpec(memory_space=pltpu.HBM)] * 2,
        out_specs=[VMEM] * 3,
        scratch_shapes=[
            pltpu.VMEM((2, half, width), BF16),
            pltpu.VMEM((rows // 128, 128), jnp.int32),
            pltpu.SemaphoreType.DMA((3,)),
        ],
        compiler_params=pltpu.CompilerParams(vmem_limit_bytes=PREPARE_LIMIT),
        name="prepare",
    )(embeddings, labels.reshape(rows // 128, 128))

    odd_only, even_only = (lambda i: i % 2 == 1), (lambda i: i % 2 == 0)
    fence = lax.optimization_barrier

    high_0a = along_shard(lo, -2)
    low = along_shard(mine, 2)
    across = partner(mine)
    high_0b = along_shard(hi, -2)

    high_0a, own_labels = fence((high_0a, labels))
    high_2a = other_rep(high_0a, 2)
    high_1a = other_rep(high_0a, 1)
    own, best, own_reach = pl.pallas_call(
        own_kernel,
        out_shape=[
            jax.ShapeDtypeStruct((rows, width), BF16),
            jax.ShapeDtypeStruct((1, rows), F32),
            jax.ShapeDtypeStruct((2,), jnp.int32),
        ],
        in_specs=[pl.BlockSpec(memory_space=pltpu.HBM), VMEM],
        out_specs=[VMEM, VMEM, SMEM],
        scratch_shapes=[
            pltpu.VMEM((8, rows), jnp.int32),
            pltpu.VMEM((4, quarter, width), BF16),
            pltpu.SemaphoreType.DMA((4,)),
        ],
        compiler_params=pltpu.CompilerParams(vmem_limit_bytes=OWN_LIMIT),
        cost_estimate=pl.CostEstimate(flops=1024, bytes_accessed=1024, transcendentals=0),
        name="own",
    )(embeddings, own_labels[None, :])

    across, low, own, best = fence((across, low, own, best))
    side_b = along_shard(across[: half + INFO], 2, even_only)
    side_a = along_shard(low[half:], -1, odd_only)
    high_0b, high_1a, high_2a, across, low = fence((high_0b, high_1a, high_2a, across, low))
    high_2b = other_rep(high_0b, 2)
    high_1b = other_rep(high_0b[:half], 1)
    high_3a = other_rep(high_2a, 1)
    line = ((1, rows), F32)
    best, of_high, reach = call(
        near_kernel, "near", [line, line, ((6,), jnp.int32)],
        [SMEM] + [VMEM] * 10 + [SMEM],
        own_reach, own, best, low, across, high_0a, high_0b, high_1a, high_2a,
    )
    (of_high,) = call(
        middle_kernel, "middle", [line], [SMEM] + [VMEM] * 6,
        reach, of_high, low, across, high_1b, high_3a,
    )
    high_2b, side_a, side_b, of_high = fence((high_2b, side_a, side_b, of_high))
    high_3b = other_rep(high_2b, 1)
    of_high, side, sides = call(
        far_kernel, "far", [line, ((2,), jnp.int32), ((quarter, width), BF16)],
        [SMEM] + [VMEM] * 13 + [SMEM, VMEM],
        reach, of_high, low, across, high_0a, high_0b, high_1a, high_1b, high_2a, high_2b,
        high_3a, side_a, side_b,
    )
    (of_high,) = call(
        last_kernel, "last", [line], [SMEM] * 2 + [VMEM] * 6,
        reach, side, of_high, low, across, high_3b, sides,
    )

    above = along_shard(of_high, 2)
    best = jnp.maximum(best, jnp.where(lax.axis_index("shard") >= 2, above, -1.0))
    others = [other_rep(best, flip) for flip in range(1, reps)]
    return functools.reduce(jnp.maximum, others, best)[0]


def solution(mesh):
    placed = (P("shard", None), P("shard"))
    return jax.shard_map(local, mesh=mesh, in_specs=placed, out_specs=P("shard"), check_vma=False)
```

```python
import functools
import math

import jax
import jax.numpy as jnp
from jax import lax
from jax.experimental import pallas as pl
from jax.experimental.pallas import tpu as pltpu
from jax.sharding import PartitionSpec as P

F32 = jnp.float32
BF16 = jnp.bfloat16
TILE = 256
WIDE = 512
INFO = 16
VMEM_LIMIT = 32 * 1024 * 1024
OWN_LIMIT = 46 * 1024 * 1024
PREPARE_LIMIT = 50 * 1024 * 1024
VMEM = pl.BlockSpec(memory_space=pltpu.VMEM)
SMEM = pl.BlockSpec(memory_space=pltpu.SMEM)


def normalize(values):
    as_float = values.astype(F32)
    width = values.shape[1]
    inverse = lax.rsqrt(jnp.sum(as_float * as_float, axis=1, keepdims=True) * (1 / width) + 1e-06)
    return (as_float * (inverse * (1 / math.sqrt(width)))).astype(BF16)


def score(keys, queries):
    return lax.dot_general(keys, queries, (((1,), (1,)), ((), ())), preferred_element_type=F32)


def fold(values):
    rows, cols = values.shape
    return jnp.max(values.reshape(rows // 8, 8, cols), axis=0)


def prepare_kernel(emb_ref, labels_hbm, lo_out, hi_out, mine_out, raw, labels_ref, sems):
    rep = lax.axis_index("rep")
    quarter = mine_out.shape[0] - INFO
    part = quarter // 2
    copies = []
    for n in range(2):
        at = pl.multiple_of(rep * quarter + n * part, part)
        copies.append(pltpu.make_async_copy(emb_ref.at[pl.ds(at, part), :], raw.at[n], sems.at[n]))
        copies[-1].start()
    fetch = pltpu.make_async_copy(labels_hbm, labels_ref, sems.at[2])
    fetch.start()
    fetch.wait()
    labels = labels_ref[...]
    first, last = jnp.min(labels), jnp.max(labels)
    head = jnp.sum((labels == first).astype(jnp.int32))
    tail = jnp.sum((labels == last).astype(jnp.int32))
    row = lax.broadcasted_iota(jnp.int32, (INFO, mine_out.shape[1]), 0)
    info = jnp.zeros(row.shape, jnp.int32)
    for n, value in enumerate([first, head // 16, head % 16, last, tail // 16, tail % 16]):
        info = jnp.where(row == n, value, info)
    info = info.astype(F32).astype(BF16)
    for n, copy in enumerate(copies):
        copy.wait()
        for m in range(part // 128):
            rows = pl.ds(m * 128, 128)
            values = normalize(raw[n, rows, :])
            mine_out[pl.ds(n * part + m * 128, 128), :] = values
            (lo_out, hi_out)[n][rows, :] = values
    hi_out[pl.ds(part, INFO), :] = info
    mine_out[pl.ds(quarter, INFO), :] = info


def read_reach(ref, at):
    block = ref[pl.ds(ref.shape[0] - INFO, INFO), pl.ds(0, 128)].astype(F32)
    packed = block[at : at + 1] + 256.0 * (16.0 * block[at + 1 : at + 2] + block[at + 2 : at + 3])
    packed = jnp.max(packed).astype(jnp.int32)
    return packed % 256, packed // 256


def group(keys, queries_ref, query_rows, out_ref, out_at, count):
    step = min(WIDE, query_rows)
    clear = functools.reduce(jnp.logical_and, [first <= 0 for *_, first in keys])
    trips = (count + step - 1) // step

    def over_queries(masked, j, _):
        at = pl.multiple_of(j * step, step)
        queries = queries_ref[pl.ds(at, step), :]
        best = None
        for ref, row, rows, first in keys:
            scores = score(ref[pl.ds(row, rows), :], queries)
            if masked:
                index = lax.broadcasted_iota(jnp.int32, scores.shape, 0)
                scores = jnp.where(index >= first, scores, -1.0)
            top = fold(scores)
            best = top if best is None else jnp.maximum(best, top)
        best = jnp.max(best, axis=0, keepdims=True)
        col = lax.broadcasted_iota(jnp.int32, best.shape, 1) + at
        cols = pl.ds(pl.multiple_of(out_at + at, TILE), step)
        out_ref[:, cols] = jnp.maximum(out_ref[:, cols], jnp.where(col < count, best, -1.0))
        return 0

    lax.fori_loop(0, jnp.where(clear, trips, 0), functools.partial(over_queries, False), 0)
    lax.fori_loop(0, jnp.where(clear, 0, trips), functools.partial(over_queries, True), 0)


def own_kernel(emb_ref, labels_ref, own_out, best_out, reach_out, start, raw, sems):
    rows = emb_ref.shape[0]
    rep = lax.axis_index("rep")
    parts = raw.shape[0]
    size = rows // parts
    copies = [
        pltpu.make_async_copy(emb_ref.at[pl.ds(n * size, size), :], raw.at[n], sems.at[n])
        for n in range(parts)
    ]
    for copy in copies:
        copy.start()
    labels = jnp.broadcast_to(labels_ref[...], start.shape)
    first = jnp.min(labels)
    reach_out[0] = first
    reach_out[1] = jnp.sum((labels == first).astype(jnp.int32)) // start.shape[0]
    lane = lax.broadcasted_iota(jnp.int32, labels.shape, 1)
    begin = jnp.where((lane == 0) | (labels != pltpu.roll(labels, 1, 1)), lane, 0)
    shift = 1
    while shift < rows:
        begin = jnp.maximum(begin, jnp.where(lane >= shift, pltpu.roll(begin, shift, 1), 0))
        shift *= 2
    start[...] = begin
    best_out[...] = jnp.full(best_out.shape, -1.0, F32)
    for n, copy in enumerate(copies):
        copy.wait()
        for m in range(size // 128):
            values = normalize(raw[n, pl.ds(m * 128, 128), :])
            own_out[pl.ds(n * size + m * 128, 128), :] = values
    for n in range(2):
        tile = rep if n == 0 else rows // TILE - 1 - rep
        at = pl.multiple_of(tile * TILE, TILE)
        keys = own_out[pl.ds(at, TILE), :]

        def over_queries(j, _):
            cols = pl.ds(pl.multiple_of(j * WIDE, WIDE), WIDE)
            scores = score(keys, own_out[cols, :])
            row = lax.broadcasted_iota(jnp.int32, scores.shape, 0) + at
            col = lax.broadcasted_iota(jnp.int32, scores.shape, 1) + j * WIDE
            keep = (row >= start[0:1, cols]) & (row < col)
            best = jnp.max(fold(jnp.where(keep, scores, -1.0)), axis=0, keepdims=True)
            best_out[:, cols] = jnp.maximum(best_out[:, cols], best)
            return 0

        lax.fori_loop(at // WIDE, rows // WIDE, over_queries, 0)


def reached(query, key, offset, limit):
    count = jnp.clip(query[1] - offset, 0, limit)
    return jnp.where(query[0] == key[0], count, 0)


def key_piece(ref, tail, rows, at, size):
    return (ref, 0, size, jnp.clip(rows - tail - at, 0, size))


def upper(pieces, keys, up, rep, out_ref, enabled=True):
    half = TILE
    for ref, flip, part in pieces:
        at = (rep ^ flip) * 2 * half + part * half
        for last, several in keys:
            count = jnp.where(enabled, reached(up, last, at, half), 0)
            group(several, ref, half, out_ref, at, count)


def lower_kernel(own_reach, own_ref, best_ref, low, best_out, lower_out):
    rows = own_ref.shape[0]
    quarter = low.shape[0] - INFO
    lower = read_reach(low, 3)
    lower_out[0], lower_out[1] = lower
    best_out[...] = best_ref[...]
    lows = [key_piece(low, lower[1], rows, lax.axis_index("rep") * quarter, quarter)]
    mine = (own_reach[0], own_reach[1])
    group(lows, own_ref, rows, best_out, 0, reached(mine, lower, 0, rows))


def near_kernel(own_reach, lower_reach, own_ref, best_ref, low, across, high_0a, high_0b, high_1a,
                high_2a, best_out, high_out, reach_out):
    rows = own_ref.shape[0]
    quarter = across.shape[0] - INFO
    rep, odd = lax.axis_index("rep"), lax.axis_index("shard") % 2
    mine = (own_reach[0], own_reach[1])
    lower = (lower_reach[0], lower_reach[1])
    beside, up = read_reach(across, 3), read_reach(high_0b, 0)
    for n, value in enumerate(lower + beside + up):
        reach_out[n] = value
    best_out[...] = best_ref[...]
    high_out[...] = jnp.full(high_out.shape, -1.0, F32)
    lows = [key_piece(low, lower[1], rows, rep * quarter, quarter)]
    besides = [key_piece(across, beside[1], rows, rep * quarter, quarter)]
    count = jnp.where(odd == 1, reached(mine, beside, 0, rows), 0)
    group(besides, own_ref, rows, best_out, 0, count)
    pieces = [(high_0a, 0, 0), (high_0b, 0, 1), (high_1a, 1, 0), (high_2a, 2, 0)]
    upper(pieces, [(beside, besides), (lower, lows)], up, rep, high_out)


def both_keys(reach_ref, low, across):
    quarter, rows = 2 * TILE, 8 * TILE
    rep = lax.axis_index("rep")
    lower, beside, up = [(reach_ref[2 * n], reach_ref[2 * n + 1]) for n in range(3)]
    at = rep * quarter
    both = [
        (beside, [key_piece(across, beside[1], rows, at, quarter)]),
        (lower, [key_piece(low, lower[1], rows, at, quarter)]),
    ]
    return rep, up, both


def middle_kernel(reach_ref, prior_ref, low, across, high_1b, high_3a, high_out):
    rep, up, both = both_keys(reach_ref, low, across)
    high_out[...] = prior_ref[...]
    upper([(high_1b, 1, 1), (high_3a, 3, 0)], both, up, rep, high_out)


def side_keys(side, sides_ref):
    quarter, rows = 2 * TILE, 8 * TILE
    at = lax.axis_index("rep") * quarter
    return [(side, [key_piece(sides_ref, side[1], rows, at, quarter)])]


def far_kernel(reach_ref, prior_ref, low, across, high_0a, high_0b, high_1a, high_1b, high_2a,
               high_2b, high_3a, side_a, side_b, high_out, side_out, sides_out):
    half = TILE
    even = lax.axis_index("shard") % 2 == 0
    side = read_reach(side_a, 3)
    side_out[0], side_out[1] = side

    @pl.when(even)
    def _():
        sides_out[pl.ds(0, half), :] = side_b[pl.ds(0, half), :]
        sides_out[pl.ds(half, half), :] = side_a[pl.ds(0, half), :]

    rep, up, both = both_keys(reach_ref, low, across)
    high_out[...] = prior_ref[...]
    upper([(high_2b, 2, 1)], both, up, rep, high_out)
    pieces = [(high_0a, 0, 0), (high_0b, 0, 1), (high_1a, 1, 0), (high_1b, 1, 1), (high_2a, 2, 0)]
    pieces += [(high_2b, 2, 1), (high_3a, 3, 0)]
    upper(pieces, side_keys(side, sides_out), up, rep, high_out, even)


def last_kernel(reach_ref, side_ref, prior_ref, low, across, high_3b, sides, high_out):
    side = (side_ref[0], side_ref[1])
    even = lax.axis_index("shard") % 2 == 0
    rep, up, both = both_keys(reach_ref, low, across)
    high_out[...] = prior_ref[...]
    upper([(high_3b, 3, 1)], both, up, rep, high_out)
    upper([(high_3b, 3, 1)], side_keys(side, sides), up, rep, high_out, even)


def local(embeddings, labels):
    rows, width = embeddings.shape
    shards, reps = lax.axis_size("shard"), lax.axis_size("rep")
    quarter = rows // reps
    half = quarter // 2

    def along_shard(block, distance, keep=lambda i: True):
        route = [
            (i, i + distance) for i in range(shards) if i + distance in range(shards) and keep(i)
        ]
        return lax.ppermute(block, "shard", route)

    def partner(block):
        return lax.ppermute(block, "shard", [(i, i ^ 1) for i in range(shards)])

    def other_rep(block, flip):
        return lax.ppermute(block, "rep", [(i, i ^ flip) for i in range(reps)])

    def call(kernel, name, shapes, specs, *arrays):
        return pl.pallas_call(
            kernel,
            out_shape=[jax.ShapeDtypeStruct(shape, dtype) for shape, dtype in shapes],
            in_specs=specs[: len(arrays)],
            out_specs=specs[len(arrays) :],
            compiler_params=pltpu.CompilerParams(vmem_limit_bytes=VMEM_LIMIT),
            cost_estimate=pl.CostEstimate(flops=1024, bytes_accessed=1024, transcendentals=0),
            name=name,
        )(*arrays)

    sizes = [half, half + INFO, quarter + INFO]
    lo, hi, mine = pl.pallas_call(
        prepare_kernel,
        out_shape=[jax.ShapeDtypeStruct((size, width), BF16) for size in sizes],
        in_specs=[pl.BlockSpec(memory_space=pltpu.HBM)] * 2,
        out_specs=[VMEM] * 3,
        scratch_shapes=[
            pltpu.VMEM((2, half, width), BF16),
            pltpu.VMEM((rows // 128, 128), jnp.int32),
            pltpu.SemaphoreType.DMA((3,)),
        ],
        compiler_params=pltpu.CompilerParams(vmem_limit_bytes=PREPARE_LIMIT),
        name="prepare",
    )(embeddings, labels.reshape(rows // 128, 128))

    odd_only, even_only = (lambda i: i % 2 == 1), (lambda i: i % 2 == 0)
    fence = lax.optimization_barrier

    high_0a = along_shard(lo, -2)
    low = along_shard(mine, 2)
    across = partner(mine)
    high_0b = along_shard(hi, -2)

    own, best, own_reach = pl.pallas_call(
        own_kernel,
        out_shape=[
            jax.ShapeDtypeStruct((rows, width), BF16),
            jax.ShapeDtypeStruct((1, rows), F32),
            jax.ShapeDtypeStruct((2,), jnp.int32),
        ],
        in_specs=[pl.BlockSpec(memory_space=pltpu.HBM), VMEM],
        out_specs=[VMEM, VMEM, SMEM],
        scratch_shapes=[
            pltpu.VMEM((8, rows), jnp.int32),
            pltpu.VMEM((4, quarter, width), BF16),
            pltpu.SemaphoreType.DMA((4,)),
        ],
        compiler_params=pltpu.CompilerParams(vmem_limit_bytes=OWN_LIMIT),
        cost_estimate=pl.CostEstimate(flops=1024, bytes_accessed=1024, transcendentals=0),
        name="own",
    )(embeddings, labels[None, :])

    high_0a, own, best = fence((high_0a, own, best))
    high_2a = other_rep(high_0a, 2)
    high_1a = other_rep(high_0a, 1)
    line = ((1, rows), F32)
    best, lower_reach = call(
        lower_kernel, "lower", [line, ((2,), jnp.int32)], [SMEM] + [VMEM] * 4 + [SMEM],
        own_reach, own, best, low,
    )

    across, low, best = fence((across, low, best))
    side_b = along_shard(across[: half + INFO], 2, even_only)
    side_a = along_shard(low[half:], -1, odd_only)
    high_0b, high_1a, high_2a, across, low = fence((high_0b, high_1a, high_2a, across, low))
    high_2b = other_rep(high_0b, 2)
    high_1b = other_rep(high_0b[:half], 1)
    high_3a = other_rep(high_2a, 1)
    best, of_high, reach = call(
        near_kernel, "near", [line, line, ((6,), jnp.int32)],
        [SMEM] * 2 + [VMEM] * 10 + [SMEM],
        own_reach, lower_reach, own, best, low, across, high_0a, high_0b, high_1a, high_2a,
    )
    best_1 = other_rep(best, 1)
    (of_high,) = call(
        middle_kernel, "middle", [line], [SMEM] + [VMEM] * 6,
        reach, of_high, low, across, high_1b, high_3a,
    )
    high_2b, side_a, side_b, of_high, best_1 = fence((high_2b, side_a, side_b, of_high, best_1))
    high_3b = other_rep(high_2b, 1)
    of_high, side, sides = call(
        far_kernel, "far", [line, ((2,), jnp.int32), ((quarter, width), BF16)],
        [SMEM] + [VMEM] * 13 + [SMEM, VMEM],
        reach, of_high, low, across, high_0a, high_0b, high_1a, high_1b, high_2a, high_2b,
        high_3a, side_a, side_b,
    )
    (of_high,) = call(
        last_kernel, "last", [line], [SMEM] * 2 + [VMEM] * 6,
        reach, side, of_high, low, across, high_3b, sides,
    )

    above = along_shard(of_high, 2)
    route = [
        (i * reps + j, (i + 2) * reps + (j ^ 1)) for i in range(shards - 2) for j in range(reps)
    ]
    above = jnp.maximum(above, lax.ppermute(of_high, ("shard", "rep"), route))
    above = jnp.where(lax.axis_index("shard") >= 2, above, -1.0)
    best = jnp.maximum(jnp.maximum(best, best_1), above)
    return jnp.maximum(best, other_rep(best, 2))[0]


def solution(mesh):
    placed = (P("shard", None), P("shard"))
    return jax.shard_map(local, mesh=mesh, in_specs=placed, out_specs=P("shard"), check_vma=False)
```

```python
import functools
import math

import jax
import jax.numpy as jnp
from jax import lax
from jax.experimental import pallas as pl
from jax.experimental.pallas import tpu as pltpu
from jax.sharding import PartitionSpec as P

F32 = jnp.float32
BF16 = jnp.bfloat16
TILE = 256
WIDE = 512
INFO = 16
VMEM_LIMIT = 32 * 1024 * 1024
OWN_LIMIT = 46 * 1024 * 1024
PREPARE_LIMIT = 50 * 1024 * 1024
VMEM = pl.BlockSpec(memory_space=pltpu.VMEM)
SMEM = pl.BlockSpec(memory_space=pltpu.SMEM)


def normalize(values):
    as_float = values.astype(F32)
    width = values.shape[1]
    inverse = lax.rsqrt(jnp.sum(as_float * as_float, axis=1, keepdims=True) * (1 / width) + 1e-06)
    return (as_float * (inverse * (1 / math.sqrt(width)))).astype(BF16)


def score(keys, queries):
    return lax.dot_general(keys, queries, (((1,), (1,)), ((), ())), preferred_element_type=F32)


def fold(values):
    rows, cols = values.shape
    return jnp.max(values.reshape(rows // 8, 8, cols), axis=0)


def prepare_kernel(emb_ref, labels_hbm, lo_out, hi_out, mine_out, raw, labels_ref, sems):
    rep = lax.axis_index("rep")
    quarter = mine_out.shape[0] - INFO
    part = quarter // 2
    copies = []
    for n in range(2):
        at = pl.multiple_of(rep * quarter + n * part, part)
        copies.append(pltpu.make_async_copy(emb_ref.at[pl.ds(at, part), :], raw.at[n], sems.at[n]))
        copies[-1].start()
    fetch = pltpu.make_async_copy(labels_hbm, labels_ref, sems.at[2])
    fetch.start()
    fetch.wait()
    labels = labels_ref[...]
    first, last = jnp.min(labels), jnp.max(labels)
    head = jnp.sum((labels == first).astype(jnp.int32))
    tail = jnp.sum((labels == last).astype(jnp.int32))
    row = lax.broadcasted_iota(jnp.int32, (INFO, mine_out.shape[1]), 0)
    info = jnp.zeros(row.shape, jnp.int32)
    for n, value in enumerate([first, head // 16, head % 16, last, tail // 16, tail % 16]):
        info = jnp.where(row == n, value, info)
    info = info.astype(F32).astype(BF16)
    for n, copy in enumerate(copies):
        copy.wait()
        for m in range(part // 128):
            rows = pl.ds(m * 128, 128)
            values = normalize(raw[n, rows, :])
            mine_out[pl.ds(n * part + m * 128, 128), :] = values
            (lo_out, hi_out)[n][rows, :] = values
    hi_out[pl.ds(part, INFO), :] = info
    mine_out[pl.ds(quarter, INFO), :] = info


def read_reach(ref, at):
    block = ref[pl.ds(ref.shape[0] - INFO, INFO), pl.ds(0, 128)].astype(F32)
    packed = block[at : at + 1] + 256.0 * (16.0 * block[at + 1 : at + 2] + block[at + 2 : at + 3])
    packed = jnp.max(packed).astype(jnp.int32)
    return packed % 256, packed // 256


def group(keys, queries_ref, query_rows, out_ref, out_at, count):
    step = min(WIDE, query_rows)
    clear = functools.reduce(jnp.logical_and, [first <= 0 for *_, first in keys])
    trips = (count + step - 1) // step

    def over_queries(masked, j, _):
        at = pl.multiple_of(j * step, step)
        queries = queries_ref[pl.ds(at, step), :]
        best = None
        for ref, row, rows, first in keys:
            scores = score(ref[pl.ds(row, rows), :], queries)
            if masked:
                index = lax.broadcasted_iota(jnp.int32, scores.shape, 0)
                scores = jnp.where(index >= first, scores, -1.0)
            top = fold(scores)
            best = top if best is None else jnp.maximum(best, top)
        best = jnp.max(best, axis=0, keepdims=True)
        col = lax.broadcasted_iota(jnp.int32, best.shape, 1) + at
        cols = pl.ds(pl.multiple_of(out_at + at, TILE), step)
        out_ref[:, cols] = jnp.maximum(out_ref[:, cols], jnp.where(col < count, best, -1.0))
        return 0

    lax.fori_loop(0, jnp.where(clear, trips, 0), functools.partial(over_queries, False), 0)
    lax.fori_loop(0, jnp.where(clear, 0, trips), functools.partial(over_queries, True), 0)


def own_kernel(emb_ref, labels_ref, own_out, best_out, reach_out, start, raw, sems):
    rows = emb_ref.shape[0]
    rep = lax.axis_index("rep")
    parts = raw.shape[0]
    size = rows // parts
    copies = [
        pltpu.make_async_copy(emb_ref.at[pl.ds(n * size, size), :], raw.at[n], sems.at[n])
        for n in range(parts)
    ]
    for copy in copies:
        copy.start()
    labels = jnp.broadcast_to(labels_ref[...], start.shape)
    first = jnp.min(labels)
    reach_out[0] = first
    reach_out[1] = jnp.sum((labels == first).astype(jnp.int32)) // start.shape[0]
    lane = lax.broadcasted_iota(jnp.int32, labels.shape, 1)
    begin = jnp.where((lane == 0) | (labels != pltpu.roll(labels, 1, 1)), lane, 0)
    shift = 1
    while shift < rows:
        begin = jnp.maximum(begin, jnp.where(lane >= shift, pltpu.roll(begin, shift, 1), 0))
        shift *= 2
    start[...] = begin
    best_out[...] = jnp.full(best_out.shape, -1.0, F32)
    for n, copy in enumerate(copies):
        copy.wait()
        for m in range(size // 128):
            values = normalize(raw[n, pl.ds(m * 128, 128), :])
            own_out[pl.ds(n * size + m * 128, 128), :] = values
    for n in range(2):
        tile = rep if n == 0 else rows // TILE - 1 - rep
        at = pl.multiple_of(tile * TILE, TILE)
        keys = own_out[pl.ds(at, TILE), :]

        def over_queries(j, _):
            cols = pl.ds(pl.multiple_of(j * WIDE, WIDE), WIDE)
            scores = score(keys, own_out[cols, :])
            row = lax.broadcasted_iota(jnp.int32, scores.shape, 0) + at
            col = lax.broadcasted_iota(jnp.int32, scores.shape, 1) + j * WIDE
            keep = (row >= start[0:1, cols]) & (row < col)
            best = jnp.max(fold(jnp.where(keep, scores, -1.0)), axis=0, keepdims=True)
            best_out[:, cols] = jnp.maximum(best_out[:, cols], best)
            return 0

        lax.fori_loop(at // WIDE, rows // WIDE, over_queries, 0)


def reached(query, key, offset, limit):
    count = jnp.clip(query[1] - offset, 0, limit)
    return jnp.where(query[0] == key[0], count, 0)


def key_piece(ref, tail, rows, at, size):
    return (ref, 0, size, jnp.clip(rows - tail - at, 0, size))


def upper(pieces, keys, up, rep, out_ref, enabled=True):
    half = TILE
    for ref, flip, part in pieces:
        at = (rep ^ flip) * 2 * half + part * half
        for last, several in keys:
            count = jnp.where(enabled, reached(up, last, at, half), 0)
            group(several, ref, half, out_ref, at, count)


def lower_kernel(own_reach, own_ref, best_ref, low, best_out, lower_out):
    rows = own_ref.shape[0]
    quarter = low.shape[0] - INFO
    lower = read_reach(low, 3)
    lower_out[0], lower_out[1] = lower
    best_out[...] = best_ref[...]
    lows = [key_piece(low, lower[1], rows, lax.axis_index("rep") * quarter, quarter)]
    mine = (own_reach[0], own_reach[1])
    group(lows, own_ref, rows, best_out, 0, reached(mine, lower, 0, rows))


def near_kernel(own_reach, lower_reach, own_ref, best_ref, low, across, high_0a, high_0b, high_1a,
                high_2a, best_out, high_out, reach_out):
    rows = own_ref.shape[0]
    quarter = across.shape[0] - INFO
    rep, odd = lax.axis_index("rep"), lax.axis_index("shard") % 2
    mine = (own_reach[0], own_reach[1])
    lower = (lower_reach[0], lower_reach[1])
    beside, up = read_reach(across, 3), read_reach(high_0b, 0)
    for n, value in enumerate(lower + beside + up):
        reach_out[n] = value
    best_out[...] = best_ref[...]
    high_out[...] = jnp.full(high_out.shape, -1.0, F32)
    lows = [key_piece(low, lower[1], rows, rep * quarter, quarter)]
    besides = [key_piece(across, beside[1], rows, rep * quarter, quarter)]
    count = jnp.where(odd == 1, reached(mine, beside, 0, rows), 0)
    group(besides, own_ref, rows, best_out, 0, count)
    pieces = [(high_0a, 0, 0), (high_0b, 0, 1), (high_1a, 1, 0), (high_2a, 2, 0)]
    upper(pieces, [(beside, besides), (lower, lows)], up, rep, high_out)


def both_keys(reach_ref, low, across):
    quarter, rows = 2 * TILE, 8 * TILE
    rep = lax.axis_index("rep")
    lower, beside, up = [(reach_ref[2 * n], reach_ref[2 * n + 1]) for n in range(3)]
    at = rep * quarter
    both = [
        (beside, [key_piece(across, beside[1], rows, at, quarter)]),
        (lower, [key_piece(low, lower[1], rows, at, quarter)]),
    ]
    return rep, up, both


def middle_kernel(reach_ref, prior_ref, low, across, high_1b, high_3a, high_out):
    rep, up, both = both_keys(reach_ref, low, across)
    high_out[...] = prior_ref[...]
    upper([(high_1b, 1, 1), (high_3a, 3, 0)], both, up, rep, high_out)


def side_keys(side, sides_ref):
    quarter, rows = 2 * TILE, 8 * TILE
    at = lax.axis_index("rep") * quarter
    return [(side, [key_piece(sides_ref, side[1], rows, at, quarter)])]


def far_kernel(reach_ref, prior_ref, low, across, high_0a, high_0b, high_1a, high_1b, high_2a,
               high_2b, high_3a, side_a, side_b, high_out, side_out, sides_out):
    half = TILE
    even = lax.axis_index("shard") % 2 == 0
    side = read_reach(side_a, 3)
    side_out[0], side_out[1] = side

    @pl.when(even)
    def _():
        sides_out[pl.ds(0, half), :] = side_b[pl.ds(0, half), :]
        sides_out[pl.ds(half, half), :] = side_a[pl.ds(0, half), :]

    rep, up, both = both_keys(reach_ref, low, across)
    high_out[...] = prior_ref[...]
    upper([(high_2b, 2, 1)], both, up, rep, high_out)
    pieces = [(high_0a, 0, 0), (high_0b, 0, 1), (high_1a, 1, 0), (high_1b, 1, 1), (high_2a, 2, 0)]
    pieces += [(high_2b, 2, 1), (high_3a, 3, 0)]
    upper(pieces, side_keys(side, sides_out), up, rep, high_out, even)


def last_kernel(reach_ref, side_ref, prior_ref, low, across, high_3b, sides, high_out):
    side = (side_ref[0], side_ref[1])
    even = lax.axis_index("shard") % 2 == 0
    rep, up, both = both_keys(reach_ref, low, across)
    high_out[...] = prior_ref[...]
    upper([(high_3b, 3, 1)], both, up, rep, high_out)
    upper([(high_3b, 3, 1)], side_keys(side, sides), up, rep, high_out, even)


def local(embeddings, labels):
    rows, width = embeddings.shape
    shards, reps = lax.axis_size("shard"), lax.axis_size("rep")
    quarter = rows // reps
    half = quarter // 2

    def along_shard(block, distance, keep=lambda i: True):
        route = [
            (i, i + distance) for i in range(shards) if i + distance in range(shards) and keep(i)
        ]
        return lax.ppermute(block, "shard", route)

    def partner(block):
        return lax.ppermute(block, "shard", [(i, i ^ 1) for i in range(shards)])

    def other_rep(block, flip):
        return lax.ppermute(block, "rep", [(i, i ^ flip) for i in range(reps)])

    def call(kernel, name, shapes, specs, *arrays):
        return pl.pallas_call(
            kernel,
            out_shape=[jax.ShapeDtypeStruct(shape, dtype) for shape, dtype in shapes],
            in_specs=specs[: len(arrays)],
            out_specs=specs[len(arrays) :],
            compiler_params=pltpu.CompilerParams(vmem_limit_bytes=VMEM_LIMIT),
            cost_estimate=pl.CostEstimate(flops=1024, bytes_accessed=1024, transcendentals=0),
            name=name,
        )(*arrays)

    sizes = [half, half + INFO, quarter + INFO]
    lo, hi, mine = pl.pallas_call(
        prepare_kernel,
        out_shape=[jax.ShapeDtypeStruct((size, width), BF16) for size in sizes],
        in_specs=[pl.BlockSpec(memory_space=pltpu.HBM)] * 2,
        out_specs=[VMEM] * 3,
        scratch_shapes=[
            pltpu.VMEM((2, half, width), BF16),
            pltpu.VMEM((rows // 128, 128), jnp.int32),
            pltpu.SemaphoreType.DMA((3,)),
        ],
        compiler_params=pltpu.CompilerParams(vmem_limit_bytes=PREPARE_LIMIT),
        name="prepare",
    )(embeddings, labels.reshape(rows // 128, 128))

    odd_only, even_only = (lambda i: i % 2 == 1), (lambda i: i % 2 == 0)
    fence = lax.optimization_barrier

    high_0a = along_shard(lo, -2)
    low = along_shard(mine, 2)
    across = partner(mine)
    high_0b = along_shard(hi, -2)

    own, best, own_reach = pl.pallas_call(
        own_kernel,
        out_shape=[
            jax.ShapeDtypeStruct((rows, width), BF16),
            jax.ShapeDtypeStruct((1, rows), F32),
            jax.ShapeDtypeStruct((2,), jnp.int32),
        ],
        in_specs=[pl.BlockSpec(memory_space=pltpu.HBM), VMEM],
        out_specs=[VMEM, VMEM, SMEM],
        scratch_shapes=[
            pltpu.VMEM((8, rows), jnp.int32),
            pltpu.VMEM((4, quarter, width), BF16),
            pltpu.SemaphoreType.DMA((4,)),
        ],
        compiler_params=pltpu.CompilerParams(vmem_limit_bytes=OWN_LIMIT),
        cost_estimate=pl.CostEstimate(flops=1024, bytes_accessed=1024, transcendentals=0),
        name="own",
    )(embeddings, labels[None, :])

    high_0a, own, best = fence((high_0a, own, best))
    high_2a = other_rep(high_0a, 2)
    high_1a = other_rep(high_0a, 1)
    line = ((1, rows), F32)
    best, lower_reach = call(
        lower_kernel, "lower", [line, ((2,), jnp.int32)], [SMEM] + [VMEM] * 4 + [SMEM],
        own_reach, own, best, low,
    )

    across, low, best = fence((across, low, best))
    side_b = along_shard(across[: half + INFO], 2, even_only)
    side_a = along_shard(low[half:], -1, odd_only)
    high_0b, high_1a, high_2a, across, low = fence((high_0b, high_1a, high_2a, across, low))
    high_2b = other_rep(high_0b, 2)
    high_1b = other_rep(high_0b[:half], 1)
    high_3a = other_rep(high_2a, 1)
    best, of_high, reach = call(
        near_kernel, "near", [line, line, ((6,), jnp.int32)],
        [SMEM] * 2 + [VMEM] * 10 + [SMEM],
        own_reach, lower_reach, own, best, low, across, high_0a, high_0b, high_1a, high_2a,
    )
    (of_high,) = call(
        middle_kernel, "middle", [line], [SMEM] + [VMEM] * 6,
        reach, of_high, low, across, high_1b, high_3a,
    )
    high_2b, side_a, side_b, of_high = fence((high_2b, side_a, side_b, of_high))
    high_3b = other_rep(high_2b, 1)
    of_high, side, sides = call(
        far_kernel, "far", [line, ((2,), jnp.int32), ((quarter, width), BF16)],
        [SMEM] + [VMEM] * 13 + [SMEM, VMEM],
        reach, of_high, low, across, high_0a, high_0b, high_1a, high_1b, high_2a, high_2b,
        high_3a, side_a, side_b,
    )
    (of_high,) = call(
        last_kernel, "last", [line], [SMEM] * 2 + [VMEM] * 6,
        reach, side, of_high, low, across, high_3b, sides,
    )

    above = along_shard(of_high, 2)
    best = jnp.maximum(best, jnp.where(lax.axis_index("shard") >= 2, above, -1.0))
    others = [other_rep(best, flip) for flip in range(1, reps)]
    return functools.reduce(jnp.maximum, others, best)[0]


def solution(mesh):
    placed = (P("shard", None), P("shard"))
    return jax.shard_map(local, mesh=mesh, in_specs=placed, out_specs=P("shard"), check_vma=False)
```

```python
import functools
import math

import jax
import jax.numpy as jnp
from jax import lax
from jax.experimental import pallas as pl
from jax.experimental.pallas import tpu as pltpu
from jax.sharding import PartitionSpec as P

F32 = jnp.float32
BF16 = jnp.bfloat16
TILE = 256
WIDE = 512
INFO = 16
VMEM_LIMIT = 32 * 1024 * 1024
OWN_LIMIT = 46 * 1024 * 1024
PREPARE_LIMIT = 50 * 1024 * 1024
VMEM = pl.BlockSpec(memory_space=pltpu.VMEM)
SMEM = pl.BlockSpec(memory_space=pltpu.SMEM)


def normalize(values):
    as_float = values.astype(F32)
    width = values.shape[1]
    inverse = lax.rsqrt(jnp.sum(as_float * as_float, axis=1, keepdims=True) * (1 / width) + 1e-06)
    return (as_float * (inverse * (1 / math.sqrt(width)))).astype(BF16)


def score(keys, queries):
    return lax.dot_general(keys, queries, (((1,), (1,)), ((), ())), preferred_element_type=F32)


def fold(values):
    rows, cols = values.shape
    return jnp.max(values.reshape(rows // 8, 8, cols), axis=0)


def prepare_kernel(emb_ref, labels_hbm, lo_out, hi_out, mine_out, raw, labels_ref, sems):
    rep = lax.axis_index("rep")
    quarter = mine_out.shape[0] - INFO
    part = quarter // 2
    copies = []
    for n in range(2):
        at = pl.multiple_of(rep * quarter + n * part, part)
        copies.append(pltpu.make_async_copy(emb_ref.at[pl.ds(at, part), :], raw.at[n], sems.at[n]))
        copies[-1].start()
    fetch = pltpu.make_async_copy(labels_hbm, labels_ref, sems.at[2])
    fetch.start()
    fetch.wait()
    labels = labels_ref[...]
    first, last = jnp.min(labels), jnp.max(labels)
    head = jnp.sum((labels == first).astype(jnp.int32))
    tail = jnp.sum((labels == last).astype(jnp.int32))
    row = lax.broadcasted_iota(jnp.int32, (INFO, mine_out.shape[1]), 0)
    info = jnp.zeros(row.shape, jnp.int32)
    for n, value in enumerate([first, head // 16, head % 16, last, tail // 16, tail % 16]):
        info = jnp.where(row == n, value, info)
    info = info.astype(F32).astype(BF16)
    for n, copy in enumerate(copies):
        copy.wait()
        for m in range(part // 128):
            rows = pl.ds(m * 128, 128)
            values = normalize(raw[n, rows, :])
            mine_out[pl.ds(n * part + m * 128, 128), :] = values
            (lo_out, hi_out)[n][rows, :] = values
    hi_out[pl.ds(part, INFO), :] = info
    mine_out[pl.ds(quarter, INFO), :] = info


def read_reach(ref, at):
    block = ref[pl.ds(ref.shape[0] - INFO, INFO), pl.ds(0, 128)].astype(F32)
    packed = block[at : at + 1] + 256.0 * (16.0 * block[at + 1 : at + 2] + block[at + 2 : at + 3])
    packed = jnp.max(packed).astype(jnp.int32)
    return packed % 256, packed // 256


def group(keys, queries_ref, query_rows, out_ref, out_at, count):
    step = min(WIDE, query_rows)

    def over_queries(j, _):
        at = pl.multiple_of(j * step, step)
        queries = queries_ref[pl.ds(at, step), :]
        best = None
        for ref, row, rows, first in keys:
            scores = score(ref[pl.ds(row, rows), :], queries)
            index = lax.broadcasted_iota(jnp.int32, scores.shape, 0)
            top = fold(jnp.where(index >= first, scores, -1.0))
            best = top if best is None else jnp.maximum(best, top)
        best = jnp.max(best, axis=0, keepdims=True)
        col = lax.broadcasted_iota(jnp.int32, best.shape, 1) + at
        cols = pl.ds(pl.multiple_of(out_at + at, TILE), step)
        out_ref[:, cols] = jnp.maximum(out_ref[:, cols], jnp.where(col < count, best, -1.0))
        return 0

    lax.fori_loop(0, (count + step - 1) // step, over_queries, 0)


def own_kernel(emb_ref, labels_ref, own_out, best_out, reach_out, start, raw, sems):
    rows = emb_ref.shape[0]
    rep = lax.axis_index("rep")
    parts = raw.shape[0]
    size = rows // parts
    copies = [
        pltpu.make_async_copy(emb_ref.at[pl.ds(n * size, size), :], raw.at[n], sems.at[n])
        for n in range(parts)
    ]
    for copy in copies:
        copy.start()
    labels = jnp.broadcast_to(labels_ref[...], start.shape)
    first = jnp.min(labels)
    reach_out[0] = first
    reach_out[1] = jnp.sum((labels == first).astype(jnp.int32)) // start.shape[0]
    lane = lax.broadcasted_iota(jnp.int32, labels.shape, 1)
    begin = jnp.where((lane == 0) | (labels != pltpu.roll(labels, 1, 1)), lane, 0)
    shift = 1
    while shift < rows:
        begin = jnp.maximum(begin, jnp.where(lane >= shift, pltpu.roll(begin, shift, 1), 0))
        shift *= 2
    start[...] = begin
    best_out[...] = jnp.full(best_out.shape, -1.0, F32)
    for n, copy in enumerate(copies):
        copy.wait()
        for m in range(size // 128):
            values = normalize(raw[n, pl.ds(m * 128, 128), :])
            own_out[pl.ds(n * size + m * 128, 128), :] = values
    for n in range(2):
        tile = rep if n == 0 else rows // TILE - 1 - rep
        at = pl.multiple_of(tile * TILE, TILE)
        keys = own_out[pl.ds(at, TILE), :]

        def over_queries(j, _):
            cols = pl.ds(pl.multiple_of(j * WIDE, WIDE), WIDE)
            scores = score(keys, own_out[cols, :])
            row = lax.broadcasted_iota(jnp.int32, scores.shape, 0) + at
            col = lax.broadcasted_iota(jnp.int32, scores.shape, 1) + j * WIDE
            keep = (row >= start[0:1, cols]) & (row < col)
            best = jnp.max(fold(jnp.where(keep, scores, -1.0)), axis=0, keepdims=True)
            best_out[:, cols] = jnp.maximum(best_out[:, cols], best)
            return 0

        lax.fori_loop(at // WIDE, rows // WIDE, over_queries, 0)


def reached(query, key, offset, limit):
    count = jnp.clip(query[1] - offset, 0, limit)
    return jnp.where(query[0] == key[0], count, 0)


def key_piece(ref, tail, rows, at, size):
    return (ref, 0, size, jnp.clip(rows - tail - at, 0, size))


def bundle(pieces, keys, up, rep, out_ref):
    half = TILE
    firsts, wanted = [], []
    for last, enabled, (_, _, rows, first) in keys:
        some = enabled & (up[0] == last[0]) & (first < rows)
        firsts.append(jnp.where(some, first, rows))
        wanted.append(some)
    starts = [(rep ^ flip) * 2 * half + part * half for _, flip, part in pieces]
    wanted = functools.reduce(jnp.logical_or, wanted)
    reached_one = functools.reduce(jnp.logical_or, [up[1] > at for at in starts])

    @pl.when(wanted & reached_one)
    def _():
        for (ref, _, _), at in zip(pieces, starts):
            queries = ref[pl.ds(0, half), :]
            best = None
            for (_, _, (key_ref, row, rows, _)), first in zip(keys, firsts):
                scores = score(key_ref[pl.ds(row, rows), :], queries)
                index = lax.broadcasted_iota(jnp.int32, scores.shape, 0)
                top = fold(jnp.where(index >= first, scores, -1.0))
                best = top if best is None else jnp.maximum(best, top)
            best = jnp.max(best, axis=0, keepdims=True)
            col = lax.broadcasted_iota(jnp.int32, best.shape, 1) + at
            cols = pl.ds(pl.multiple_of(at, half), half)
            out_ref[:, cols] = jnp.maximum(out_ref[:, cols], jnp.where(col < up[1], best, -1.0))


def near_kernel(own_reach, own_ref, best_ref, low, across, high_0a, high_0b, high_1a, high_2a,
                best_out, high_out, reach_out):
    rows = own_ref.shape[0]
    quarter = across.shape[0] - INFO
    rep, odd = lax.axis_index("rep"), lax.axis_index("shard") % 2
    mine = (own_reach[0], own_reach[1])
    lower, beside, up = read_reach(low, 3), read_reach(across, 3), read_reach(high_0b, 0)
    for n, value in enumerate(lower + beside + up):
        reach_out[n] = value
    best_out[...] = best_ref[...]
    high_out[...] = jnp.full(high_out.shape, -1.0, F32)
    lows = [key_piece(low, lower[1], rows, rep * quarter, quarter)]
    besides = [key_piece(across, beside[1], rows, rep * quarter, quarter)]
    group(lows, own_ref, rows, best_out, 0, reached(mine, lower, 0, rows))
    count = jnp.where(odd == 1, reached(mine, beside, 0, rows), 0)
    group(besides, own_ref, rows, best_out, 0, count)
    both = [(beside, True, besides[0]), (lower, True, lows[0])]
    bundle([(high_0a, 0, 0), (high_0b, 0, 1)], both, up, rep, high_out)
    bundle([(high_1a, 1, 0)], both, up, rep, high_out)
    bundle([(high_2a, 2, 0)], both, up, rep, high_out)


def both_keys(reach_ref, low, across):
    quarter, rows = 2 * TILE, 8 * TILE
    rep = lax.axis_index("rep")
    lower, beside, up = [(reach_ref[2 * n], reach_ref[2 * n + 1]) for n in range(3)]
    at = rep * quarter
    both = [
        (beside, True, key_piece(across, beside[1], rows, at, quarter)),
        (lower, True, key_piece(low, lower[1], rows, at, quarter)),
    ]
    return rep, up, both


def middle_kernel(reach_ref, prior_ref, low, across, high_1b, high_3a, high_out):
    rep, up, both = both_keys(reach_ref, low, across)
    high_out[...] = prior_ref[...]
    bundle([(high_1b, 1, 1)], both, up, rep, high_out)
    bundle([(high_3a, 3, 0)], both, up, rep, high_out)


def side_keys(side, sides_ref):
    quarter, rows = 2 * TILE, 8 * TILE
    even = lax.axis_index("shard") % 2 == 0
    at = lax.axis_index("rep") * quarter
    return [(side, even, key_piece(sides_ref, side[1], rows, at, quarter))]


def far_kernel(reach_ref, prior_ref, low, across, high_0a, high_0b, high_1a, high_1b, high_2a,
               high_2b, high_3a, side_a, side_b, high_out, side_out, sides_out):
    half = TILE
    side = read_reach(side_a, 3)
    side_out[0], side_out[1] = side
    sides_out[pl.ds(0, half), :] = side_b[pl.ds(0, half), :]
    sides_out[pl.ds(half, half), :] = side_a[pl.ds(0, half), :]
    rep, up, both = both_keys(reach_ref, low, across)
    high_out[...] = prior_ref[...]
    sides = side_keys(side, sides_out)
    bundle([(high_2b, 2, 1)], both, up, rep, high_out)
    bundle([(high_0a, 0, 0), (high_0b, 0, 1)], sides, up, rep, high_out)
    bundle([(high_1a, 1, 0), (high_1b, 1, 1)], sides, up, rep, high_out)
    bundle([(high_2a, 2, 0), (high_2b, 2, 1)], sides, up, rep, high_out)
    bundle([(high_3a, 3, 0)], sides, up, rep, high_out)


def last_kernel(reach_ref, side_ref, prior_ref, low, across, high_3b, sides, high_out):
    side = (side_ref[0], side_ref[1])
    rep, up, both = both_keys(reach_ref, low, across)
    high_out[...] = prior_ref[...]
    bundle([(high_3b, 3, 1)], both + side_keys(side, sides), up, rep, high_out)


def local(embeddings, labels):
    rows, width = embeddings.shape
    shards, reps = lax.axis_size("shard"), lax.axis_size("rep")
    quarter = rows // reps
    half = quarter // 2

    def along_shard(block, distance, keep=lambda i: True):
        route = [
            (i, i + distance) for i in range(shards) if i + distance in range(shards) and keep(i)
        ]
        return lax.ppermute(block, "shard", route)

    def partner(block):
        return lax.ppermute(block, "shard", [(i, i ^ 1) for i in range(shards)])

    def other_rep(block, flip):
        return lax.ppermute(block, "rep", [(i, i ^ flip) for i in range(reps)])

    def call(kernel, name, shapes, specs, *arrays):
        return pl.pallas_call(
            kernel,
            out_shape=[jax.ShapeDtypeStruct(shape, dtype) for shape, dtype in shapes],
            in_specs=specs[: len(arrays)],
            out_specs=specs[len(arrays) :],
            compiler_params=pltpu.CompilerParams(vmem_limit_bytes=VMEM_LIMIT),
            cost_estimate=pl.CostEstimate(flops=1024, bytes_accessed=1024, transcendentals=0),
            name=name,
        )(*arrays)

    sizes = [half, half + INFO, quarter + INFO]
    lo, hi, mine = pl.pallas_call(
        prepare_kernel,
        out_shape=[jax.ShapeDtypeStruct((size, width), BF16) for size in sizes],
        in_specs=[pl.BlockSpec(memory_space=pltpu.HBM)] * 2,
        out_specs=[VMEM] * 3,
        scratch_shapes=[
            pltpu.VMEM((2, half, width), BF16),
            pltpu.VMEM((rows // 128, 128), jnp.int32),
            pltpu.SemaphoreType.DMA((3,)),
        ],
        compiler_params=pltpu.CompilerParams(vmem_limit_bytes=PREPARE_LIMIT),
        name="prepare",
    )(embeddings, labels.reshape(rows // 128, 128))

    odd_only, even_only = (lambda i: i % 2 == 1), (lambda i: i % 2 == 0)
    fence = lax.optimization_barrier

    high_0a = along_shard(lo, -2)
    low = along_shard(mine, 2)
    across = partner(mine)
    high_0b = along_shard(hi, -2)

    high_0a, own_labels = fence((high_0a, labels))
    high_2a = other_rep(high_0a, 2)
    high_1a = other_rep(high_0a, 1)
    own, best, own_reach = pl.pallas_call(
        own_kernel,
        out_shape=[
            jax.ShapeDtypeStruct((rows, width), BF16),
            jax.ShapeDtypeStruct((1, rows), F32),
            jax.ShapeDtypeStruct((2,), jnp.int32),
        ],
        in_specs=[pl.BlockSpec(memory_space=pltpu.HBM), VMEM],
        out_specs=[VMEM, VMEM, SMEM],
        scratch_shapes=[
            pltpu.VMEM((8, rows), jnp.int32),
            pltpu.VMEM((4, quarter, width), BF16),
            pltpu.SemaphoreType.DMA((4,)),
        ],
        compiler_params=pltpu.CompilerParams(vmem_limit_bytes=OWN_LIMIT),
        cost_estimate=pl.CostEstimate(flops=1024, bytes_accessed=1024, transcendentals=0),
        name="own",
    )(embeddings, own_labels[None, :])

    across, low, own, best = fence((across, low, own, best))
    side_b = along_shard(across[: half + INFO], 2, even_only)
    side_a = along_shard(low[half:], -1, odd_only)
    high_0b, high_1a, high_2a, across, low = fence((high_0b, high_1a, high_2a, across, low))
    high_2b = other_rep(high_0b, 2)
    high_1b = other_rep(high_0b[:half], 1)
    high_3a = other_rep(high_2a, 1)
    line = ((1, rows), F32)
    best, of_high, reach = call(
        near_kernel, "near", [line, line, ((6,), jnp.int32)],
        [SMEM] + [VMEM] * 10 + [SMEM],
        own_reach, own, best, low, across, high_0a, high_0b, high_1a, high_2a,
    )
    (of_high,) = call(
        middle_kernel, "middle", [line], [SMEM] + [VMEM] * 6,
        reach, of_high, low, across, high_1b, high_3a,
    )
    high_2b, side_a, side_b, of_high = fence((high_2b, side_a, side_b, of_high))
    high_3b = other_rep(high_2b, 1)
    of_high, side, sides = call(
        far_kernel, "far", [line, ((2,), jnp.int32), ((quarter, width), BF16)],
        [SMEM] + [VMEM] * 13 + [SMEM, VMEM],
        reach, of_high, low, across, high_0a, high_0b, high_1a, high_1b, high_2a, high_2b,
        high_3a, side_a, side_b,
    )
    (of_high,) = call(
        last_kernel, "last", [line], [SMEM] * 2 + [VMEM] * 6,
        reach, side, of_high, low, across, high_3b, sides,
    )

    above = along_shard(of_high, 2)
    best = jnp.maximum(best, jnp.where(lax.axis_index("shard") >= 2, above, -1.0))
    others = [other_rep(best, flip) for flip in range(1, reps)]
    return functools.reduce(jnp.maximum, others, best)[0]


def solution(mesh):
    placed = (P("shard", None), P("shard"))
    return jax.shard_map(local, mesh=mesh, in_specs=placed, out_specs=P("shard"), check_vma=False)
```

```python
import functools
import math

import jax
import jax.numpy as jnp
from jax import lax
from jax.experimental import pallas as pl
from jax.experimental.pallas import tpu as pltpu
from jax.sharding import PartitionSpec as P

F32 = jnp.float32
BF16 = jnp.bfloat16
TILE = 256
WIDE = 512
INFO = 16
VMEM_LIMIT = 32 * 1024 * 1024
OWN_LIMIT = 46 * 1024 * 1024
PREPARE_LIMIT = 50 * 1024 * 1024
VMEM = pl.BlockSpec(memory_space=pltpu.VMEM)
SMEM = pl.BlockSpec(memory_space=pltpu.SMEM)


def normalize(values):
    as_float = values.astype(F32)
    width = values.shape[1]
    inverse = lax.rsqrt(jnp.sum(as_float * as_float, axis=1, keepdims=True) * (1 / width) + 1e-06)
    return (as_float * (inverse * (1 / math.sqrt(width)))).astype(BF16)


def score(keys, queries):
    return lax.dot_general(keys, queries, (((1,), (1,)), ((), ())), preferred_element_type=F32)


def fold(values):
    rows, cols = values.shape
    return jnp.max(values.reshape(rows // 8, 8, cols), axis=0)


def prepare_kernel(emb_ref, labels_hbm, lo_out, hi_out, mine_out, raw, labels_ref, sems):
    rep = lax.axis_index("rep")
    quarter = mine_out.shape[0] - INFO
    part = quarter // 2
    copies = []
    for n in range(2):
        at = pl.multiple_of(rep * quarter + n * part, part)
        copies.append(pltpu.make_async_copy(emb_ref.at[pl.ds(at, part), :], raw.at[n], sems.at[n]))
        copies[-1].start()
    fetch = pltpu.make_async_copy(labels_hbm, labels_ref, sems.at[2])
    fetch.start()
    fetch.wait()
    labels = labels_ref[...]
    first, last = jnp.min(labels), jnp.max(labels)
    head = jnp.sum((labels == first).astype(jnp.int32))
    tail = jnp.sum((labels == last).astype(jnp.int32))
    row = lax.broadcasted_iota(jnp.int32, (INFO, mine_out.shape[1]), 0)
    info = jnp.zeros(row.shape, jnp.int32)
    for n, value in enumerate([first, head // 16, head % 16, last, tail // 16, tail % 16]):
        info = jnp.where(row == n, value, info)
    info = info.astype(F32).astype(BF16)
    for n, copy in enumerate(copies):
        copy.wait()
        for m in range(part // 128):
            rows = pl.ds(m * 128, 128)
            values = normalize(raw[n, rows, :])
            mine_out[pl.ds(n * part + m * 128, 128), :] = values
            (lo_out, hi_out)[n][rows, :] = values
    hi_out[pl.ds(part, INFO), :] = info
    mine_out[pl.ds(quarter, INFO), :] = info


def read_reach(ref, at):
    block = ref[pl.ds(ref.shape[0] - INFO, INFO), pl.ds(0, 128)].astype(F32)
    packed = block[at : at + 1] + 256.0 * (16.0 * block[at + 1 : at + 2] + block[at + 2 : at + 3])
    packed = jnp.max(packed).astype(jnp.int32)
    return packed % 256, packed // 256


def group(keys, queries_ref, query_rows, out_ref, out_at, count):
    step = min(WIDE, query_rows)

    def over_queries(j, _):
        at = pl.multiple_of(j * step, step)
        queries = queries_ref[pl.ds(at, step), :]
        best = None
        for ref, row, rows, first in keys:
            scores = score(ref[pl.ds(row, rows), :], queries)
            index = lax.broadcasted_iota(jnp.int32, scores.shape, 0)
            top = fold(jnp.where(index >= first, scores, -1.0))
            best = top if best is None else jnp.maximum(best, top)
        best = jnp.max(best, axis=0, keepdims=True)
        col = lax.broadcasted_iota(jnp.int32, best.shape, 1) + at
        cols = pl.ds(pl.multiple_of(out_at + at, TILE), step)
        out_ref[:, cols] = jnp.maximum(out_ref[:, cols], jnp.where(col < count, best, -1.0))
        return 0

    lax.fori_loop(0, (count + step - 1) // step, over_queries, 0)


def own_kernel(emb_ref, labels_ref, own_out, best_out, reach_out, start, raw, sems):
    rows = emb_ref.shape[0]
    rep = lax.axis_index("rep")
    parts = raw.shape[0]
    size = rows // parts
    copies = [
        pltpu.make_async_copy(emb_ref.at[pl.ds(n * size, size), :], raw.at[n], sems.at[n])
        for n in range(parts)
    ]
    for copy in copies:
        copy.start()
    labels = jnp.broadcast_to(labels_ref[...], start.shape)
    first = jnp.min(labels)
    reach_out[0] = first
    reach_out[1] = jnp.sum((labels == first).astype(jnp.int32)) // start.shape[0]
    lane = lax.broadcasted_iota(jnp.int32, labels.shape, 1)
    begin = jnp.where((lane == 0) | (labels != pltpu.roll(labels, 1, 1)), lane, 0)
    shift = 1
    while shift < rows:
        begin = jnp.maximum(begin, jnp.where(lane >= shift, pltpu.roll(begin, shift, 1), 0))
        shift *= 2
    start[...] = begin
    best_out[...] = jnp.full(best_out.shape, -1.0, F32)
    for n, copy in enumerate(copies):
        copy.wait()
        for m in range(size // 128):
            values = normalize(raw[n, pl.ds(m * 128, 128), :])
            own_out[pl.ds(n * size + m * 128, 128), :] = values
    for n in range(2):
        tile = rep if n == 0 else rows // TILE - 1 - rep
        at = pl.multiple_of(tile * TILE, TILE)
        keys = own_out[pl.ds(at, TILE), :]

        def over_queries(j, _):
            cols = pl.ds(pl.multiple_of(j * WIDE, WIDE), WIDE)
            scores = score(keys, own_out[cols, :])
            row = lax.broadcasted_iota(jnp.int32, scores.shape, 0) + at
            col = lax.broadcasted_iota(jnp.int32, scores.shape, 1) + j * WIDE
            keep = (row >= start[0:1, cols]) & (row < col)
            best = jnp.max(fold(jnp.where(keep, scores, -1.0)), axis=0, keepdims=True)
            best_out[:, cols] = jnp.maximum(best_out[:, cols], best)
            return 0

        lax.fori_loop(at // WIDE, rows // WIDE, over_queries, 0)


def reached(query, key, offset, limit):
    count = jnp.clip(query[1] - offset, 0, limit)
    return jnp.where(query[0] == key[0], count, 0)


def key_piece(ref, tail, rows, at, size):
    return (ref, 0, size, jnp.clip(rows - tail - at, 0, size))


def bundle(pieces, keys, up, rep, out_ref):
    half = TILE
    firsts, wanted = [], []
    for last, enabled, (_, _, rows, first) in keys:
        some = enabled & (up[0] == last[0]) & (first < rows)
        firsts.append(jnp.where(some, first, rows))
        wanted.append(some)
    starts = [(rep ^ flip) * 2 * half + part * half for _, flip, part in pieces]
    wanted = functools.reduce(jnp.logical_or, wanted)
    reached_one = functools.reduce(jnp.logical_or, [up[1] > at for at in starts])

    @pl.when(wanted & reached_one)
    def _():
        for (ref, _, _), at in zip(pieces, starts):
            queries = ref[pl.ds(0, half), :]
            best = None
            for (_, _, (key_ref, row, rows, _)), first in zip(keys, firsts):
                scores = score(key_ref[pl.ds(row, rows), :], queries)
                index = lax.broadcasted_iota(jnp.int32, scores.shape, 0)
                top = fold(jnp.where(index >= first, scores, -1.0))
                best = top if best is None else jnp.maximum(best, top)
            best = jnp.max(best, axis=0, keepdims=True)
            col = lax.broadcasted_iota(jnp.int32, best.shape, 1) + at
            cols = pl.ds(pl.multiple_of(at, half), half)
            out_ref[:, cols] = jnp.maximum(out_ref[:, cols], jnp.where(col < up[1], best, -1.0))


def near_kernel(own_reach, own_ref, best_ref, low, across, high_0a, high_0b, high_1a, high_2a,
                best_out, high_out, reach_out):
    rows = own_ref.shape[0]
    quarter = across.shape[0] - INFO
    rep, odd = lax.axis_index("rep"), lax.axis_index("shard") % 2
    mine = (own_reach[0], own_reach[1])
    lower, beside, up = read_reach(low, 3), read_reach(across, 3), read_reach(high_0b, 0)
    for n, value in enumerate(lower + beside + up):
        reach_out[n] = value
    best_out[...] = best_ref[...]
    high_out[...] = jnp.full(high_out.shape, -1.0, F32)
    lows = [key_piece(low, lower[1], rows, rep * quarter, quarter)]
    besides = [key_piece(across, beside[1], rows, rep * quarter, quarter)]
    group(lows, own_ref, rows, best_out, 0, reached(mine, lower, 0, rows))
    count = jnp.where(odd == 1, reached(mine, beside, 0, rows), 0)
    group(besides, own_ref, rows, best_out, 0, count)
    both = [(beside, True, besides[0]), (lower, True, lows[0])]
    bundle([(high_0a, 0, 0), (high_0b, 0, 1)], both, up, rep, high_out)
    bundle([(high_1a, 1, 0)], both, up, rep, high_out)
    bundle([(high_2a, 2, 0)], both, up, rep, high_out)


def both_keys(reach_ref, low, across):
    quarter, rows = 2 * TILE, 8 * TILE
    rep = lax.axis_index("rep")
    lower, beside, up = [(reach_ref[2 * n], reach_ref[2 * n + 1]) for n in range(3)]
    at = rep * quarter
    both = [
        (beside, True, key_piece(across, beside[1], rows, at, quarter)),
        (lower, True, key_piece(low, lower[1], rows, at, quarter)),
    ]
    return rep, up, both


def middle_kernel(reach_ref, prior_ref, low, across, high_1b, high_3a, high_out):
    rep, up, both = both_keys(reach_ref, low, across)
    high_out[...] = prior_ref[...]
    bundle([(high_1b, 1, 1)], both, up, rep, high_out)
    bundle([(high_3a, 3, 0)], both, up, rep, high_out)


def side_keys(side, sides_ref):
    quarter, rows = 2 * TILE, 8 * TILE
    even = lax.axis_index("shard") % 2 == 0
    at = lax.axis_index("rep") * quarter
    return [(side, even, key_piece(sides_ref, side[1], rows, at, quarter))]


def far_kernel(reach_ref, prior_ref, low, across, high_0a, high_0b, high_1a, high_1b, high_2a,
               high_2b, high_3a, side_a, side_b, high_out, side_out, sides_out):
    half = TILE
    side = read_reach(side_a, 3)
    side_out[0], side_out[1] = side
    sides_out[pl.ds(0, half), :] = side_b[pl.ds(0, half), :]
    sides_out[pl.ds(half, half), :] = side_a[pl.ds(0, half), :]
    rep, up, both = both_keys(reach_ref, low, across)
    high_out[...] = prior_ref[...]
    sides = side_keys(side, sides_out)
    bundle([(high_2b, 2, 1)], both, up, rep, high_out)
    bundle([(high_0a, 0, 0), (high_0b, 0, 1)], sides, up, rep, high_out)
    bundle([(high_1a, 1, 0), (high_1b, 1, 1)], sides, up, rep, high_out)
    bundle([(high_2a, 2, 0), (high_2b, 2, 1)], sides, up, rep, high_out)
    bundle([(high_3a, 3, 0)], sides, up, rep, high_out)


def last_kernel(reach_ref, side_ref, prior_ref, low, across, high_3b, sides, high_out):
    side = (side_ref[0], side_ref[1])
    rep, up, both = both_keys(reach_ref, low, across)
    high_out[...] = prior_ref[...]
    bundle([(high_3b, 3, 1)], both + side_keys(side, sides), up, rep, high_out)


def local(embeddings, labels):
    rows, width = embeddings.shape
    shards, reps = lax.axis_size("shard"), lax.axis_size("rep")
    quarter = rows // reps
    half = quarter // 2

    def along_shard(block, distance, keep=lambda i: True):
        route = [
            (i, i + distance) for i in range(shards) if i + distance in range(shards) and keep(i)
        ]
        return lax.ppermute(block, "shard", route)

    def partner(block):
        return lax.ppermute(block, "shard", [(i, i ^ 1) for i in range(shards)])

    def other_rep(block, flip):
        return lax.ppermute(block, "rep", [(i, i ^ flip) for i in range(reps)])

    def call(kernel, name, shapes, specs, *arrays):
        return pl.pallas_call(
            kernel,
            out_shape=[jax.ShapeDtypeStruct(shape, dtype) for shape, dtype in shapes],
            in_specs=specs[: len(arrays)],
            out_specs=specs[len(arrays) :],
            compiler_params=pltpu.CompilerParams(vmem_limit_bytes=VMEM_LIMIT),
            cost_estimate=pl.CostEstimate(flops=1024, bytes_accessed=1024, transcendentals=0),
            name=name,
        )(*arrays)

    sizes = [half, half + INFO, quarter + INFO]
    lo, hi, mine = pl.pallas_call(
        prepare_kernel,
        out_shape=[jax.ShapeDtypeStruct((size, width), BF16) for size in sizes],
        in_specs=[pl.BlockSpec(memory_space=pltpu.HBM)] * 2,
        out_specs=[VMEM] * 3,
        scratch_shapes=[
            pltpu.VMEM((2, half, width), BF16),
            pltpu.VMEM((rows // 128, 128), jnp.int32),
            pltpu.SemaphoreType.DMA((3,)),
        ],
        compiler_params=pltpu.CompilerParams(vmem_limit_bytes=PREPARE_LIMIT),
        name="prepare",
    )(embeddings, labels.reshape(rows // 128, 128))

    odd_only, even_only = (lambda i: i % 2 == 1), (lambda i: i % 2 == 0)
    fence = lax.optimization_barrier

    high_0a = along_shard(lo, -2)
    low = along_shard(mine, 2)
    across = partner(mine)
    high_0b = along_shard(hi, -2)

    high_0a, own_labels = fence((high_0a, labels))
    high_2a = other_rep(high_0a, 2)
    high_1a = other_rep(high_0a, 1)
    own, best, own_reach = pl.pallas_call(
        own_kernel,
        out_shape=[
            jax.ShapeDtypeStruct((rows, width), BF16),
            jax.ShapeDtypeStruct((1, rows), F32),
            jax.ShapeDtypeStruct((2,), jnp.int32),
        ],
        in_specs=[pl.BlockSpec(memory_space=pltpu.HBM), VMEM],
        out_specs=[VMEM, VMEM, SMEM],
        scratch_shapes=[
            pltpu.VMEM((8, rows), jnp.int32),
            pltpu.VMEM((4, quarter, width), BF16),
            pltpu.SemaphoreType.DMA((4,)),
        ],
        compiler_params=pltpu.CompilerParams(vmem_limit_bytes=OWN_LIMIT),
        cost_estimate=pl.CostEstimate(flops=1024, bytes_accessed=1024, transcendentals=0),
        name="own",
    )(embeddings, own_labels[None, :])

    across, low, own, best = fence((across, low, own, best))
    side_b = along_shard(across[: half + INFO], 2, even_only)
    side_a = along_shard(low[half:], -1, odd_only)
    high_0b, high_1a, high_2a, across, low = fence((high_0b, high_1a, high_2a, across, low))
    rest = high_0b[:half]
    high_2b = other_rep(rest, 2)
    high_1b = other_rep(rest, 1)
    high_3a = other_rep(high_2a, 1)
    line = ((1, rows), F32)
    best, of_high, reach = call(
        near_kernel, "near", [line, line, ((6,), jnp.int32)],
        [SMEM] + [VMEM] * 10 + [SMEM],
        own_reach, own, best, low, across, high_0a, high_0b, high_1a, high_2a,
    )
    (of_high,) = call(
        middle_kernel, "middle", [line], [SMEM] + [VMEM] * 6,
        reach, of_high, low, across, high_1b, high_3a,
    )
    high_2b, side_a, side_b, of_high = fence((high_2b, side_a, side_b, of_high))
    high_3b = other_rep(high_2b, 1)
    of_high, side, sides = call(
        far_kernel, "far", [line, ((2,), jnp.int32), ((quarter, width), BF16)],
        [SMEM] + [VMEM] * 13 + [SMEM, VMEM],
        reach, of_high, low, across, high_0a, high_0b, high_1a, high_1b, high_2a, high_2b,
        high_3a, side_a, side_b,
    )
    (of_high,) = call(
        last_kernel, "last", [line], [SMEM] * 2 + [VMEM] * 6,
        reach, side, of_high, low, across, high_3b, sides,
    )

    above = along_shard(of_high, 2)
    best = jnp.maximum(best, jnp.where(lax.axis_index("shard") >= 2, above, -1.0))
    others = [other_rep(best, flip) for flip in range(1, reps)]
    return functools.reduce(jnp.maximum, others, best)[0]


def solution(mesh):
    placed = (P("shard", None), P("shard"))
    return jax.shard_map(local, mesh=mesh, in_specs=placed, out_specs=P("shard"), check_vma=False)
```

```python
import functools
import math

import jax
import jax.numpy as jnp
from jax import lax
from jax.experimental import pallas as pl
from jax.experimental.pallas import tpu as pltpu
from jax.sharding import PartitionSpec as P

F32 = jnp.float32
BF16 = jnp.bfloat16
TILE = 256
WIDE = 512
INFO = 16
VMEM_LIMIT = 32 * 1024 * 1024
OWN_LIMIT = 46 * 1024 * 1024
PREPARE_LIMIT = 50 * 1024 * 1024
VMEM = pl.BlockSpec(memory_space=pltpu.VMEM)
SMEM = pl.BlockSpec(memory_space=pltpu.SMEM)


def normalize(values):
    as_float = values.astype(F32)
    width = values.shape[1]
    inverse = lax.rsqrt(jnp.sum(as_float * as_float, axis=1, keepdims=True) * (1 / width) + 1e-06)
    return (as_float * (inverse * (1 / math.sqrt(width)))).astype(BF16)


def score(keys, queries):
    return lax.dot_general(keys, queries, (((1,), (1,)), ((), ())), preferred_element_type=F32)


def fold(values):
    rows, cols = values.shape
    return jnp.max(values.reshape(rows // 8, 8, cols), axis=0)


def prepare_kernel(emb_ref, labels_hbm, lo_out, hi_out, mine_out, raw, labels_ref, sems):
    rep = lax.axis_index("rep")
    quarter = mine_out.shape[0] - INFO
    part = quarter // 2
    copies = []
    for n in range(2):
        at = pl.multiple_of(rep * quarter + n * part, part)
        copies.append(pltpu.make_async_copy(emb_ref.at[pl.ds(at, part), :], raw.at[n], sems.at[n]))
        copies[-1].start()
    fetch = pltpu.make_async_copy(labels_hbm, labels_ref, sems.at[2])
    fetch.start()
    fetch.wait()
    labels = labels_ref[...]
    first, last = jnp.min(labels), jnp.max(labels)
    head = jnp.sum((labels == first).astype(jnp.int32))
    tail = jnp.sum((labels == last).astype(jnp.int32))
    row = lax.broadcasted_iota(jnp.int32, (INFO, mine_out.shape[1]), 0)
    info = jnp.zeros(row.shape, jnp.int32)
    for n, value in enumerate([first, head // 16, head % 16, last, tail // 16, tail % 16]):
        info = jnp.where(row == n, value, info)
    info = info.astype(F32).astype(BF16)
    for n, copy in enumerate(copies):
        copy.wait()
        for m in range(part // 128):
            rows = pl.ds(m * 128, 128)
            values = normalize(raw[n, rows, :])
            mine_out[pl.ds(n * part + m * 128, 128), :] = values
            (lo_out, hi_out)[n][rows, :] = values
    hi_out[pl.ds(part, INFO), :] = info
    mine_out[pl.ds(quarter, INFO), :] = info


def read_reach(ref, at):
    block = ref[pl.ds(ref.shape[0] - INFO, INFO), pl.ds(0, 128)].astype(F32)
    packed = block[at : at + 1] + 256.0 * (16.0 * block[at + 1 : at + 2] + block[at + 2 : at + 3])
    packed = jnp.max(packed).astype(jnp.int32)
    return packed % 256, packed // 256


def group(keys, queries_ref, query_rows, out_ref, out_at, count):
    step = min(WIDE, query_rows)

    def over_queries(j, _):
        at = pl.multiple_of(j * step, step)
        queries = queries_ref[pl.ds(at, step), :]
        best = None
        for ref, row, rows, first in keys:
            scores = score(ref[pl.ds(row, rows), :], queries)
            index = lax.broadcasted_iota(jnp.int32, scores.shape, 0)
            top = fold(jnp.where(index >= first, scores, -1.0))
            best = top if best is None else jnp.maximum(best, top)
        best = jnp.max(best, axis=0, keepdims=True)
        col = lax.broadcasted_iota(jnp.int32, best.shape, 1) + at
        cols = pl.ds(pl.multiple_of(out_at + at, TILE), step)
        out_ref[:, cols] = jnp.maximum(out_ref[:, cols], jnp.where(col < count, best, -1.0))
        return 0

    lax.fori_loop(0, (count + step - 1) // step, over_queries, 0)


def own_kernel(emb_ref, labels_ref, own_out, best_out, reach_out, start, raw, sems):
    rows = emb_ref.shape[0]
    rep = lax.axis_index("rep")
    parts = raw.shape[0]
    size = rows // parts
    copies = [
        pltpu.make_async_copy(emb_ref.at[pl.ds(n * size, size), :], raw.at[n], sems.at[n])
        for n in range(parts)
    ]
    for copy in copies:
        copy.start()
    labels = jnp.broadcast_to(labels_ref[...], start.shape)
    first = jnp.min(labels)
    reach_out[0] = first
    reach_out[1] = jnp.sum((labels == first).astype(jnp.int32)) // start.shape[0]
    lane = lax.broadcasted_iota(jnp.int32, labels.shape, 1)
    begin = jnp.where((lane == 0) | (labels != pltpu.roll(labels, 1, 1)), lane, 0)
    shift = 1
    while shift < rows:
        begin = jnp.maximum(begin, jnp.where(lane >= shift, pltpu.roll(begin, shift, 1), 0))
        shift *= 2
    start[...] = begin
    best_out[...] = jnp.full(best_out.shape, -1.0, F32)
    for n, copy in enumerate(copies):
        copy.wait()
        for m in range(size // 128):
            values = normalize(raw[n, pl.ds(m * 128, 128), :])
            own_out[pl.ds(n * size + m * 128, 128), :] = values
    for n in range(2):
        tile = rep if n == 0 else rows // TILE - 1 - rep
        at = pl.multiple_of(tile * TILE, TILE)
        keys = own_out[pl.ds(at, TILE), :]

        def over_queries(j, _):
            cols = pl.ds(pl.multiple_of(j * WIDE, WIDE), WIDE)
            scores = score(keys, own_out[cols, :])
            row = lax.broadcasted_iota(jnp.int32, scores.shape, 0) + at
            col = lax.broadcasted_iota(jnp.int32, scores.shape, 1) + j * WIDE
            keep = (row >= start[0:1, cols]) & (row < col)
            best = jnp.max(fold(jnp.where(keep, scores, -1.0)), axis=0, keepdims=True)
            best_out[:, cols] = jnp.maximum(best_out[:, cols], best)
            return 0

        lax.fori_loop(at // WIDE, rows // WIDE, over_queries, 0)


def reached(query, key, offset, limit):
    count = jnp.clip(query[1] - offset, 0, limit)
    return jnp.where(query[0] == key[0], count, 0)


def key_piece(ref, tail, rows, at, size):
    return (ref, 0, size, jnp.clip(rows - tail - at, 0, size))


def bundle(pieces, keys, up, rep, out_ref):
    half = TILE
    firsts, wanted = [], []
    for last, enabled, (_, _, rows, first) in keys:
        some = enabled & (up[0] == last[0]) & (first < rows)
        firsts.append(jnp.where(some, first, rows))
        wanted.append(some)
    starts = [(rep ^ flip) * 2 * half + part * half for _, flip, part in pieces]
    wanted = functools.reduce(jnp.logical_or, wanted)
    reached_one = functools.reduce(jnp.logical_or, [up[1] > at for at in starts])

    @pl.when(wanted & reached_one)
    def _():
        for (ref, _, _), at in zip(pieces, starts):
            queries = ref[pl.ds(0, half), :]
            best = None
            for (_, _, (key_ref, row, rows, _)), first in zip(keys, firsts):
                scores = score(key_ref[pl.ds(row, rows), :], queries)
                index = lax.broadcasted_iota(jnp.int32, scores.shape, 0)
                top = fold(jnp.where(index >= first, scores, -1.0))
                best = top if best is None else jnp.maximum(best, top)
            best = jnp.max(best, axis=0, keepdims=True)
            col = lax.broadcasted_iota(jnp.int32, best.shape, 1) + at
            cols = pl.ds(pl.multiple_of(at, half), half)
            out_ref[:, cols] = jnp.maximum(out_ref[:, cols], jnp.where(col < up[1], best, -1.0))


def near_kernel(own_reach, own_ref, best_ref, low, across, high_0a, high_0b, high_1a, high_2a,
                best_out, high_out, reach_out):
    rows = own_ref.shape[0]
    quarter = across.shape[0] - INFO
    rep, odd = lax.axis_index("rep"), lax.axis_index("shard") % 2
    mine = (own_reach[0], own_reach[1])
    lower, beside, up = read_reach(low, 3), read_reach(across, 3), read_reach(high_0b, 0)
    for n, value in enumerate(lower + beside + up):
        reach_out[n] = value
    best_out[...] = best_ref[...]
    high_out[...] = jnp.full(high_out.shape, -1.0, F32)
    lows = [key_piece(low, lower[1], rows, rep * quarter, quarter)]
    besides = [key_piece(across, beside[1], rows, rep * quarter, quarter)]
    group(lows, own_ref, rows, best_out, 0, reached(mine, lower, 0, rows))
    count = jnp.where(odd == 1, reached(mine, beside, 0, rows), 0)
    group(besides, own_ref, rows, best_out, 0, count)
    both = [(beside, True, besides[0]), (lower, True, lows[0])]
    bundle([(high_0a, 0, 0), (high_0b, 0, 1)], both, up, rep, high_out)
    bundle([(high_1a, 1, 0)], both, up, rep, high_out)
    bundle([(high_2a, 2, 0)], both, up, rep, high_out)


def both_keys(reach_ref, low, across):
    quarter, rows = 2 * TILE, 8 * TILE
    rep = lax.axis_index("rep")
    lower, beside, up = [(reach_ref[2 * n], reach_ref[2 * n + 1]) for n in range(3)]
    at = rep * quarter
    both = [
        (beside, True, key_piece(across, beside[1], rows, at, quarter)),
        (lower, True, key_piece(low, lower[1], rows, at, quarter)),
    ]
    return rep, up, both


def middle_kernel(reach_ref, prior_ref, low, across, high_1b, high_3a, high_out):
    rep, up, both = both_keys(reach_ref, low, across)
    high_out[...] = prior_ref[...]
    bundle([(high_1b, 1, 1)], both, up, rep, high_out)
    bundle([(high_3a, 3, 0)], both, up, rep, high_out)


def side_keys(side, sides_ref):
    quarter, rows = 2 * TILE, 8 * TILE
    even = lax.axis_index("shard") % 2 == 0
    at = lax.axis_index("rep") * quarter
    return [(side, even, key_piece(sides_ref, side[1], rows, at, quarter))]


def far_kernel(reach_ref, prior_ref, low, across, high_0a, high_0b, high_1a, high_1b, high_2a,
               high_2b, high_3a, side_a, side_b, high_out, side_out, sides_out):
    half = TILE
    side = read_reach(side_a, 3)
    side_out[0], side_out[1] = side
    sides_out[pl.ds(0, half), :] = side_b[pl.ds(0, half), :]
    sides_out[pl.ds(half, half), :] = side_a[pl.ds(INFO, half), :]
    rep, up, both = both_keys(reach_ref, low, across)
    high_out[...] = prior_ref[...]
    sides = side_keys(side, sides_out)
    bundle([(high_2b, 2, 1)], both, up, rep, high_out)
    bundle([(high_0a, 0, 0), (high_0b, 0, 1)], sides, up, rep, high_out)
    bundle([(high_1a, 1, 0), (high_1b, 1, 1)], sides, up, rep, high_out)
    bundle([(high_2a, 2, 0), (high_2b, 2, 1)], sides, up, rep, high_out)
    bundle([(high_3a, 3, 0)], sides, up, rep, high_out)


def last_kernel(reach_ref, side_ref, prior_ref, low, across, high_3b, sides, high_out):
    side = (side_ref[0], side_ref[1])
    rep, up, both = both_keys(reach_ref, low, across)
    high_out[...] = prior_ref[...]
    bundle([(high_3b, 3, 1)], both + side_keys(side, sides), up, rep, high_out)


def local(embeddings, labels):
    rows, width = embeddings.shape
    shards, reps = lax.axis_size("shard"), lax.axis_size("rep")
    quarter = rows // reps
    half = quarter // 2

    def along_shard(block, distance, keep=lambda i: True):
        route = [
            (i, i + distance) for i in range(shards) if i + distance in range(shards) and keep(i)
        ]
        return lax.ppermute(block, "shard", route)

    def partner(block):
        return lax.ppermute(block, "shard", [(i, i ^ 1) for i in range(shards)])

    def other_rep(block, flip):
        return lax.ppermute(block, "rep", [(i, i ^ flip) for i in range(reps)])

    def call(kernel, name, shapes, specs, *arrays):
        return pl.pallas_call(
            kernel,
            out_shape=[jax.ShapeDtypeStruct(shape, dtype) for shape, dtype in shapes],
            in_specs=specs[: len(arrays)],
            out_specs=specs[len(arrays) :],
            compiler_params=pltpu.CompilerParams(vmem_limit_bytes=VMEM_LIMIT),
            cost_estimate=pl.CostEstimate(flops=1024, bytes_accessed=1024, transcendentals=0),
            name=name,
        )(*arrays)

    sizes = [half, half + INFO, quarter + INFO]
    lo, hi, mine = pl.pallas_call(
        prepare_kernel,
        out_shape=[jax.ShapeDtypeStruct((size, width), BF16) for size in sizes],
        in_specs=[pl.BlockSpec(memory_space=pltpu.HBM)] * 2,
        out_specs=[VMEM] * 3,
        scratch_shapes=[
            pltpu.VMEM((2, half, width), BF16),
            pltpu.VMEM((rows // 128, 128), jnp.int32),
            pltpu.SemaphoreType.DMA((3,)),
        ],
        compiler_params=pltpu.CompilerParams(vmem_limit_bytes=PREPARE_LIMIT),
        name="prepare",
    )(embeddings, labels.reshape(rows // 128, 128))

    odd_only, even_only = (lambda i: i % 2 == 1), (lambda i: i % 2 == 0)
    fence = lax.optimization_barrier

    high_0a = along_shard(lo, -2)
    low = along_shard(mine, 2)
    across = partner(mine)
    high_0b = along_shard(hi, -2)

    high_0a, own_labels = fence((high_0a, labels))
    high_2a = other_rep(high_0a, 2)
    high_1a = other_rep(high_0a, 1)
    own, best, own_reach = pl.pallas_call(
        own_kernel,
        out_shape=[
            jax.ShapeDtypeStruct((rows, width), BF16),
            jax.ShapeDtypeStruct((1, rows), F32),
            jax.ShapeDtypeStruct((2,), jnp.int32),
        ],
        in_specs=[pl.BlockSpec(memory_space=pltpu.HBM), VMEM],
        out_specs=[VMEM, VMEM, SMEM],
        scratch_shapes=[
            pltpu.VMEM((8, rows), jnp.int32),
            pltpu.VMEM((4, quarter, width), BF16),
            pltpu.SemaphoreType.DMA((4,)),
        ],
        compiler_params=pltpu.CompilerParams(vmem_limit_bytes=OWN_LIMIT),
        cost_estimate=pl.CostEstimate(flops=1024, bytes_accessed=1024, transcendentals=0),
        name="own",
    )(embeddings, own_labels[None, :])

    across, low, own, best = fence((across, low, own, best))
    side_b = along_shard(across[: half + 2 * INFO], 2, even_only)
    side_a = along_shard(low[half - INFO :], -1, odd_only)
    high_0b, high_1a, high_2a, across, low = fence((high_0b, high_1a, high_2a, across, low))
    rest = high_0b[:half]
    high_2b = other_rep(high_0b, 2)
    high_1b = other_rep(rest, 1)
    high_3a = other_rep(high_2a, 1)
    line = ((1, rows), F32)
    best, of_high, reach = call(
        near_kernel, "near", [line, line, ((6,), jnp.int32)],
        [SMEM] + [VMEM] * 10 + [SMEM],
        own_reach, own, best, low, across, high_0a, high_0b, high_1a, high_2a,
    )
    (of_high,) = call(
        middle_kernel, "middle", [line], [SMEM] + [VMEM] * 6,
        reach, of_high, low, across, high_1b, high_3a,
    )
    high_2b, side_a, side_b, of_high = fence((high_2b, side_a, side_b, of_high))
    high_3b = other_rep(high_2b, 1)
    of_high, side, sides = call(
        far_kernel, "far", [line, ((2,), jnp.int32), ((quarter, width), BF16)],
        [SMEM] + [VMEM] * 13 + [SMEM, VMEM],
        reach, of_high, low, across, high_0a, high_0b, high_1a, high_1b, high_2a, high_2b,
        high_3a, side_a, side_b,
    )
    (of_high,) = call(
        last_kernel, "last", [line], [SMEM] * 2 + [VMEM] * 6,
        reach, side, of_high, low, across, high_3b, sides,
    )

    above = along_shard(of_high, 2)
    best = jnp.maximum(best, jnp.where(lax.axis_index("shard") >= 2, above, -1.0))
    others = [other_rep(best, flip) for flip in range(1, reps)]
    return functools.reduce(jnp.maximum, others, best)[0]


def solution(mesh):
    placed = (P("shard", None), P("shard"))
    return jax.shard_map(local, mesh=mesh, in_specs=placed, out_specs=P("shard"), check_vma=False)
```
